32 devices in a mesh: img: 8 (over z, x), row: 4 (over y, core).
Axes of the slice: x: 2, y: 2, z: 4, core: 2. Of those that a mesh axis runs over, the one named last changes fastest.
Arguments:
- feature_map: bfloat16 [448, 24, 16, 1024], P('img', 'row'), may hold values from -6 to 6
- image_group: int32 [448], P('img'), may hold values from 0 to 2, as said below
- row_counts: int32 [448, 4], P('img', 'row'), may hold values from 1 to 6, as said below
- reduce_weight: bfloat16 [1024, 256], replicated, may hold values from -0.1875 to 0.1875
- gain_first: float32 [256], replicated, may hold values from 0.25 to 1.75
- shift_first: float32 [256], replicated, may hold values from -0.5 to 0.5
- split_weight: bfloat16 [3, 3, 128, 512], replicated, may hold values from -0.1875 to 0.1875
- gain_second: float32 [512], replicated, may hold values from 0.25 to 1.75
- shift_second: float32 [512], replicated, may hold values from -0.5 to 0.5
- attn_down: bfloat16 [256, 128], replicated, may hold values from -0.375 to 0.375
- gain_attend: float32 [128], replicated, may hold values from 0.25 to 1.75
- shift_attend: float32 [128], replicated, may hold values from -0.5 to 0.5
- attn_up: bfloat16 [128, 512], replicated, may hold values from -0.5 to 0.5
- attn_bias: float32 [512], replicated, may hold values from -1 to 1
- expand_weight: bfloat16 [256, 1024], replicated, may hold values from -0.375 to 0.375
- gain_third: float32 [1024], replicated, may hold values from 0.25 to 1.75
- shift_third: float32 [1024], replicated, may hold values from -0.5 to 0.5
- cotangent: bfloat16 [448, 24, 16, 1024], P('img', 'row'), may hold values from -6 to 6
Outputs:
- block_out: bfloat16 [448, 24, 16, 1024], P('img', 'row')
- grad_input: bfloat16 [448, 24, 16, 1024], P('img', 'row')
- grad_reduce: float32 [1024, 256], P('row')
- grad_split: float32 [3, 3, 128, 512], P(None, None, 'row')
- grad_expand: float32 [256, 1024], P('row')
- grad_down: float32 [256, 128], replicated
- grad_up: float32 [128, 512], replicated
- grad_bias: float32 [512], replicated
- grad_gain_first: float32 [256], replicated
- grad_shift_first: float32 [256], replicated
- grad_gain_second: float32 [512], replicated
- grad_shift_second: float32 [512], replicated
- grad_gain_attend: float32 [128], replicated
- grad_shift_attend: float32 [128], replicated
- grad_gain_third: float32 [1024], replicated
- grad_shift_third: float32 [1024], replicated
The draws below stay inside these ranges and needn't reach their ends.
Inputs may be any that keep to these rules, and one draw needn't show every extreme that they name: Image i is 12 + 2 * image_group[i] rows tall and as wide; image 0 is of group 2. `row_counts`: for each image the counts over the 4 devices of row sum to its height; every device holds at least one row of every image; some image has 6 rows on one device.
All inputs are finite; a program needn't handle non-finite values.
Results may differ from the reference program's by a relative error of at most 0.0081.
Values may be sent and summed in bfloat16 or wider, within the bound.
A program may use at most 512 MiB of HBM per device.

```python
import jax
import jax.numpy as jnp
from jax import lax

CH = 1024
MID = 256
INTER = 128
WMAX = 16
RCAP = 6
IMAGES = 448
SLOTS = 24
N_ROW = 4


def split_table(key):
    first_key, second_key, third_key = jax.random.split(key, 3)
    group = jax.random.randint(first_key, (IMAGES,), 0, 3).astype(jnp.int32)
    group = group.at[0].set(2)
    height = 12 + 2 * group
    ranks = jnp.arange(4, dtype=jnp.int32)
    base = height[:, None] // 4 + (ranks[None, :] < (height % 4)[:, None]).astype(jnp.int32)
    upper = jax.random.randint(second_key, (IMAGES,), -1, 3).astype(jnp.int32)
    upper = upper.at[0].set(2)
    lower = jax.random.randint(third_key, (IMAGES,), -1, 3).astype(jnp.int32)
    moves = jnp.stack([upper, -upper, -lower, lower], axis=1)
    return (group, (base + moves).astype(jnp.int32))


def draw_image_group(key, part):
    table = split_table(key)
    return table[0]


def draw_row_counts(key, part):
    table = split_table(key)
    return table[1]


def block_scale(stream_key, shape, shards, smallest, high):
    def one(dim, parts):
        heights = jax.random.uniform(jax.random.fold_in(jax.random.fold_in(stream_key, 6), dim), (parts,), jnp.float32, smallest / len(shards), high / len(shards))
        return jnp.repeat(jnp.exp(heights), shape[dim] // parts).reshape((-1,) + (1,) * (len(shape) - dim - 1))

    loudness = one(*shards[0])
    for cut in shards[1:]:
        loudness = loudness * one(*cut)
    return loudness


def scatter_about(own_key, extent, scale, bound, cuts=(), held_as=jnp.bfloat16):
    values = jax.random.normal(own_key, extent, jnp.float32) * scale
    if len(cuts) > 0:
        values = block_scale(own_key, extent, cuts, -0.22, 0.18) * values
    return jnp.clip(values, min=-bound, max=bound).astype(held_as)


def setup_inputs(seed: int = 0) -> dict:
    streams_of = jax.random.split(jax.random.key(seed), 19)
    return {
        "feature_map": scatter_about(streams_of[0], (IMAGES, SLOTS, WMAX, CH), 1.0, 6.0, ((0, 8), (1, 4))),
        "image_group": draw_image_group(jax.random.fold_in(streams_of[18], 71), 0),
        "row_counts": draw_row_counts(jax.random.fold_in(streams_of[18], 71), 0),
        "reduce_weight": scatter_about(streams_of[3], (CH, MID), CH ** -0.5, 0.1875),
        "gain_first": jnp.clip(1.0 + 0.15 * jax.random.normal(streams_of[4], (MID,), jnp.float32), 0.25, 1.75),
        "shift_first": jnp.clip(jax.random.uniform(streams_of[5], (MID,), jnp.float32, -0.5, 0.5), -0.5, 0.5),
        "split_weight": scatter_about(streams_of[6], (3, 3, MID // 2, 2 * MID), (9 * MID // 2) ** -0.5, 0.1875),
        "gain_second": jnp.clip(1.0 + 0.15 * jax.random.normal(streams_of[7], (2 * MID,), jnp.float32), 0.25, 1.75),
        "shift_second": jnp.clip(jax.random.uniform(streams_of[8], (2 * MID,), jnp.float32, -0.5, 0.5), -0.5, 0.5),
        "attn_down": scatter_about(streams_of[9], (MID, INTER), MID ** -0.5, 0.375),
        "gain_attend": jnp.clip(1.0 + 0.15 * jax.random.normal(streams_of[10], (INTER,), jnp.float32), 0.25, 1.75),
        "shift_attend": jnp.clip(jax.random.uniform(streams_of[11], (INTER,), jnp.float32, -0.5, 0.5), -0.5, 0.5),
        "attn_up": scatter_about(streams_of[12], (INTER, 2 * MID), INTER ** -0.5, 0.5),
        "attn_bias": jnp.clip(jax.random.uniform(streams_of[13], (2 * MID,), jnp.float32, -1.0, 1.0), -1.0, 1.0),
        "expand_weight": scatter_about(streams_of[14], (MID, CH), MID ** -0.5, 0.375),
        "gain_third": jnp.clip(1.0 + 0.15 * jax.random.normal(streams_of[15], (CH,), jnp.float32), 0.25, 1.75),
        "shift_third": jnp.clip(jax.random.uniform(streams_of[16], (CH,), jnp.float32, -0.5, 0.5), -0.5, 0.5),
        "cotangent": scatter_about(streams_of[17], (IMAGES, SLOTS, WMAX, CH), 1.0, 6.0, ((0, 8), (1, 4))),
    }


HIGH = lax.Precision.HIGHEST
EPS = 1e-05

@jax.custom_vjp
def low(v):
    return lax.optimization_barrier(v.astype(jnp.bfloat16)).astype(jnp.float32)

@jax.custom_vjp
def low_back(v):
    return v

def low_keep(v):
    return (low(v), None)

def low_pass(kept, grad):
    return (grad,)

def back_keep(v):
    return (v, None)

def back_low(kept, grad):
    return (low(grad),)
low.defvjp(low_keep, low_pass)
low_back.defvjp(back_keep, back_low)

def layout(image_group, row_counts):
    height = (12 + 2 * image_group).astype(jnp.int32)
    ends = jnp.cumsum(row_counts, axis=1).astype(jnp.int32)
    starts = (ends - row_counts).astype(jnp.int32)
    lines = jnp.arange(WMAX, dtype=jnp.int32)
    device_of = lax.optimization_barrier(jnp.sum((ends[:, None, :] <= lines[None, :, None]).astype(jnp.int32), axis=2))
    device_of = jnp.minimum(device_of, N_ROW - 1).astype(jnp.int32)
    start_of = jnp.take_along_axis(starts, device_of, axis=1)
    slot_of = jnp.clip(device_of * RCAP + lines[None, :] - start_of, 0, SLOTS - 1).astype(jnp.int32)
    inside = (lines[None, :] < height[:, None]).astype(jnp.float32)
    compact_mask = inside[:, :, None] * inside[:, None, :]
    slot_ids = jnp.arange(SLOTS, dtype=jnp.int32)
    owner = (slot_ids // RCAP).astype(jnp.int32)
    within = (slot_ids % RCAP).astype(jnp.int32)
    row_of = jnp.clip(starts[:, owner] + within[None, :], 0, WMAX - 1).astype(jnp.int32)
    held = (within[None, :] < row_counts[:, owner]).astype(jnp.float32)
    slot_mask = held[:, :, None] * inside[:, None, :]
    return (height, slot_of, compact_mask, row_of, slot_mask)

def to_compact(array, slot_of, compact_mask):
    picks = jnp.arange(IMAGES, dtype=jnp.int32)[:, None]
    return array[picks, slot_of].astype(jnp.float32) * compact_mask[..., None]

def to_slots(array, row_of, slot_mask):
    picks = jnp.arange(IMAGES, dtype=jnp.int32)[:, None]
    return array[picks, row_of] * slot_mask[..., None]

def batchnorm(values, mask, count, gain, shift):
    axes = tuple(range(values.ndim - 1))
    total = lax.optimization_barrier(jnp.sum(values * mask, axis=axes))
    square = lax.optimization_barrier(jnp.sum(values * values * mask, axis=axes))
    mean = total / count
    spread = square / count - mean * mean
    return ((values - mean) * lax.rsqrt(spread + EPS) * gain + shift) * mask

def split_conv(activity, weight):
    padded = jnp.pad(activity, ((0, 0), (1, 1), (1, 1), (0, 0)))
    half = MID // 2
    total = jnp.zeros(activity.shape[:3] + (2 * MID,), jnp.float32)
    for row_step in range(3):
        for col_step in range(3):
            patch = padded[:, row_step:row_step + WMAX, col_step:col_step + WMAX, :]
            left = jnp.einsum('bhwc,cd->bhwd', patch[..., :half], weight[row_step, col_step, :, :MID], precision=HIGH)
            right = jnp.einsum('bhwc,cd->bhwd', patch[..., half:], weight[row_step, col_step, :, MID:], precision=HIGH)
            total = total + jnp.concatenate([left, right], axis=-1)
    return total

def forward(inputs, reduce_weight, gain_first, shift_first, split_weight, gain_second, shift_second, attn_down, gain_attend, shift_attend, attn_up, attn_bias, expand_weight, gain_third, shift_third, compact_mask, height):
    mask = compact_mask[..., None]
    count = jnp.sum(compact_mask)
    first_pre = low_back(jnp.einsum('bhwc,cd->bhwd', inputs, reduce_weight, precision=HIGH))
    first_act = low(jax.nn.silu(batchnorm(first_pre, mask, count, gain_first, shift_first)))
    second_pre = low_back(split_conv(first_act, split_weight))
    second_act = jax.nn.silu(batchnorm(second_pre, mask, count, gain_second, shift_second))
    part_zero = second_act[..., :MID]
    part_one = second_act[..., MID:]
    area = (height * height).astype(jnp.float32)
    pooled = lax.optimization_barrier(jnp.sum(part_zero + part_one, axis=(1, 2))) / area[:, None]
    squeeze = jnp.dot(pooled, attn_down, precision=HIGH)
    image_count = jnp.asarray(IMAGES, jnp.float32)
    attend = jax.nn.silu(batchnorm(squeeze, jnp.asarray(1.0, jnp.float32), image_count, gain_attend, shift_attend))
    logits = jnp.dot(attend, attn_up, precision=HIGH) + attn_bias
    weights = jax.nn.softmax(logits.reshape(IMAGES, 2, MID), axis=1)
    mixed = low(weights[:, 0, None, None, :] * part_zero + weights[:, 1, None, None, :] * part_one)
    third_pre = low_back(jnp.einsum('bhwc,cd->bhwd', mixed, expand_weight, precision=HIGH))
    summed = batchnorm(third_pre, mask, count, gain_third, shift_third) + inputs
    return jax.nn.silu(summed) * mask

def reference(feature_map, image_group, row_counts, reduce_weight, gain_first, shift_first, split_weight, gain_second, shift_second, attn_down, gain_attend, shift_attend, attn_up, attn_bias, expand_weight, gain_third, shift_third, cotangent):
    height, slot_of, compact_mask, row_of, slot_mask = layout(image_group, row_counts)
    inputs = to_compact(feature_map, slot_of, compact_mask)
    params = (reduce_weight.astype(jnp.float32), gain_first, shift_first, split_weight.astype(jnp.float32), gain_second, shift_second, attn_down.astype(jnp.float32), gain_attend, shift_attend, attn_up.astype(jnp.float32), attn_bias, expand_weight.astype(jnp.float32), gain_third, shift_third)

    def wrapped(inputs, *rest):
        return forward(inputs, *rest, compact_mask, height)
    result, pullback = jax.vjp(wrapped, inputs, *params)
    grads = pullback(to_compact(cotangent, slot_of, compact_mask))
    block_out = to_slots(result, row_of, slot_mask).astype(jnp.bfloat16)
    grad_input = to_slots(grads[0], row_of, slot_mask).astype(jnp.bfloat16)
    return (block_out, grad_input, grads[1], grads[4], grads[12], grads[7], grads[10], grads[11], grads[2], grads[3], grads[5], grads[6], grads[8], grads[9], grads[13], grads[14])
```

```python
import functools

import jax
import jax.numpy as jnp
from jax import lax
from jax.experimental import pallas as pl
from jax.experimental.pallas import tpu as pltpu
from jax.sharding import PartitionSpec as P

MESH = pl.DeviceIdType.MESH
HIGH = lax.Precision.HIGHEST
F32 = jnp.float32
BF16 = jnp.bfloat16
EPS = 1e-05
GROUP = 8
ANY = pl.BlockSpec(memory_space=pl.ANY)
VMEM = pl.BlockSpec(memory_space=pltpu.VMEM)
SMEM = pl.BlockSpec(memory_space=pltpu.SMEM)


def dot(a, b, dims, precision=None):
    return lax.dot_general(
        a, b, (dims, ((), ())), preferred_element_type=F32, precision=precision
    )


def mm(a, b, precision=None):
    return dot(a, b, ((1,), (0,)), precision)


def mm_nt(a, b, precision=None):
    return dot(a, b, ((1,), (1,)), precision)


def mm_tn(a, b, precision=None):
    return dot(a, b, ((0,), (0,)), precision)


def mm_terms(product, a, b, terms):
    total = None
    for _ in range(terms):
        part = a.astype(BF16)
        a = a - part.astype(F32)
        value = product(part, b)
        total = value if total is None else total + value
    return total


def sigmoid(v):
    return 0.5 * jnp.tanh(0.5 * v) + 0.5


def swish_slope(v):
    s = sigmoid(v)
    return s * (1.0 + v * (1.0 - s))


def wide(mask, times):
    return jnp.concatenate([mask] * times, axis=1)


def fold(v):
    return jnp.sum(v.reshape(v.shape[0] // 8, 8, v.shape[1]), axis=0)


def row_sum(v):
    return jnp.sum(v, axis=0, keepdims=True)


class Links:
    def __init__(self, n_img, n_row):
        self.ni, self.nr = n_img, n_row
        self.i, self.r = lax.axis_index("img"), lax.axis_index("row")

    def greet(self):
        bar = pltpu.get_barrier_semaphore()

        def go(k, c):
            pl.semaphore_signal(
                bar, inc=1, device_id=self.peer(k), device_id_type=MESH
            )
            return c

        lax.fori_loop(1, self.ni * self.nr, go, 0)

    def met(self):
        pl.semaphore_wait(pltpu.get_barrier_semaphore(), self.ni * self.nr - 1)

    def peer(self, k):
        return (lax.rem(self.i + k // self.nr, self.ni), lax.rem(self.r + k % self.nr, self.nr))

    def copy(self, buf, send, recv, me, k, target):
        return pltpu.make_async_remote_copy(
            src_ref=buf.at[me],
            dst_ref=buf.at[me],
            send_sem=send.at[k],
            recv_sem=recv.at[k],
            device_id=target,
            device_id_type=MESH,
        )

    def all_me(self):
        return self.i * self.nr + self.r

    def all_start(self, buf, sems):
        def go(k, c):
            self.copy(buf, sems.at[0], sems.at[1], self.all_me(), k, self.peer(k)).start()
            return c

        lax.fori_loop(1, self.ni * self.nr, go, 0)

    def all_wait(self, buf, sems):
        def go(k, c):
            self.copy(buf, sems.at[0], sems.at[1], self.all_me(), k, self.peer(k)).wait()
            return c

        lax.fori_loop(1, self.ni * self.nr, go, 0)
        return jnp.sum(buf[...], axis=0)

    def row_copies(self, buf, sems):
        return [
            self.copy(buf, sems.at[0], sems.at[1], self.r, k, (self.i, lax.rem(self.r + k, self.nr)))
            for k in range(1, self.nr)
        ]

    def img_copy(self, buf, sems, k):
        return self.copy(
            buf, sems.at[0], sems.at[1], self.i, k, (lax.rem(self.i + k, self.ni), self.r)
        )

    def row_total(self, buf, sems):
        copies = self.row_copies(buf, sems)
        for c in copies:
            c.start()
        for c in copies:
            c.wait()
        return jnp.sum(buf[...], axis=0)

    def img_total(self, buf, sems):
        def go(k, c):
            self.img_copy(buf, sems, k).start()
            return c

        def end(k, c):
            self.img_copy(buf, sems, k).wait()
            return c

        lax.fori_loop(1, self.ni, go, 0)
        lax.fori_loop(1, self.ni, end, 0)
        return jnp.sum(buf[...], axis=0)


def norm_terms(total, square, count, gain, shift):
    mean = total / count
    factor = lax.rsqrt(square / count - mean * mean + EPS)
    scale = gain * factor
    return mean, factor, scale, shift - mean * scale


def norm_back_terms(mean, factor, scale, count, s0, s1):
    slope = scale * factor * (s1 / count)
    return slope, scale * (s0 / count) - slope * mean


def forward_kernel(
    n_img,
    n_row,
    counts,
    heights,
    x_hbm,
    area,
    wr,
    g1,
    h1,
    ws,
    g2,
    h2,
    down,
    g_at,
    h_at,
    up,
    bias,
    we,
    g3,
    h3,
    fp_hbm,
    a3_hbm,
    sp_hbm,
    pd_hbm,
    mx_hbm,
    mk_hbm,
    v1,
    v2,
    v3,
    v_at,
    at_norm,
    at_out,
    w0,
    w1,
    pooled,
    gw,
    mixed_sum,
    fp,
    sp,
    pp,
    pd,
    mx,
    mk,
    xbuf,
    a3,
    acc1,
    acc2,
    gram,
    bottom,
    above,
    below,
    buf1,
    buf2,
    rbuf3,
    ibuf3,
    rbuf4,
    ibuf4,
    xsem,
    osem,
    a3sem,
    hsem,
    sem1,
    sem2,
    rsem3,
    isem3,
    rsem4,
    isem4,
):
    images, slots, cols, ch = x_hbm.shape
    mid = wr.shape[1]
    half = mid // 2
    blocks = images // GROUP
    cells = slots * cols
    links = Links(n_img, n_row)
    r = links.r
    links.greet()

    def x_copy(b, slot):
        return pltpu.make_async_copy(
            x_hbm.at[pl.ds(b * GROUP, GROUP)], xbuf.at[slot], xsem.at[slot]
        )

    x_copy(0, 0).start()

    def first(b, c):
        slot = lax.rem(b, 2)

        @pl.when(b + 1 < blocks)
        def _():
            x_copy(b + 1, 1 - slot).start()

        x_copy(b, slot).wait()
        pre = mm(xbuf[slot].reshape(GROUP * cells, ch), wr[...])
        fp[pl.ds(b * GROUP, GROUP)] = pre.reshape(GROUP, slots, cols, mid)
        return c

    lax.fori_loop(0, blocks, first, 0)
    out_fp = pltpu.make_async_copy(fp, fp_hbm, osem.at[0])
    out_fp.start()
    acc1[...] = jnp.zeros_like(acc1)

    def first_sums(i, c):
        count, height = counts[i], heights[i]
        rows = lax.broadcasted_iota(jnp.int32, (slots, cols, 128), 0)
        columns = lax.broadcasted_iota(jnp.int32, (slots, cols, 128), 1)
        m = jnp.where((rows < count) & (columns < height), 1.0, 0.0).astype(F32)
        mk[i] = m
        m = m.reshape(cells, 128)
        v = fp[i].reshape(cells, mid)
        w = v * wide(m, mid // 128)
        acc1[0] += fold(w)
        acc1[1] += fold(w * v)
        acc1[2, :, 0:128] += fold(m)
        bottom[i] = fp[i, jnp.maximum(count - 1, 0)]
        return c

    lax.fori_loop(0, images, first_sums, 0)
    out_mk = pltpu.make_async_copy(mk, mk_hbm, osem.at[1])
    out_mk.start()

    me = links.all_me()
    buf1[me, 0:1] = row_sum(acc1[0])
    buf1[me, 1:2] = row_sum(acc1[1])
    n_here = row_sum(acc1[2, :, 0:128])
    buf1[me, 2:3] = wide(n_here, mid // 128)
    buf1[me, 3:4] = jnp.zeros((1, mid), F32)

    prev_dev = (links.i, lax.rem(r + n_row - 1, n_row))
    next_dev = (links.i, lax.rem(r + 1, n_row))
    to_prev = pltpu.make_async_remote_copy(
        src_ref=fp.at[:, 0],
        dst_ref=below,
        send_sem=hsem.at[0],
        recv_sem=hsem.at[1],
        device_id=prev_dev,
        device_id_type=MESH,
    )
    to_next = pltpu.make_async_remote_copy(
        src_ref=bottom,
        dst_ref=above,
        send_sem=hsem.at[2],
        recv_sem=hsem.at[3],
        device_id=next_dev,
        device_id_type=MESH,
    )
    has_prev = r > 0
    has_next = r < n_row - 1

    links.met()
    links.all_start(buf1, sem1)

    @pl.when(has_prev)
    def _():
        to_prev.start()

    @pl.when(has_next)
    def _():
        to_next.start()

    @pl.when(jnp.logical_not(has_prev))
    def _():
        above[...] = jnp.zeros_like(above)

    @pl.when(jnp.logical_not(has_next))
    def _():
        below[...] = jnp.zeros_like(below)

    total = links.all_wait(buf1, sem1)
    n = total[2:3, 0:1]
    mean, factor, scale, offset = norm_terms(total[0:1], total[1:2], n, g1[...], h1[...])
    v1[0:1] = mean
    v1[1:2] = factor
    v1[2:3] = scale
    v1[3:4] = offset
    v1[4:5] = total[2:3]
    v1[5:8] = jnp.zeros((3, mid), F32)

    @pl.when(has_prev)
    def _():
        to_prev.wait_send()
        to_next.wait_recv()

    @pl.when(has_next)
    def _():
        to_next.wait_send()
        to_prev.wait_recv()

    prev_flag = has_prev.astype(F32)
    next_flag = has_next.astype(F32)
    ext = (slots + 2) * cols
    col_index = lax.rem(lax.broadcasted_iota(jnp.int32, (ext, mid), 0), cols)
    acc2[...] = jnp.zeros_like(acc2)

    def a3_copy(b, slot):
        return pltpu.make_async_copy(
            a3.at[slot], a3_hbm.at[pl.ds(b * GROUP, GROUP)], a3sem.at[slot]
        )

    def second(b, c):
        slot = lax.rem(b, 2)

        @pl.when(b >= 2)
        def _():
            a3_copy(b - 2, slot).wait()

        def spread(k, c):
            i = b * GROUP + k
            m = mk[i].reshape(cells, 128)
            cm = wide(m[0:cols], mid // 128)
            z = fp[i].reshape(cells, mid) * v1[2:3] + v1[3:4]
            own = z * sigmoid(z) * wide(m, mid // 128)
            z = above[i] * v1[2:3] + v1[3:4]
            top = z * sigmoid(z) * (cm * prev_flag)
            z = below[i] * v1[2:3] + v1[3:4]
            low = z * sigmoid(z) * (cm * next_flag)
            count = counts[i]
            parts = [top]
            for s in range(slots + 1):
                here = low * jnp.where(count == s, 1.0, 0.0).astype(F32)
                if s < slots:
                    here = here + own[s * cols : (s + 1) * cols]
                parts.append(here)
            full = jnp.concatenate(parts, axis=0)
            left = jnp.where(col_index == 0, 0.0, pltpu.roll(full, 1, 0)).astype(BF16)
            right = jnp.where(col_index == cols - 1, 0.0, pltpu.roll(full, ext - 1, 0)).astype(BF16)
            full = full.astype(BF16)
            pieces = []
            for g in range(2):
                for v in (left, full, right):
                    pieces.append(v[:, g * half : (g + 1) * half])
            a3[slot, k] = jnp.concatenate(pieces, axis=1).reshape(slots + 2, cols, 6 * half)
            return c

        lax.fori_loop(0, GROUP, spread, 0)
        for g in range(2):
            value = None
            for dy in range(3):
                lhs = a3[slot, :, dy : dy + slots, :, g * 3 * half : (g + 1) * 3 * half]
                part = mm(
                    lhs.reshape(GROUP * cells, 3 * half), ws[dy, :, g * mid : (g + 1) * mid]
                )
                value = part if value is None else value + part
            sp[pl.ds(b * GROUP, GROUP), :, :, g * mid : (g + 1) * mid] = value.reshape(
                GROUP, slots, cols, mid
            )
        a3_copy(b, slot).start()
        return c

    lax.fori_loop(0, blocks, second, 0)
    out_sp = pltpu.make_async_copy(sp, sp_hbm, osem.at[2])
    out_sp.start()

    def second_sums(i, c):
        m = wide(mk[i].reshape(cells, 128), mid // 128)
        for g in range(2):
            lanes = slice(g * mid, (g + 1) * mid)
            v = sp[i, :, :, lanes].reshape(cells, mid)
            w = v * m
            acc2[0, :, lanes] += fold(w)
            acc2[1, :, lanes] += fold(w * v)
        return c

    lax.fori_loop(0, images, second_sums, 0)
    buf2[me, 0:1] = row_sum(acc2[0])
    buf2[me, 1:2] = row_sum(acc2[1])
    links.all_start(buf2, sem2)
    total = links.all_wait(buf2, sem2)
    mean, factor, scale, offset = norm_terms(total[0:1], total[1:2], n, g2[...], h2[...])
    v2[0:1] = mean
    v2[1:2] = factor
    v2[2:3] = scale
    v2[3:4] = offset
    v2[4:8] = jnp.zeros((4, 2 * mid), F32)

    def second_act(i, c):
        m = wide(mk[i].reshape(cells, 128), mid // 128)
        both = None
        for g in range(2):
            lanes = slice(g * mid, (g + 1) * mid)
            z = sp[i, :, :, lanes].reshape(cells, mid) * v2[2:3, lanes] + v2[3:4, lanes]
            p = z * sigmoid(z) * m
            pp[i, :, :, lanes] = p.reshape(slots, cols, mid)
            part = fold(p)
            both = part if both is None else both + part
        pooled[pl.ds(i, 1)] = row_sum(both)
        return c

    lax.fori_loop(0, images, second_act, 0)
    pooled[...] = pooled[...] / area[...]
    rbuf3[r] = mm(pooled[...], down[...].astype(F32), HIGH)
    squeeze = links.row_total(rbuf3, rsem3)
    ibuf3[links.i, 0:1] = row_sum(squeeze)
    ibuf3[links.i, 1:2] = row_sum(squeeze * squeeze)
    total = links.img_total(ibuf3, isem3)
    mean, factor, scale, offset = norm_terms(
        total[0:1], total[1:2], float(images * n_img), g_at[...], h_at[...]
    )
    v_at[0:1] = factor
    v_at[1:8] = jnp.zeros((7, v_at.shape[1]), F32)
    at_norm[...] = (squeeze - mean) * factor
    z = at_norm[...] * g_at[...] + h_at[...]
    at_out[...] = z
    attend = z * sigmoid(z)
    upf = up[...].astype(F32)
    lean = mm(attend, upf[:, :mid] - upf[:, mid:], HIGH) + (bias[:, :mid] - bias[:, mid:])
    w0[...] = sigmoid(lean)
    w1[...] = sigmoid(-lean)

    gram[...] = jnp.zeros_like(gram)
    mixed_sum[...] = jnp.zeros_like(mixed_sum)

    def mixing(b, c):
        def one(k, c):
            i = b * GROUP + k
            p0 = pp[i, :, :, 0:mid].reshape(cells, mid)
            p1 = pp[i, :, :, mid:].reshape(cells, mid)
            v = w0[pl.ds(i, 1)] * p0 + w1[pl.ds(i, 1)] * p1
            mx[i] = v.astype(BF16).reshape(slots, cols, mid)
            pd[i] = (p0 - p1).astype(BF16).reshape(slots, cols, mid)
            return c

        lax.fori_loop(0, GROUP, one, 0)
        v = mx[pl.ds(b * GROUP, GROUP)].reshape(GROUP * cells, mid)
        gram[...] += mm_tn(v, v)
        mixed_sum[...] += mm_tn(v, jnp.ones((GROUP * cells, 128), BF16))
        return c

    lax.fori_loop(0, blocks, mixing, 0)
    out_mx = pltpu.make_async_copy(mx, mx_hbm, osem.at[4])
    out_mx.start()
    out_pd = pltpu.make_async_copy(pd, pd_hbm, osem.at[3])
    out_pd.start()
    gw[...] = mm_terms(mm, gram[...], we[...], 3)
    wef = we[...].astype(F32)
    rbuf4[r, 0:1] = row_sum(wide(mixed_sum[...], ch // 128) * wef)
    rbuf4[r, 1:2] = row_sum(gw[...] * wef)
    ibuf4[links.i] = links.row_total(rbuf4, rsem4)
    total = links.img_total(ibuf4, isem4)
    mean, factor, scale, offset = norm_terms(total[0:1], total[1:2], n, g3[...], h3[...])
    v3[0:1] = mean
    v3[1:2] = factor
    v3[2:3] = scale
    v3[3:4] = offset
    v3[4:8] = jnp.zeros((4, ch), F32)

    for slot in range(2):
        a3_copy(0, slot).wait()
    out_fp.wait()
    out_mk.wait()
    out_sp.wait()
    out_pd.wait()
    out_mx.wait()


def sd(shape, dtype=F32):
    return jax.ShapeDtypeStruct(shape, dtype)


def call_forward(n_img, n_row, args, images, slots, cols, ch, mid, inter):
    n = n_img * n_row
    cells = (images, slots, cols)
    outs = [
        (sd(cells + (mid,)), ANY),
        (sd((images, slots + 2, cols, 3 * mid), BF16), ANY),
        (sd(cells + (2 * mid,)), ANY),
        (sd(cells + (mid,), BF16), ANY),
        (sd(cells + (mid,), BF16), ANY),
        (sd(cells + (128,)), ANY),
        (sd((8, mid)), VMEM),
        (sd((8, 2 * mid)), VMEM),
        (sd((8, ch)), VMEM),
        (sd((8, inter)), VMEM),
        (sd((images, inter)), VMEM),
        (sd((images, inter)), VMEM),
        (sd((images, mid)), VMEM),
        (sd((images, mid)), VMEM),
        (sd((images, mid)), VMEM),
        (sd((mid, ch)), VMEM),
        (sd((mid, 128)), VMEM),
    ]
    dma = pltpu.SemaphoreType.DMA
    scratch = [
        pltpu.VMEM(cells + (mid,), F32),
        pltpu.VMEM(cells + (2 * mid,), F32),
        pltpu.VMEM(cells + (2 * mid,), F32),
        pltpu.VMEM(cells + (mid,), BF16),
        pltpu.VMEM(cells + (mid,), BF16),
        pltpu.VMEM(cells + (128,), F32),
        pltpu.VMEM((2, GROUP, slots, cols, ch), BF16),
        pltpu.VMEM((2, GROUP, slots + 2, cols, 3 * mid), BF16),
        pltpu.VMEM((3, 8, mid), F32),
        pltpu.VMEM((2, 8, 2 * mid), F32),
        pltpu.VMEM((mid, mid), F32),
        pltpu.VMEM((images, cols, mid), F32),
        pltpu.VMEM((images, cols, mid), F32),
        pltpu.VMEM((images, cols, mid), F32),
        pltpu.VMEM((n, 4, mid), F32),
        pltpu.VMEM((n, 2, 2 * mid), F32),
        pltpu.VMEM((n_row, images, inter), F32),
        pltpu.VMEM((n_img, 2, inter), F32),
        pltpu.VMEM((n_row, 2, ch), F32),
        pltpu.VMEM((n_img, 2, ch), F32),
        dma((2,)),
        dma((5,)),
        dma((2,)),
        dma((4,)),
        dma((2, n)),
        dma((2, n)),
        dma((2, n_row)),
        dma((2, n_img)),
        dma((2, n_row)),
        dma((2, n_img)),
    ]
    in_specs = [SMEM, SMEM, ANY] + [VMEM] * (len(args) - 3)
    return pl.pallas_call(
        functools.partial(forward_kernel, n_img, n_row),
        out_shape=[o for o, _ in outs],
        in_specs=in_specs,
        out_specs=[s for _, s in outs],
        scratch_shapes=scratch,
        name="forward",
        compiler_params=pltpu.CompilerParams(
            collective_id=0, has_side_effects=True, vmem_limit_bytes=60 * 1024 * 1024
        ),
    )(*args)


def third_kernel(
    counts, x, cot, mx, mk, we, awe, v3, bo, sg, q, m_out, tbuf
):
    step = pl.program_id(0)
    per, slots, cols, ch = x.shape
    mid = mx.shape[-1]
    cells = per * slots * cols
    t = mm(mx[...].reshape(cells, mid), we[...])
    tbuf[...] = t.reshape(tbuf.shape)

    def image(k, c):
        count = counts[step * per + k]
        m = mk[k, 0]
        m = wide(m, ch // 128)

        def row(s, c):
            zh = tbuf[k, s] * v3[0:1] + v3[1:2] + 0.5 * x[k, s].astype(F32)
            th = jnp.tanh(zh)
            up = 1.0 + th
            act = zh * up
            bo[k, s] = (act * m).astype(BF16)
            slope = up + act * (1.0 - th)
            sg[k, s] = (cot[k, s].astype(F32) * (0.5 * m) * slope).astype(BF16)
            return c

        def blank(s, c):
            bo[k, s] = jnp.zeros((cols, ch), BF16)
            sg[k, s] = jnp.zeros((cols, ch), BF16)
            return c

        lax.fori_loop(0, count, row, 0)
        lax.fori_loop(count, slots, blank, 0)
        return c

    lax.fori_loop(0, per, image, 0)
    s = sg[...].reshape(cells, ch)
    q[...] = mm(s, awe[...]).reshape(q.shape)

    @pl.when(step == 0)
    def _():
        m_out[...] = jnp.zeros_like(m_out)

    m_out[0:mid] += mm_tn(mx[...].reshape(cells, mid), s)
    m_out[mid : mid + 16] += mm(jnp.ones((16, cells), BF16), s)


def call_third(counts, x, cot, mx, mk, we, awe, v3):
    images, slots, cols, ch = x.shape
    mid = mx.shape[-1]
    per = 4

    def cells(c):
        return pl.BlockSpec((per, slots, cols, c), lambda b, *_: (b, 0, 0, 0))

    def whole(a):
        return pl.BlockSpec(a.shape, lambda b, *_: (0,) * a.ndim)

    return pl.pallas_call(
        third_kernel,
        out_shape=[
            sd(x.shape, BF16),
            sd(x.shape, BF16),
            sd((images, slots, cols, mid)),
            sd((mid + 16, ch)),
        ],
        grid_spec=pltpu.PrefetchScalarGridSpec(
            num_scalar_prefetch=1,
            grid=(images // per,),
            in_specs=[cells(ch), cells(ch), cells(mid), cells(128), whole(we), whole(awe), whole(v3)],
            out_specs=[
                cells(ch),
                cells(ch),
                cells(mid),
                pl.BlockSpec((mid + 16, ch), lambda b, *_: (0, 0)),
            ],
            scratch_shapes=[pltpu.VMEM((per, slots, cols, ch), F32)],
        ),
        name="third",
        compiler_params=pltpu.CompilerParams(vmem_limit_bytes=48 * 1024 * 1024),
    )(counts, x, cot, mx, mk, we, awe, v3)


def backward_kernel(
    n_img,
    n_row,
    counts,
    q_hbm,
    fp_hbm,
    a3_hbm,
    sp_hbm,
    pd_hbm,
    mx_hbm,
    mk_hbm,
    v1,
    v2,
    v3,
    v_at,
    at_norm,
    at_out,
    w0,
    w1,
    pooled,
    gw,
    mixed_sum,
    m_in,
    area,
    g_at,
    ws,
    down,
    up,
    we,
    awe,
    fu_hbm,
    expand_part,
    split_part,
    down_part,
    up_part,
    bias_part,
    b1,
    b2,
    b3,
    b_at,
    mg,
    fp,
    sp,
    pd,
    ub,
    mx,
    mk,
    a3,
    gpad,
    edge,
    ret,
    acc1,
    acc2,
    mb,
    dpart,
    pgrad,
    ibuf5,
    rbuf5,
    rbuf6,
    ibuf6,
    buf7,
    buf8,
    lsem,
    a3sem,
    hsem,
    rsem5,
    isem5,
    rsem6,
    isem6,
    sem7,
    sem8,
):
    images, slots, cols, mid = q_hbm.shape
    ch = we.shape[1]
    half = mid // 2
    blocks = images // GROUP
    cells = slots * cols
    links = Links(n_img, n_row)
    r, me = links.r, links.all_me()
    links.greet()
    loads = [
        pltpu.make_async_copy(src, dst, lsem.at[k])
        for k, (src, dst) in enumerate(
            [(mx_hbm, mx), (q_hbm, mg), (pd_hbm, pd), (mk_hbm, mk), (sp_hbm, sp), (fp_hbm, fp)]
        )
    ]
    for load in loads:
        load.start()

    n = v1[4:5, 0:1]
    mean3, factor3, scale3 = v3[0:1], v3[1:2], v3[2:3]
    wef = we[...].astype(F32)
    rbuf5[r, 0:1] = m_in[mid : mid + 1]
    rbuf5[r, 1:2] = factor3 * (row_sum(m_in[0:mid] * wef) - mean3 * m_in[mid : mid + 1])
    links.met()
    ibuf5[links.i] = links.row_total(rbuf5, rsem5)
    total = links.img_total(ibuf5, isem5)
    b3[...] = total
    slope3, offset3 = norm_back_terms(mean3, factor3, scale3, n, total[0:1], total[1:2])
    slope = factor3 * (total[1:2] / n)
    mb[...] = mm_terms(mm, wef * slope, awe[...], 2)
    level = total[0:1] / n - slope * mean3
    ev = mm_terms(mm, jnp.broadcast_to(level, (8, ch)), awe[...], 3)[0:1]
    expand_part[...] = (
        m_in[0:mid] * scale3 - wide(mixed_sum[...], ch // 128) * offset3 - gw[...] * slope3
    )

    for load in loads[:4]:
        load.wait()

    def mix_back(b, c):
        v = mx[pl.ds(b * GROUP, GROUP)].reshape(GROUP * cells, mid)
        high = mb[...].astype(BF16)
        fix = mm(v, high) + mm(v, (mb[...] - high.astype(F32)).astype(BF16))
        mg[pl.ds(b * GROUP, GROUP)] -= fix.reshape(GROUP, slots, cols, mid)

        def one(k, c):
            i = b * GROUP + k
            m = wide(mk[i].reshape(cells, 128), mid // 128)
            v = mg[i].reshape(cells, mid) - m * ev
            mg[i] = v.reshape(slots, cols, mid)
            d = pd[i].reshape(cells, mid).astype(F32)
            dpart[pl.ds(i, 1)] = row_sum(fold(v * d))
            return c

        lax.fori_loop(0, GROUP, one, 0)
        return c

    lax.fori_loop(0, blocks, mix_back, 0)

    upf = up[...].astype(F32)
    lean = dpart[...] * w0[...] * w1[...]
    rbuf6[r] = mm_nt(lean, upf[:, :mid] - upf[:, mid:], HIGH)
    z = at_out[...]
    attend = z * sigmoid(z)
    up_part[...] = mm_tn(attend, lean, HIGH)
    bias_part[...] = jnp.broadcast_to(row_sum(lean), bias_part.shape)
    attend_grad = links.row_total(rbuf6, rsem6) * swish_slope(z)
    ibuf6[links.i, 0:1] = row_sum(attend_grad)
    ibuf6[links.i, 1:2] = row_sum(attend_grad * at_norm[...])
    total = links.img_total(ibuf6, isem6)
    b_at[...] = total
    count = float(images * n_img)
    squeeze_grad = (
        g_at[...]
        * v_at[0:1]
        * (attend_grad - total[0:1] / count - at_norm[...] * (total[1:2] / count))
    )
    down_part[...] = mm_tn(pooled[...], squeeze_grad, HIGH)
    pgrad[...] = mm_nt(squeeze_grad, down[...].astype(F32), HIGH) / area[...]

    loads[4].wait()
    acc2[...] = jnp.zeros_like(acc2)

    def second_back(i, c):
        m = wide(mk[i].reshape(cells, 128), mid // 128)
        v = mg[i].reshape(cells, mid)
        for g, w in enumerate((w0, w1)):
            lanes = slice(g * mid, (g + 1) * mid)
            s = sp[i, :, :, lanes].reshape(cells, mid)
            z = s * v2[2:3, lanes] + v2[3:4, lanes]
            grad = (v * w[pl.ds(i, 1)] + pgrad[pl.ds(i, 1)]) * swish_slope(z) * m
            ub[i, :, :, lanes] = grad.reshape(slots, cols, mid)
            acc2[0, :, lanes] += fold(grad)
            acc2[1, :, lanes] += fold(grad * s)
        return c

    lax.fori_loop(0, images, second_back, 0)
    mean2, factor2, scale2 = v2[0:1], v2[1:2], v2[2:3]
    s0 = row_sum(acc2[0])
    buf7[me, 0:1] = s0
    buf7[me, 1:2] = factor2 * (row_sum(acc2[1]) - mean2 * s0)
    links.all_start(buf7, sem7)
    total = links.all_wait(buf7, sem7)
    b2[...] = total
    slope2, offset2 = norm_back_terms(mean2, factor2, scale2, n, total[0:1], total[1:2])

    def second_grad(grad, s, m):
        return (grad * scale2 - m * (offset2 + slope2 * s)).astype(BF16)

    prev_dev = (links.i, lax.rem(r + n_row - 1, n_row))
    next_dev = (links.i, lax.rem(r + 1, n_row))
    has_prev = r > 0
    has_next = r < n_row - 1
    to_prev = pltpu.make_async_remote_copy(
        src_ref=edge.at[0],
        dst_ref=ret.at[1],
        send_sem=hsem.at[0],
        recv_sem=hsem.at[1],
        device_id=prev_dev,
        device_id_type=MESH,
    )
    to_next = pltpu.make_async_remote_copy(
        src_ref=edge.at[1],
        dst_ref=ret.at[0],
        send_sem=hsem.at[2],
        recv_sem=hsem.at[3],
        device_id=next_dev,
        device_id_type=MESH,
    )

    def columns_back(t, lines):
        col = lax.rem(lax.broadcasted_iota(jnp.int32, (lines, half), 0), cols)
        left = jnp.where(col == cols - 1, 0.0, pltpu.roll(t[:, 0:half], lines - 1, 0))
        right = jnp.where(col == 0, 0.0, pltpu.roll(t[:, 2 * half : 3 * half], 1, 0))
        return left + t[:, half : 2 * half] + right

    for side, dy in ((0, 0), (1, 2)):

        def edge_rows(b, c):
            def one(k, c):
                i = b * GROUP + k
                at = 0 if side == 0 else jnp.maximum(counts[i] - 1, 0)
                m = wide(mk[i, 0], 2 * mid // 128)
                gpad[k, 0] = second_grad(ub[i, at], sp[i, at], m)
                return c

            lax.fori_loop(0, GROUP, one, 0)
            for g in range(2):
                v = gpad[:, 0, :, g * mid : (g + 1) * mid].reshape(GROUP * cols, mid)
                t = mm_nt(v, ws[dy, :, g * mid : (g + 1) * mid])
                edge[side, pl.ds(b * GROUP, GROUP), :, g * half : (g + 1) * half] = (
                    columns_back(t, GROUP * cols).astype(BF16).reshape(GROUP, cols, half)
                )
            return c

        lax.fori_loop(0, blocks, edge_rows, 0)
        if side == 0:

            @pl.when(has_prev)
            def _():
                to_prev.start()

        else:

            @pl.when(has_next)
            def _():
                to_next.start()

    @pl.when(jnp.logical_not(has_prev))
    def _():
        ret[0] = jnp.zeros(ret.shape[1:], BF16)

    @pl.when(jnp.logical_not(has_next))
    def _():
        ret[1] = jnp.zeros(ret.shape[1:], BF16)

    def a3_copy(b, slot):
        return pltpu.make_async_copy(
            a3_hbm.at[pl.ds(b * GROUP, GROUP)], a3.at[slot], a3sem.at[slot]
        )

    a3_copy(0, 0).start()
    gpad[:, 0] = jnp.zeros((GROUP, cols, 2 * mid), BF16)
    gpad[:, slots + 1] = jnp.zeros((GROUP, cols, 2 * mid), BF16)
    split_part[...] = jnp.zeros_like(split_part)

    def conv_back(b, c):
        slot = lax.rem(b, 2)

        @pl.when(b + 1 < blocks)
        def _():
            a3_copy(b + 1, 1 - slot).start()

        def one(k, c):
            i = b * GROUP + k
            m = wide(mk[i].reshape(cells, 128), 2 * mid // 128)
            v = second_grad(
                ub[i].reshape(cells, 2 * mid), sp[i].reshape(cells, 2 * mid), m
            )
            gpad[k, 1 : slots + 1] = v.reshape(slots, cols, 2 * mid)
            return c

        lax.fori_loop(0, GROUP, one, 0)
        for g in range(2):
            lanes = slice(g * mid, (g + 1) * mid)
            value = None
            for dy in range(3):
                v = gpad[:, 2 - dy : 2 - dy + slots, :, lanes].reshape(GROUP * cells, mid)
                part = mm_nt(v, ws[dy, :, lanes])
                value = part if value is None else value + part
            mg[pl.ds(b * GROUP, GROUP), :, :, g * half : (g + 1) * half] = columns_back(
                value, GROUP * cells
            ).reshape(GROUP, slots, cols, half)
        a3_copy(b, slot).wait()
        for g in range(2):
            lanes = slice(g * mid, (g + 1) * mid)
            v = gpad[:, 1 : slots + 1, :, lanes].reshape(GROUP * cells, mid)
            for dy in range(3):
                taps = a3[slot, :, dy : dy + slots, :, g * 3 * half : (g + 1) * 3 * half]
                split_part[dy, g] += mm_tn(v, taps.reshape(GROUP * cells, 3 * half))
        return c

    lax.fori_loop(0, blocks, conv_back, 0)

    @pl.when(has_prev)
    def _():
        to_prev.wait_send()
        to_next.wait_recv()

    @pl.when(has_next)
    def _():
        to_next.wait_send()
        to_prev.wait_recv()

    loads[5].wait()
    acc1[...] = jnp.zeros_like(acc1)

    def first_back(i, c):
        m = wide(mk[i].reshape(cells, 128), mid // 128)
        count = counts[i]
        low = ret[1, i].astype(F32)
        parts = []
        for s in range(slots):
            here = mg[i, s] + low * jnp.where(count - 1 == s, 1.0, 0.0).astype(F32)
            if s == 0:
                here = here + ret[0, i].astype(F32)
            parts.append(here)
        v = fp[i].reshape(cells, mid)
        z = v * v1[2:3] + v1[3:4]
        grad = jnp.concatenate(parts, axis=0) * swish_slope(z) * m
        mg[i] = grad.reshape(slots, cols, mid)
        acc1[0] += fold(grad)
        acc1[1] += fold(grad * v)
        return c

    lax.fori_loop(0, images, first_back, 0)
    out_fu = pltpu.make_async_copy(mg, fu_hbm, lsem.at[6])
    out_fu.start()
    s0 = row_sum(acc1[0])
    buf8[me, 0:1] = s0
    buf8[me, 1:2] = v1[1:2] * (row_sum(acc1[1]) - v1[0:1] * s0)
    links.all_start(buf8, sem8)
    total = links.all_wait(buf8, sem8)
    b1[...] = total
    out_fu.wait()


def call_backward(n_img, n_row, args, ch, inter):
    q = args[1]
    images, slots, cols, mid = q.shape
    half = mid // 2
    n = n_img * n_row
    cells = (images, slots, cols)
    outs = [
        (sd(cells + (mid,)), ANY),
        (sd((mid, ch)), VMEM),
        (sd((3, 2, mid, 3 * half)), VMEM),
        (sd((mid, inter)), VMEM),
        (sd((inter, mid)), VMEM),
        (sd((8, mid)), VMEM),
        (sd((2, mid)), VMEM),
        (sd((2, 2 * mid)), VMEM),
        (sd((2, ch)), VMEM),
        (sd((2, inter)), VMEM),
    ]
    dma = pltpu.SemaphoreType.DMA
    scratch = [
        pltpu.VMEM(cells + (mid,), F32),
        pltpu.VMEM(cells + (mid,), F32),
        pltpu.VMEM(cells + (2 * mid,), F32),
        pltpu.VMEM(cells + (mid,), BF16),
        pltpu.VMEM(cells + (2 * mid,), F32),
        pltpu.VMEM(cells + (mid,), BF16),
        pltpu.VMEM(cells + (128,), F32),
        pltpu.VMEM((2, GROUP, slots + 2, cols, 3 * mid), BF16),
        pltpu.VMEM((GROUP, slots + 2, cols, 2 * mid), BF16),
        pltpu.VMEM((2, images, cols, mid), BF16),
        pltpu.VMEM((2, images, cols, mid), BF16),
        pltpu.VMEM((2, 8, mid), F32),
        pltpu.VMEM((2, 8, 2 * mid), F32),
        pltpu.VMEM((mid, mid), F32),
        pltpu.VMEM((images, mid), F32),
        pltpu.VMEM((images, mid), F32),
        pltpu.VMEM((n_img, 2, ch), F32),
        pltpu.VMEM((n_row, 2, ch), F32),
        pltpu.VMEM((n_row, images, inter), F32),
        pltpu.VMEM((n_img, 2, inter), F32),
        pltpu.VMEM((n, 2, 2 * mid), F32),
        pltpu.VMEM((n, 2, mid), F32),
        dma((7,)),
        dma((2,)),
        dma((4,)),
        dma((2, n_row)),
        dma((2, n_img)),
        dma((2, n_row)),
        dma((2, n_img)),
        dma((2, n)),
        dma((2, n)),
    ]
    in_specs = [SMEM] + [ANY] * 7 + [VMEM] * (len(args) - 8)
    return pl.pallas_call(
        functools.partial(backward_kernel, n_img, n_row),
        out_shape=[o for o, _ in outs],
        in_specs=in_specs,
        out_specs=[s for _, s in outs],
        scratch_shapes=scratch,
        name="backward",
        compiler_params=pltpu.CompilerParams(
            collective_id=1, has_side_effects=True, vmem_limit_bytes=60 * 1024 * 1024
        ),
    )(*args)


def input_kernel(fu, fp, mk, x, sg, wr, vec, gi, red):
    per, slots, cols, ch = x.shape
    mid = fp.shape[-1]
    cells = per * slots * cols

    m = wide(mk[...].reshape(cells, 128), mid // 128)
    fg = fu[...].reshape(cells, mid) * vec[0:1] - m * (
        vec[1:2] + vec[2:3] * fp[...].reshape(cells, mid)
    )
    fg = fg.astype(BF16)
    value = mm_nt(fg, wr[...]) + sg[...].reshape(cells, ch).astype(F32)
    gi[...] = value.astype(BF16).reshape(gi.shape)

    @pl.when(pl.program_id(0) == 0)
    def _():
        red[...] = jnp.zeros_like(red)

    red[...] += mm_tn(fg, x[...].reshape(cells, ch))


def call_input(fu, fp, mk, x, sg, wr, vec):
    images, slots, cols, ch = x.shape
    mid = fp.shape[-1]
    per = 4

    def cells(c):
        return pl.BlockSpec((per, slots, cols, c), lambda b: (b, 0, 0, 0))

    def whole(a):
        return pl.BlockSpec(a.shape, lambda b: (0,) * a.ndim)

    return pl.pallas_call(
        input_kernel,
        out_shape=[sd(x.shape, BF16), sd((mid, ch))],
        grid=(images // per,),
        in_specs=[cells(mid), cells(mid), cells(128), cells(ch), cells(ch), whole(wr), whole(vec)],
        out_specs=[cells(ch), pl.BlockSpec((mid, ch), lambda b: (0, 0))],
        name="input_grad",
        compiler_params=pltpu.CompilerParams(vmem_limit_bytes=48 * 1024 * 1024),
    )(fu, fp, mk, x, sg, wr, vec)


def body(
    n_img,
    n_row,
    feature_map,
    image_group,
    row_counts,
    reduce_weight,
    gain_first,
    shift_first,
    split_weight,
    gain_second,
    shift_second,
    attn_down,
    gain_attend,
    shift_attend,
    attn_up,
    attn_bias,
    expand_weight,
    gain_third,
    shift_third,
    cotangent,
):
    images, slots, cols, ch = feature_map.shape
    mid = reduce_weight.shape[1]
    inter = attn_down.shape[1]
    half = mid // 2
    counts = row_counts[:, 0]
    heights = 12 + 2 * image_group
    area = jnp.broadcast_to((heights * heights).astype(F32)[:, None], (images, mid))
    ws = split_weight.reshape(3, 3 * half, 2 * mid)

    def line(v):
        return v[None, :]

    (
        fp, a3, sp, pd, mx, mk, v1, v2, v3, v_at, at_norm, at_out, w0, w1, pooled, gw, mixed_sum,
    ) = call_forward(
        n_img,
        n_row,
        (
            counts,
            heights,
            feature_map,
            area,
            reduce_weight,
            line(gain_first),
            line(shift_first),
            ws,
            line(gain_second),
            line(shift_second),
            attn_down,
            line(gain_attend),
            line(shift_attend),
            attn_up,
            line(attn_bias),
            expand_weight,
            line(gain_third),
            line(shift_third),
        ),
        images, slots, cols, ch, mid, inter,
    )
    awe = (expand_weight.astype(F32) * v3[2:3]).astype(BF16).T
    half_terms = jnp.concatenate([0.5 * v3[2:4], jnp.zeros((6, ch), F32)], axis=0)
    block_out, sg, q, m_sum = call_third(
        counts, feature_map, cotangent, mx, mk, expand_weight, awe, half_terms
    )
    (
        fu, expand_part, split_part, down_part, up_part, bias_part, b1, b2, b3, b_at,
    ) = call_backward(
        n_img,
        n_row,
        (
            counts, q, fp, a3, sp, pd, mx, mk, v1, v2, v3, v_at, at_norm, at_out, w0, w1, pooled,
            gw, mixed_sum, m_sum, area, line(gain_attend), ws, attn_down, attn_up, expand_weight,
            awe,
        ),
        ch, inter,
    )
    slope1, offset1 = norm_back_terms(v1[0:1], v1[1:2], v1[2:3], v1[4, 0], b1[0:1], b1[1:2])
    vec = jnp.concatenate([v1[2:3], offset1, slope1, jnp.zeros((5, mid), F32)], axis=0)
    grad_input, reduce_t = call_input(fu, fp, mk, feature_map, sg, reduce_weight, vec)

    split = split_part.reshape(3, 2, mid, 3, half).transpose(0, 3, 4, 1, 2)
    split = split.reshape(3, 3, half, 2 * mid)

    def shared(v, dim):
        v = lax.psum_scatter(v, "row", scatter_dimension=dim, tiled=True)
        return lax.psum(v, "img")

    grad_reduce = shared(reduce_t.T, 0)
    grad_split = shared(split, 2)
    grad_expand = shared(expand_part, 0)
    grad_down, grad_up, grad_bias = lax.psum((down_part, up_part, bias_part[0]), ("img", "row"))
    return (
        block_out,
        grad_input,
        grad_reduce,
        grad_split,
        grad_expand,
        grad_down,
        jnp.concatenate([grad_up, -grad_up], axis=1),
        jnp.concatenate([grad_bias, -grad_bias]),
        b1[1],
        b1[0],
        b2[1],
        b2[0],
        b_at[1],
        b_at[0],
        b3[1],
        b3[0],
    )


def solution(mesh):
    cells = P("img", "row", None, None)
    in_specs = (cells, P("img"), P("img", "row")) + (P(),) * 14 + (cells,)
    out_specs = (cells, cells, P("row", None), P(None, None, "row", None), P("row", None)) + (P(),) * 11
    return jax.shard_map(
        functools.partial(body, mesh.shape["img"], mesh.shape["row"]),
        mesh=mesh,
        in_specs=in_specs,
        out_specs=out_specs,
        check_vma=False,
    )
```

```python
import functools

import jax
import jax.numpy as jnp
from jax import lax
from jax.experimental import pallas as pl
from jax.experimental.pallas import tpu as pltpu
from jax.sharding import PartitionSpec as P

MESH = pl.DeviceIdType.MESH
HIGH = lax.Precision.HIGHEST
F32 = jnp.float32
BF16 = jnp.bfloat16
EPS = 1e-05
GROUP = 8
ANY = pl.BlockSpec(memory_space=pl.ANY)
VMEM = pl.BlockSpec(memory_space=pltpu.VMEM)
SMEM = pl.BlockSpec(memory_space=pltpu.SMEM)


def dot(a, b, dims, precision=None):
    return lax.dot_general(
        a, b, (dims, ((), ())), preferred_element_type=F32, precision=precision
    )


def mm(a, b, precision=None):
    return dot(a, b, ((1,), (0,)), precision)


def mm_nt(a, b, precision=None):
    return dot(a, b, ((1,), (1,)), precision)


def mm_tn(a, b, precision=None):
    return dot(a, b, ((0,), (0,)), precision)


def mm_terms(product, a, b, terms):
    total = None
    for _ in range(terms):
        part = a.astype(BF16)
        a = a - part.astype(F32)
        value = product(part, b)
        total = value if total is None else total + value
    return total


def sigmoid(v):
    return 0.5 * jnp.tanh(0.5 * v) + 0.5


def swish_slope(v):
    s = sigmoid(v)
    return s * (1.0 + v * (1.0 - s))


def wide(mask, times):
    return jnp.concatenate([mask] * times, axis=1)


def fold(v):
    return jnp.sum(v.reshape(v.shape[0] // 8, 8, v.shape[1]), axis=0)


def row_sum(v):
    return jnp.sum(v, axis=0, keepdims=True)


class Links:
    def __init__(self, n_img, n_row):
        self.ni, self.nr = n_img, n_row
        self.i, self.r = lax.axis_index("img"), lax.axis_index("row")

    def greet(self):
        bar = pltpu.get_barrier_semaphore()

        def go(k, c):
            pl.semaphore_signal(
                bar, inc=1, device_id=self.peer(k), device_id_type=MESH
            )
            return c

        lax.fori_loop(1, self.ni * self.nr, go, 0)

    def met(self):
        pl.semaphore_wait(pltpu.get_barrier_semaphore(), self.ni * self.nr - 1)

    def peer(self, k):
        return (lax.rem(self.i + k // self.nr, self.ni), lax.rem(self.r + k % self.nr, self.nr))

    def copy(self, buf, send, recv, me, k, target):
        return pltpu.make_async_remote_copy(
            src_ref=buf.at[me],
            dst_ref=buf.at[me],
            send_sem=send.at[k],
            recv_sem=recv.at[k],
            device_id=target,
            device_id_type=MESH,
        )

    def all_me(self):
        return self.i * self.nr + self.r

    def all_start(self, buf, sems):
        def go(k, c):
            self.copy(buf, sems.at[0], sems.at[1], self.all_me(), k, self.peer(k)).start()
            return c

        lax.fori_loop(1, self.ni * self.nr, go, 0)

    def all_wait(self, buf, sems):
        def go(k, c):
            self.copy(buf, sems.at[0], sems.at[1], self.all_me(), k, self.peer(k)).wait()
            return c

        lax.fori_loop(1, self.ni * self.nr, go, 0)
        return jnp.sum(buf[...], axis=0)

    def row_copies(self, buf, sems):
        return [
            self.copy(buf, sems.at[0], sems.at[1], self.r, k, (self.i, lax.rem(self.r + k, self.nr)))
            for k in range(1, self.nr)
        ]

    def img_copy(self, buf, sems, k):
        return self.copy(
            buf, sems.at[0], sems.at[1], self.i, k, (lax.rem(self.i + k, self.ni), self.r)
        )

    def row_total(self, buf, sems):
        copies = self.row_copies(buf, sems)
        for c in copies:
            c.start()
        for c in copies:
            c.wait()
        return jnp.sum(buf[...], axis=0)

    def img_total(self, buf, sems):
        def go(k, c):
            self.img_copy(buf, sems, k).start()
            return c

        def end(k, c):
            self.img_copy(buf, sems, k).wait()
            return c

        lax.fori_loop(1, self.ni, go, 0)
        lax.fori_loop(1, self.ni, end, 0)
        return jnp.sum(buf[...], axis=0)


class Reducer:
    @staticmethod
    def layout(n_img, rows, width, dtype):
        lane_parts = min(width // 128, n_img)
        row_parts = n_img // lane_parts
        tile = 16 if dtype == BF16 else 8
        share = -(-rows // (row_parts * tile)) * tile
        return lane_parts, share, share * row_parts

    @staticmethod
    def scratch(n_img, rows, width, dtype):
        lane_parts, share, padded = Reducer.layout(n_img, rows, width, dtype)
        lanes = width // lane_parts
        return [
            pltpu.VMEM((2, padded, width), dtype),
            pltpu.VMEM((2, padded, width), dtype),
            pltpu.VMEM((padded, width), dtype),
            pltpu.VMEM((padded, width), dtype),
            pltpu.VMEM((padded, width), F32),
            pltpu.VMEM((n_img, share, lanes), dtype),
            pltpu.VMEM((padded, width), dtype),
            pltpu.SemaphoreType.DMA((2, 2 + 2 * n_img)),
        ]

    COUNT = 8

    def __init__(self, links, rows, width, refs):
        self.links, self.rows, self.width = links, rows, width
        (self.sb1, self.rb1, self.sb2, self.rb2, self.mine, self.rb3, self.ag, self.sems) = refs
        self.dtype = self.sb1.dtype
        self.lane_parts, self.share, self.padded = Reducer.layout(links.ni, rows, width, self.dtype)
        self.lanes = width // self.lane_parts
        r = links.r
        self.one = r + 1 - 2 * lax.rem(r, 2)
        self.two = lax.rem(r + 2, 4)

    def copy(self, src, dst, k, target):
        return pltpu.make_async_remote_copy(
            src_ref=src,
            dst_ref=dst,
            send_sem=self.sems.at[0, k],
            recv_sem=self.sems.at[1, k],
            device_id=target,
            device_id_type=MESH,
        )

    def copy1(self):
        return self.copy(self.sb1, self.rb1, 0, (self.links.i, self.one))

    def copy2(self):
        return self.copy(self.sb2, self.rb2, 1, (self.links.i, self.two))

    def part(self, ref, j):
        row = pl.multiple_of((j // self.lane_parts) * self.share, self.share)
        lane = pl.multiple_of(lax.rem(j, self.lane_parts) * self.lanes, self.lanes)
        return ref.at[pl.ds(row, self.share), pl.ds(lane, self.lanes)]

    def peer(self, k):
        return lax.rem(self.links.i + k, self.links.ni)

    def copy3(self, k):
        return self.copy(
            self.part(self.sb2, self.peer(k)), self.rb3.at[self.links.i], 2 + k, (self.peer(k), self.links.r)
        )

    def copy4(self, k):
        mine = self.part(self.ag, self.links.i)
        return self.copy(mine, mine, 2 + self.links.ni + k, (self.peer(k), self.links.r))

    def each(self, make, act):
        def go(k, c):
            act(make(k))
            return c

        lax.fori_loop(1, self.links.ni, go, 0)

    def begin(self, piece):
        odd = 1 - lax.rem(self.links.r, 2)
        for k in range(2):
            self.sb1[k, 0 : self.rows] = piece(odd + 2 * k).astype(self.dtype)
        self.copy1().start()

    def second(self, piece):
        self.copy1().wait()
        r = self.links.r
        kept = self.rb1[self.two // 2, 0 : self.rows].astype(F32)
        self.sb2[0 : self.rows] = (piece(self.two) + kept).astype(self.dtype)
        self.copy2().start()
        self.mine[0 : self.rows] = piece(r) + self.rb1[r // 2, 0 : self.rows].astype(F32)

    def third(self):
        self.copy2().wait()
        total = self.mine[0 : self.rows] + self.rb2[0 : self.rows].astype(F32)
        self.mine[0 : self.rows] = total
        self.sb2[0 : self.rows] = total.astype(self.dtype)
        self.each(self.copy3, lambda c: c.start())

    def fourth(self):
        self.each(self.copy3, lambda c: c.wait())
        total = self.part(self.mine, self.links.i)[...]
        for k in range(1, self.links.ni):
            total = total + self.rb3[self.peer(k)].astype(F32)
        self.part(self.ag, self.links.i)[...] = total.astype(self.dtype)
        self.each(self.copy4, lambda c: c.start())

    def end(self):
        self.each(self.copy4, lambda c: c.wait())
        return self.ag[0 : self.rows].astype(F32)


def norm_terms(total, square, count, gain, shift):
    mean = total / count
    factor = lax.rsqrt(square / count - mean * mean + EPS)
    scale = gain * factor
    return mean, factor, scale, shift - mean * scale


def norm_back_terms(mean, factor, scale, count, s0, s1):
    slope = scale * factor * (s1 / count)
    return slope, scale * (s0 / count) - slope * mean


def forward_kernel(
    n_img,
    n_row,
    counts,
    heights,
    x_hbm,
    area,
    wr,
    g1,
    h1,
    ws,
    g2,
    h2,
    down,
    g_at,
    h_at,
    up,
    bias,
    we,
    g3,
    h3,
    fp_hbm,
    a3_hbm,
    sp_hbm,
    pd_hbm,
    mx_hbm,
    mk_hbm,
    xt_hbm,
    v1,
    v2,
    v3,
    v_at,
    at_norm,
    at_out,
    w0,
    w1,
    pooled,
    gw,
    mixed_sum,
    fp,
    sp,
    pp,
    pd,
    mx,
    mk,
    xt,
    xbuf,
    a3,
    acc1,
    acc2,
    gram,
    bottom,
    above,
    below,
    buf1,
    buf2,
    rbuf3,
    ibuf3,
    rbuf4,
    ibuf4,
    xsem,
    osem,
    a3sem,
    hsem,
    sem1,
    sem2,
    rsem3,
    isem3,
    rsem4,
    isem4,
):
    images, slots, cols, ch = x_hbm.shape
    mid = wr.shape[1]
    half = mid // 2
    blocks = images // GROUP
    cells = slots * cols
    links = Links(n_img, n_row)
    r = links.r
    links.greet()

    def x_copy(b, slot):
        return pltpu.make_async_copy(
            x_hbm.at[pl.ds(b * GROUP, GROUP)], xbuf.at[slot], xsem.at[slot]
        )

    x_copy(0, 0).start()
    pending = []

    def first(b, c):
        slot = lax.rem(b, 2)

        @pl.when(b + 1 < blocks)
        def _():
            x_copy(b + 1, 1 - slot).start()

        x_copy(b, slot).wait()
        pre = mm(xbuf[slot].reshape(GROUP * cells, ch), wr[...])
        fp[pl.ds(b * GROUP, GROUP)] = pre.reshape(GROUP, slots, cols, mid)
        return c

    lax.fori_loop(0, blocks, first, 0)
    out_fp = pltpu.make_async_copy(fp, fp_hbm, osem.at[0])
    out_fp.start()
    pending.append(out_fp)
    acc1[...] = jnp.zeros_like(acc1)

    def first_sums(i, c):
        count, height = counts[i], heights[i]
        rows = lax.broadcasted_iota(jnp.int32, (slots, cols, 128), 0)
        columns = lax.broadcasted_iota(jnp.int32, (slots, cols, 128), 1)
        m = jnp.where((rows < count) & (columns < height), 1.0, 0.0).astype(F32)
        mk[i] = m
        m = m.reshape(cells, 128)
        v = fp[i].reshape(cells, mid)
        w = v * wide(m, mid // 128)
        acc1[0] += fold(w)
        acc1[1] += fold(w * v)
        acc1[2, :, 0:128] += fold(m)
        bottom[i] = fp[i, jnp.maximum(count - 1, 0)]
        return c

    lax.fori_loop(0, images, first_sums, 0)
    out_mk = pltpu.make_async_copy(mk, mk_hbm, osem.at[1])
    out_mk.start()
    pending.append(out_mk)

    me = links.all_me()
    buf1[me, 0:1] = row_sum(acc1[0])
    buf1[me, 1:2] = row_sum(acc1[1])
    n_here = row_sum(acc1[2, :, 0:128])
    buf1[me, 2:3] = wide(n_here, mid // 128)
    buf1[me, 3:4] = jnp.zeros((1, mid), F32)

    prev_dev = (links.i, lax.rem(r + n_row - 1, n_row))
    next_dev = (links.i, lax.rem(r + 1, n_row))
    to_prev = pltpu.make_async_remote_copy(
        src_ref=fp.at[:, 0],
        dst_ref=below,
        send_sem=hsem.at[0],
        recv_sem=hsem.at[1],
        device_id=prev_dev,
        device_id_type=MESH,
    )
    to_next = pltpu.make_async_remote_copy(
        src_ref=bottom,
        dst_ref=above,
        send_sem=hsem.at[2],
        recv_sem=hsem.at[3],
        device_id=next_dev,
        device_id_type=MESH,
    )
    has_prev = r > 0
    has_next = r < n_row - 1

    links.met()
    links.all_start(buf1, sem1)

    @pl.when(has_prev)
    def _():
        to_prev.start()

    @pl.when(has_next)
    def _():
        to_next.start()

    @pl.when(jnp.logical_not(has_prev))
    def _():
        above[...] = jnp.zeros_like(above)

    @pl.when(jnp.logical_not(has_next))
    def _():
        below[...] = jnp.zeros_like(below)

    x_copy(0, 0).start()
    xt[...] = jnp.zeros_like(xt)

    def against_input(b, c):
        slot = lax.rem(b, 2)

        @pl.when(b + 1 < blocks)
        def _():
            x_copy(b + 1, 1 - slot).start()

        m = mk[pl.ds(b * GROUP, GROUP)].reshape(GROUP * cells, 128)
        v = fp[pl.ds(b * GROUP, GROUP)].reshape(GROUP * cells, mid) * wide(m, mid // 128)
        v = jnp.concatenate([v.astype(BF16), m.astype(BF16)], axis=1)
        x_copy(b, slot).wait()
        xt[...] += mm_tn(v, xbuf[slot].reshape(GROUP * cells, ch))
        return c

    lax.fori_loop(0, blocks, against_input, 0)
    out_xt = pltpu.make_async_copy(xt, xt_hbm, osem.at[5])
    out_xt.start()
    pending.append(out_xt)
    total = links.all_wait(buf1, sem1)
    n = total[2:3, 0:1]
    mean, factor, scale, offset = norm_terms(total[0:1], total[1:2], n, g1[...], h1[...])
    v1[0:1] = mean
    v1[1:2] = factor
    v1[2:3] = scale
    v1[3:4] = offset
    v1[4:5] = total[2:3]
    v1[5:8] = jnp.zeros((3, mid), F32)

    @pl.when(has_prev)
    def _():
        to_prev.wait_send()
        to_next.wait_recv()

    @pl.when(has_next)
    def _():
        to_next.wait_send()
        to_prev.wait_recv()

    prev_flag = has_prev.astype(F32)
    next_flag = has_next.astype(F32)
    ext = (slots + 2) * cols
    col_index = lax.rem(lax.broadcasted_iota(jnp.int32, (ext, mid), 0), cols)
    acc2[...] = jnp.zeros_like(acc2)

    def a3_copy(b, slot):
        return pltpu.make_async_copy(
            a3.at[slot], a3_hbm.at[pl.ds(b * GROUP, GROUP)], a3sem.at[slot]
        )

    def second(b, c):
        slot = lax.rem(b, 2)

        @pl.when(b >= 2)
        def _():
            a3_copy(b - 2, slot).wait()

        def spread(k, c):
            i = b * GROUP + k
            m = mk[i].reshape(cells, 128)
            cm = wide(m[0:cols], mid // 128)
            z = fp[i].reshape(cells, mid) * v1[2:3] + v1[3:4]
            own = z * sigmoid(z) * wide(m, mid // 128)
            z = above[i] * v1[2:3] + v1[3:4]
            top = z * sigmoid(z) * (cm * prev_flag)
            z = below[i] * v1[2:3] + v1[3:4]
            low = z * sigmoid(z) * (cm * next_flag)
            count = counts[i]
            parts = [top]
            for s in range(slots + 1):
                here = low * jnp.where(count == s, 1.0, 0.0).astype(F32)
                if s < slots:
                    here = here + own[s * cols : (s + 1) * cols]
                parts.append(here)
            full = jnp.concatenate(parts, axis=0)
            left = jnp.where(col_index == 0, 0.0, pltpu.roll(full, 1, 0)).astype(BF16)
            right = jnp.where(col_index == cols - 1, 0.0, pltpu.roll(full, ext - 1, 0)).astype(BF16)
            full = full.astype(BF16)
            pieces = []
            for g in range(2):
                for v in (left, full, right):
                    pieces.append(v[:, g * half : (g + 1) * half])
            a3[slot, k] = jnp.concatenate(pieces, axis=1).reshape(slots + 2, cols, 6 * half)
            return c

        lax.fori_loop(0, GROUP, spread, 0)
        for g in range(2):
            value = None
            for dy in range(3):
                lhs = a3[slot, :, dy : dy + slots, :, g * 3 * half : (g + 1) * 3 * half]
                part = mm(
                    lhs.reshape(GROUP * cells, 3 * half), ws[dy, :, g * mid : (g + 1) * mid]
                )
                value = part if value is None else value + part
            sp[pl.ds(b * GROUP, GROUP), :, :, g * mid : (g + 1) * mid] = value.reshape(
                GROUP, slots, cols, mid
            )
        a3_copy(b, slot).start()
        return c

    lax.fori_loop(0, blocks, second, 0)
    pending += [a3_copy(0, 0), a3_copy(0, 1)]
    out_sp = pltpu.make_async_copy(sp, sp_hbm, osem.at[2])
    out_sp.start()
    pending.append(out_sp)

    def second_sums(i, c):
        m = wide(mk[i].reshape(cells, 128), mid // 128)
        for g in range(2):
            lanes = slice(g * mid, (g + 1) * mid)
            v = sp[i, :, :, lanes].reshape(cells, mid)
            w = v * m
            acc2[0, :, lanes] += fold(w)
            acc2[1, :, lanes] += fold(w * v)
        return c

    lax.fori_loop(0, images, second_sums, 0)
    buf2[me, 0:1] = row_sum(acc2[0])
    buf2[me, 1:2] = row_sum(acc2[1])
    links.all_start(buf2, sem2)
    total = links.all_wait(buf2, sem2)
    mean, factor, scale, offset = norm_terms(total[0:1], total[1:2], n, g2[...], h2[...])
    v2[0:1] = mean
    v2[1:2] = factor
    v2[2:3] = scale
    v2[3:4] = offset
    v2[4:8] = jnp.zeros((4, 2 * mid), F32)

    def second_act(i, c):
        m = wide(mk[i].reshape(cells, 128), mid // 128)
        both = None
        for g in range(2):
            lanes = slice(g * mid, (g + 1) * mid)
            z = sp[i, :, :, lanes].reshape(cells, mid) * v2[2:3, lanes] + v2[3:4, lanes]
            p = z * sigmoid(z) * m
            pp[i, :, :, lanes] = p.reshape(slots, cols, mid)
            part = fold(p)
            both = part if both is None else both + part
        pooled[pl.ds(i, 1)] = row_sum(both)
        return c

    lax.fori_loop(0, images, second_act, 0)
    pooled[...] = pooled[...] / area[...]
    rbuf3[r] = mm(pooled[...], down[...].astype(F32), HIGH)
    squeeze = links.row_total(rbuf3, rsem3)
    ibuf3[links.i, 0:1] = row_sum(squeeze)
    ibuf3[links.i, 1:2] = row_sum(squeeze * squeeze)
    total = links.img_total(ibuf3, isem3)
    mean, factor, scale, offset = norm_terms(
        total[0:1], total[1:2], float(images * n_img), g_at[...], h_at[...]
    )
    v_at[0:1] = factor
    v_at[1:8] = jnp.zeros((7, v_at.shape[1]), F32)
    at_norm[...] = (squeeze - mean) * factor
    z = at_norm[...] * g_at[...] + h_at[...]
    at_out[...] = z
    attend = z * sigmoid(z)
    upf = up[...].astype(F32)
    lean = mm(attend, upf[:, :mid] - upf[:, mid:], HIGH) + (bias[:, :mid] - bias[:, mid:])
    w0[...] = sigmoid(lean)
    w1[...] = sigmoid(-lean)

    gram[...] = jnp.zeros_like(gram)
    mixed_sum[...] = jnp.zeros_like(mixed_sum)

    def mixing(b, c):
        def one(k, c):
            i = b * GROUP + k
            p0 = pp[i, :, :, 0:mid].reshape(cells, mid)
            p1 = pp[i, :, :, mid:].reshape(cells, mid)
            v = w0[pl.ds(i, 1)] * p0 + w1[pl.ds(i, 1)] * p1
            mx[i] = v.astype(BF16).reshape(slots, cols, mid)
            pd[i] = (p0 - p1).astype(BF16).reshape(slots, cols, mid)
            return c

        lax.fori_loop(0, GROUP, one, 0)
        v = mx[pl.ds(b * GROUP, GROUP)].reshape(GROUP * cells, mid)
        gram[...] += mm_tn(v, v)
        mixed_sum[...] += mm_tn(v, jnp.ones((GROUP * cells, 128), BF16))
        return c

    lax.fori_loop(0, blocks, mixing, 0)
    out_mx = pltpu.make_async_copy(mx, mx_hbm, osem.at[4])
    out_mx.start()
    pending.append(out_mx)
    out_pd = pltpu.make_async_copy(pd, pd_hbm, osem.at[3])
    out_pd.start()
    pending.append(out_pd)
    gw[...] = mm_terms(mm, gram[...], we[...], 3)
    wef = we[...].astype(F32)
    rbuf4[r, 0:1] = row_sum(wide(mixed_sum[...], ch // 128) * wef)
    rbuf4[r, 1:2] = row_sum(gw[...] * wef)
    ibuf4[links.i] = links.row_total(rbuf4, rsem4)
    total = links.img_total(ibuf4, isem4)
    mean, factor, scale, offset = norm_terms(total[0:1], total[1:2], n, g3[...], h3[...])
    v3[0:1] = mean
    v3[1:2] = factor
    v3[2:3] = scale
    v3[3:4] = offset
    v3[4:8] = jnp.zeros((4, ch), F32)

    for copy in pending:
        copy.wait()


def sd(shape, dtype=F32):
    return jax.ShapeDtypeStruct(shape, dtype)


def call_forward(n_img, n_row, args, images, slots, cols, ch, mid, inter):
    n = n_img * n_row
    cells = (images, slots, cols)
    outs = [
        (sd(cells + (mid,)), ANY),
        (sd((images, slots + 2, cols, 3 * mid), BF16), ANY),
        (sd(cells + (2 * mid,)), ANY),
        (sd(cells + (mid,), BF16), ANY),
        (sd(cells + (mid,), BF16), ANY),
        (sd(cells + (128,)), ANY),
        (sd((mid + 128, ch)), ANY),
        (sd((8, mid)), VMEM),
        (sd((8, 2 * mid)), VMEM),
        (sd((8, ch)), VMEM),
        (sd((8, inter)), VMEM),
        (sd((images, inter)), VMEM),
        (sd((images, inter)), VMEM),
        (sd((images, mid)), VMEM),
        (sd((images, mid)), VMEM),
        (sd((images, mid)), VMEM),
        (sd((mid, ch)), VMEM),
        (sd((mid, 128)), VMEM),
    ]
    dma = pltpu.SemaphoreType.DMA
    scratch = [
        pltpu.VMEM(cells + (mid,), F32),
        pltpu.VMEM(cells + (2 * mid,), F32),
        pltpu.VMEM(cells + (2 * mid,), F32),
        pltpu.VMEM(cells + (mid,), BF16),
        pltpu.VMEM(cells + (mid,), BF16),
        pltpu.VMEM(cells + (128,), F32),
        pltpu.VMEM((mid + 128, ch), F32),
        pltpu.VMEM((2, GROUP, slots, cols, ch), BF16),
        pltpu.VMEM((2, GROUP, slots + 2, cols, 3 * mid), BF16),
        pltpu.VMEM((3, 8, mid), F32),
        pltpu.VMEM((2, 8, 2 * mid), F32),
        pltpu.VMEM((mid, mid), F32),
        pltpu.VMEM((images, cols, mid), F32),
        pltpu.VMEM((images, cols, mid), F32),
        pltpu.VMEM((images, cols, mid), F32),
        pltpu.VMEM((n, 4, mid), F32),
        pltpu.VMEM((n, 2, 2 * mid), F32),
        pltpu.VMEM((n_row, images, inter), F32),
        pltpu.VMEM((n_img, 2, inter), F32),
        pltpu.VMEM((n_row, 2, ch), F32),
        pltpu.VMEM((n_img, 2, ch), F32),
        dma((2,)),
        dma((6,)),
        dma((2,)),
        dma((4,)),
        dma((2, n)),
        dma((2, n)),
        dma((2, n_row)),
        dma((2, n_img)),
        dma((2, n_row)),
        dma((2, n_img)),
    ]
    in_specs = [SMEM, SMEM, ANY] + [VMEM] * (len(args) - 3)
    return pl.pallas_call(
        functools.partial(forward_kernel, n_img, n_row),
        out_shape=[o for o, _ in outs],
        in_specs=in_specs,
        out_specs=[s for _, s in outs],
        scratch_shapes=scratch,
        name="forward",
        compiler_params=pltpu.CompilerParams(
            collective_id=0, has_side_effects=True, vmem_limit_bytes=60 * 1024 * 1024
        ),
    )(*args)


def third_kernel(
    counts, x, cot, mx, mk, we, awe, v3, bo, sg, q, m_out, tbuf
):
    step = pl.program_id(0)
    per, slots, cols, ch = x.shape
    mid = mx.shape[-1]
    cells = per * slots * cols
    t = mm(mx[...].reshape(cells, mid), we[...])
    tbuf[...] = t.reshape(tbuf.shape)

    def image(k, c):
        count = counts[step * per + k]
        m = mk[k, 0]
        m = wide(m, ch // 128)

        def row(s, c):
            zh = tbuf[k, s] * v3[0:1] + v3[1:2] + 0.5 * x[k, s].astype(F32)
            th = jnp.tanh(zh)
            up = 1.0 + th
            act = zh * up
            bo[k, s] = (act * m).astype(BF16)
            slope = up + act * (1.0 - th)
            sg[k, s] = (cot[k, s].astype(F32) * (0.5 * m) * slope).astype(BF16)
            return c

        def blank(s, c):
            bo[k, s] = jnp.zeros((cols, ch), BF16)
            sg[k, s] = jnp.zeros((cols, ch), BF16)
            return c

        lax.fori_loop(0, count, row, 0)
        lax.fori_loop(count, slots, blank, 0)
        return c

    lax.fori_loop(0, per, image, 0)
    s = sg[...].reshape(cells, ch)
    q[...] = mm(s, awe[...]).reshape(q.shape)

    @pl.when(step == 0)
    def _():
        m_out[...] = jnp.zeros_like(m_out)

    m_out[0:mid] += mm_tn(mx[...].reshape(cells, mid), s)
    m_out[mid : mid + 16] += mm(jnp.ones((16, cells), BF16), s)


def call_third(counts, x, cot, mx, mk, we, awe, v3):
    images, slots, cols, ch = x.shape
    mid = mx.shape[-1]
    per = 4

    def cells(c):
        return pl.BlockSpec((per, slots, cols, c), lambda b, *_: (b, 0, 0, 0))

    def whole(a):
        return pl.BlockSpec(a.shape, lambda b, *_: (0,) * a.ndim)

    return pl.pallas_call(
        third_kernel,
        out_shape=[
            sd(x.shape, BF16),
            sd(x.shape, BF16),
            sd((images, slots, cols, mid)),
            sd((mid + 16, ch)),
        ],
        grid_spec=pltpu.PrefetchScalarGridSpec(
            num_scalar_prefetch=1,
            grid=(images // per,),
            in_specs=[cells(ch), cells(ch), cells(mid), cells(128), whole(we), whole(awe), whole(v3)],
            out_specs=[
                cells(ch),
                cells(ch),
                cells(mid),
                pl.BlockSpec((mid + 16, ch), lambda b, *_: (0, 0)),
            ],
            scratch_shapes=[pltpu.VMEM((per, slots, cols, ch), F32)],
        ),
        name="third",
        compiler_params=pltpu.CompilerParams(vmem_limit_bytes=48 * 1024 * 1024),
    )(counts, x, cot, mx, mk, we, awe, v3)


def backward_kernel(
    n_img,
    n_row,
    counts,
    q_hbm,
    fp_hbm,
    a3_hbm,
    sp_hbm,
    pd_hbm,
    mx_hbm,
    mk_hbm,
    xt_hbm,
    x_hbm,
    v1,
    v2,
    v3,
    v_at,
    at_norm,
    at_out,
    w0,
    w1,
    pooled,
    gw,
    mixed_sum,
    m_in,
    area,
    g_at,
    ws,
    down,
    up,
    we,
    awe,
    fg_hbm,
    expand_out,
    split_out,
    reduce_out,
    up_out,
    down_out,
    b1,
    b2,
    b3,
    b_at,
    mg,
    sp,
    pd,
    mx,
    mk,
    split_part,
    small_part,
    rows_all,
    geb,
    edge,
    ret,
    acc1,
    acc2,
    mb,
    dpart,
    pgrad,
    ibuf5,
    rbuf5,
    rbuf6,
    ibuf6,
    buf7,
    buf8,
    lsem,
    a3sem,
    xsem,
    hsem,
    rsem5,
    isem5,
    rsem6,
    isem6,
    sem7,
    sem8,
    rsem9,
    *reducers,
):
    images, slots, cols, mid = q_hbm.shape
    ch = we.shape[1]
    inter = down.shape[1]
    half = mid // 2
    blocks = images // GROUP
    cells = slots * cols
    links = Links(n_img, n_row)
    r, me = links.r, links.all_me()
    links.greet()
    sizes = reducer_sizes(n_row, ch, mid, inter)
    count = Reducer.COUNT
    expand_red, split_red, reduce_red, small_red = [
        Reducer(links, rows, width, reducers[k * count : (k + 1) * count])
        for k, (rows, width, _) in enumerate(sizes)
    ]
    loads = [
        pltpu.make_async_copy(src, dst, lsem.at[k])
        for k, (src, dst) in enumerate(
            [(mx_hbm, mx), (q_hbm, mg), (pd_hbm, pd), (mk_hbm, mk), (sp_hbm, sp)]
        )
    ]
    for load in loads:
        load.start()
    pending = list(loads)

    n = v1[4:5, 0:1]
    mean3, factor3, scale3 = v3[0:1], v3[1:2], v3[2:3]
    wef = we[...].astype(F32)
    rbuf5[r, 0:1] = m_in[mid : mid + 1]
    rbuf5[r, 1:2] = factor3 * (row_sum(m_in[0:mid] * wef) - mean3 * m_in[mid : mid + 1])
    links.met()
    ibuf5[links.i] = links.row_total(rbuf5, rsem5)
    total = links.img_total(ibuf5, isem5)
    b3[...] = total
    slope3, offset3 = norm_back_terms(mean3, factor3, scale3, n, total[0:1], total[1:2])
    slope = factor3 * (total[1:2] / n)
    mb[...] = mm_terms(mm, wef * slope, awe[...], 2)
    level = total[0:1] / n - slope * mean3
    ev = mm_terms(mm, jnp.broadcast_to(level, (8, ch)), awe[...], 3)[0:1]

    def expand_piece(p):
        rows = pl.ds(pl.multiple_of(p * (mid // n_row), mid // n_row), mid // n_row)
        return (
            m_in[rows] * scale3 - wide(mixed_sum[rows], ch // 128) * offset3 - gw[rows] * slope3
        )

    expand_red.begin(expand_piece)

    for load in loads[:4]:
        load.wait()
    del pending[:4]

    def mix_back(b, c):
        v = mx[pl.ds(b * GROUP, GROUP)].reshape(GROUP * cells, mid)
        high = mb[...].astype(BF16)
        fix = mm(v, high) + mm(v, (mb[...] - high.astype(F32)).astype(BF16))
        mg[pl.ds(b * GROUP, GROUP)] -= fix.reshape(GROUP, slots, cols, mid)

        def one(k, c):
            i = b * GROUP + k
            m = wide(mk[i].reshape(cells, 128), mid // 128)
            v = mg[i].reshape(cells, mid) - m * ev
            mg[i] = v.reshape(slots, cols, mid)
            d = pd[i].reshape(cells, mid).astype(F32)
            dpart[pl.ds(i, 1)] = row_sum(fold(v * d))
            return c

        lax.fori_loop(0, GROUP, one, 0)
        return c

    lax.fori_loop(0, blocks, mix_back, 0)

    expand_red.second(expand_piece)
    upf = up[...].astype(F32)
    lean = dpart[...] * w0[...] * w1[...]
    rbuf6[r] = mm_nt(lean, upf[:, :mid] - upf[:, mid:], HIGH)
    z = at_out[...]
    attend = z * sigmoid(z)
    up_part = mm_tn(attend, lean, HIGH)
    buf7[me, 2:3] = wide(row_sum(lean), 2)
    attend_grad = links.row_total(rbuf6, rsem6) * swish_slope(z)
    ibuf6[links.i, 0:1] = row_sum(attend_grad)
    ibuf6[links.i, 1:2] = row_sum(attend_grad * at_norm[...])
    total = links.img_total(ibuf6, isem6)
    b_at[...] = total
    count = float(images * n_img)
    squeeze_grad = (
        g_at[...]
        * v_at[0:1]
        * (attend_grad - total[0:1] / count - at_norm[...] * (total[1:2] / count))
    )
    down_part = mm_tn(pooled[...], squeeze_grad, HIGH)
    up_rows, down_rows = inter // n_row, mid // n_row
    for p in range(n_row):
        lines = down_part[p * down_rows : (p + 1) * down_rows]
        small_part[p, 0:up_rows] = up_part[p * up_rows : (p + 1) * up_rows]
        small_part[p, up_rows:] = jnp.concatenate(
            [lines[: down_rows // 2], lines[down_rows // 2 :]], axis=1
        )

    def small_piece(p):
        return small_part[p]

    expand_red.third()
    small_red.begin(small_piece)
    pgrad[...] = mm_nt(squeeze_grad, down[...].astype(F32), HIGH) / area[...]

    prev_dev = (links.i, lax.rem(r + n_row - 1, n_row))
    next_dev = (links.i, lax.rem(r + 1, n_row))
    has_prev = r > 0
    has_next = r < n_row - 1
    to_prev = pltpu.make_async_remote_copy(
        src_ref=edge.at[0],
        dst_ref=ret.at[1],
        send_sem=hsem.at[0],
        recv_sem=hsem.at[1],
        device_id=prev_dev,
        device_id_type=MESH,
    )
    to_next = pltpu.make_async_remote_copy(
        src_ref=edge.at[1],
        dst_ref=ret.at[0],
        send_sem=hsem.at[2],
        recv_sem=hsem.at[3],
        device_id=next_dev,
        device_id_type=MESH,
    )

    def columns_back(t, lines):
        col = lax.rem(lax.broadcasted_iota(jnp.int32, (lines, half), 0), cols)
        left = jnp.where(col == cols - 1, 0.0, pltpu.roll(t[:, 0:half], lines - 1, 0))
        right = jnp.where(col == 0, 0.0, pltpu.roll(t[:, 2 * half : 3 * half], 1, 0))
        return left + t[:, half : 2 * half] + right

    def to_second_grads(ub, a3):
        loads[4].wait()
        del pending[0]
        acc2[...] = jnp.zeros_like(acc2)

        def second_back(i, c):
            m = wide(mk[i].reshape(cells, 128), mid // 128)
            v = mg[i].reshape(cells, mid)
            for g, w in enumerate((w0, w1)):
                lanes = slice(g * mid, (g + 1) * mid)
                s = sp[i, :, :, lanes].reshape(cells, mid)
                z = s * v2[2:3, lanes] + v2[3:4, lanes]
                grad = (v * w[pl.ds(i, 1)] + pgrad[pl.ds(i, 1)]) * swish_slope(z) * m
                ub[i, :, :, lanes] = grad.reshape(slots, cols, mid)
                acc2[0, :, lanes] += fold(grad)
                acc2[1, :, lanes] += fold(grad * s)
            return c

        lax.fori_loop(0, images, second_back, 0)
        expand_red.fourth()
        small_red.second(small_piece)
        mean2, factor2, scale2 = v2[0:1], v2[1:2], v2[2:3]
        s0 = row_sum(acc2[0])
        buf7[me, 0:1] = s0
        buf7[me, 1:2] = factor2 * (row_sum(acc2[1]) - mean2 * s0)
        links.all_start(buf7, sem7)
        total = links.all_wait(buf7, sem7)
        b2[...] = total
        slope2, offset2 = norm_back_terms(mean2, factor2, scale2, n, total[0:1], total[1:2])
        expand_out[...] = expand_red.end()
        small_red.third()

        def second_grad(grad, s, m):
            return (grad * scale2 - m * (offset2 + slope2 * s)).astype(BF16)

        for side, dy in ((0, 0), (1, 2)):

            def edge_rows(b, c):
                def one(k, c):
                    i = b * GROUP + k
                    at = 0 if side == 0 else jnp.maximum(counts[i] - 1, 0)
                    m = wide(mk[i, 0], 2 * mid // 128)
                    geb[k] = second_grad(ub[i, at], sp[i, at], m)
                    return c

                lax.fori_loop(0, GROUP, one, 0)
                for g in range(2):
                    v = geb[:, :, g * mid : (g + 1) * mid].reshape(GROUP * cols, mid)
                    t = mm_nt(v, ws[dy, :, g * mid : (g + 1) * mid])
                    edge[side, pl.ds(b * GROUP, GROUP), :, g * half : (g + 1) * half] = (
                        columns_back(t, GROUP * cols).astype(BF16).reshape(GROUP, cols, half)
                    )
                return c

            lax.fori_loop(0, blocks, edge_rows, 0)
            if side == 0:

                @pl.when(has_prev)
                def _():
                    to_prev.start()

            else:

                @pl.when(has_next)
                def _():
                    to_next.start()

        @pl.when(jnp.logical_not(has_prev))
        def _():
            ret[0] = jnp.zeros(ret.shape[1:], BF16)

        @pl.when(jnp.logical_not(has_next))
        def _():
            ret[1] = jnp.zeros(ret.shape[1:], BF16)

        def a3_copy(b, slot):
            return pltpu.make_async_copy(
                a3_hbm.at[pl.ds(b * GROUP, GROUP)], a3.at[slot], a3sem.at[slot]
            )

        a3_copy(0, 0).start()
        split_part[...] = jnp.zeros_like(split_part)

        def split_grads(b, c):
            slot = lax.rem(b, 2)

            @pl.when(b + 1 < blocks)
            def _():
                a3_copy(b + 1, 1 - slot).start()

            def one(k, c):
                i = b * GROUP + k
                m = wide(mk[i].reshape(cells, 128), 2 * mid // 128)
                v = second_grad(ub[i].reshape(cells, 2 * mid), sp[i].reshape(cells, 2 * mid), m)
                mx[i] = v[:, 0:mid].reshape(slots, cols, mid)
                pd[i] = v[:, mid:].reshape(slots, cols, mid)
                return c

            lax.fori_loop(0, GROUP, one, 0)
            a3_copy(b, slot).wait()
            for g, grads in enumerate((mx, pd)):
                v = grads[pl.ds(b * GROUP, GROUP)].reshape(GROUP * cells, mid)
                taps = jnp.concatenate(
                    [
                        a3[slot, :, dy : dy + slots, :, g * 3 * half : (g + 1) * 3 * half].reshape(
                            GROUP * cells, 3 * half
                        )
                        for dy in range(3)
                    ],
                    axis=1,
                )
                split_part[g] += mm_tn(v, taps)
            return c

        lax.fori_loop(0, blocks, split_grads, 0)

    pl.run_scoped(
        to_second_grads,
        pltpu.VMEM((images, slots, cols, 2 * mid), F32),
        pltpu.VMEM((2, GROUP, slots + 2, cols, 3 * mid), BF16),
    )

    def to_inputs(fp, xbuf, xt, xu, split_rows):
        loads = [
            pltpu.make_async_copy(fp_hbm, fp, lsem.at[5]),
            pltpu.make_async_copy(xt_hbm, xt, lsem.at[6]),
        ]
        for load in loads:
            load.start()
        small_red.fourth()

        def split_piece(p):
            lines = []
            for tap in range(9):
                at = pl.multiple_of(tap * half + p * (half // n_row), half // n_row)
                lines.append(split_rows[pl.ds(at, half // n_row)])
            return jnp.concatenate(lines, axis=0)

        for g in range(2):
            for tap in range(9):
                split_rows[tap * half : (tap + 1) * half, g * mid : (g + 1) * mid] = jnp.transpose(
                    split_part[g, :, tap * half : (tap + 1) * half]
                )
        split_red.begin(split_piece)

        def conv_back(b, c):
            @pl.when(b == 2)
            def _():
                split_red.second(split_piece)

            @pl.when(b == 4)
            def _():
                split_red.third()

            blank = jnp.zeros((GROUP, 1, cols, mid), BF16)
            for g, grads in enumerate((mx, pd)):
                lanes = slice(g * mid, (g + 1) * mid)
                v = grads[pl.ds(b * GROUP, GROUP)]
                moved = (
                    jnp.concatenate([v[:, 1:], blank], axis=1),
                    v,
                    jnp.concatenate([blank, v[:, : slots - 1]], axis=1),
                )
                value = None
                for dy in range(3):
                    part = mm_nt(moved[dy].reshape(GROUP * cells, mid), ws[dy, :, lanes])
                    value = part if value is None else value + part
                mg[pl.ds(b * GROUP, GROUP), :, :, g * half : (g + 1) * half] = columns_back(
                    value, GROUP * cells
                ).reshape(GROUP, slots, cols, half)
            return c

        lax.fori_loop(0, blocks, conv_back, 0)
        rows_all[r] = small_red.end()
        rows_copies = links.row_copies(rows_all, rsem9)
        for copy in rows_copies:
            copy.start()
        @pl.when(has_prev)
        def _():
            to_prev.wait_send()
            to_next.wait_recv()

        @pl.when(has_next)
        def _():
            to_next.wait_send()
            to_prev.wait_recv()

        loads[0].wait()
        acc1[...] = jnp.zeros_like(acc1)

        def first_back(i, c):
            m = wide(mk[i].reshape(cells, 128), mid // 128)
            count = counts[i]
            low = ret[1, i].astype(F32)
            parts = []
            for s in range(slots):
                here = mg[i, s] + low * jnp.where(count - 1 == s, 1.0, 0.0).astype(F32)
                if s == 0:
                    here = here + ret[0, i].astype(F32)
                parts.append(here)
            v = fp[i].reshape(cells, mid)
            z = v * v1[2:3] + v1[3:4]
            grad = jnp.concatenate(parts, axis=0) * swish_slope(z) * m
            mg[i] = grad.reshape(slots, cols, mid)
            acc1[0] += fold(grad)
            acc1[1] += fold(grad * v)
            return c

        lax.fori_loop(0, images, first_back, 0)
        s0 = row_sum(acc1[0])
        buf8[me, 0:1] = s0
        buf8[me, 1:2] = v1[1:2] * (row_sum(acc1[1]) - v1[0:1] * s0)
        links.all_start(buf8, sem8)
        split_red.fourth()

        def x_copy(b, slot):
            return pltpu.make_async_copy(
                x_hbm.at[pl.ds(b * GROUP, GROUP)], xbuf.at[slot], xsem.at[slot]
            )

        x_copy(0, 0).start()
        xu[...] = jnp.zeros_like(xu)

        def against_input(b, c):
            slot = lax.rem(b, 2)

            @pl.when(b + 1 < blocks)
            def _():
                x_copy(b + 1, 1 - slot).start()

            v = mg[pl.ds(b * GROUP, GROUP)].reshape(GROUP * cells, mid).astype(BF16)
            x_copy(b, slot).wait()
            xu[...] += mm_tn(v, xbuf[slot].reshape(GROUP * cells, ch))
            return c

        lax.fori_loop(0, blocks, against_input, 0)
        loads[1].wait()
        total = links.all_wait(buf8, sem8)
        b1[...] = total
        slope1, offset1 = norm_back_terms(v1[0:1], v1[1:2], v1[2:3], n, total[0:1], total[1:2])

        def reduce_piece(p):
            lanes = pl.ds(pl.multiple_of(p * (ch // n_row), ch // n_row), ch // n_row)
            return (
                jnp.transpose(xu[:, lanes]) * v1[2:3]
                - jnp.transpose(xt[mid : mid + 128, lanes])[:, 0:1] * offset1
                - jnp.transpose(xt[0:mid, lanes]) * slope1
            )

        reduce_red.begin(reduce_piece)

        def first_grad(i, c):
            m = wide(mk[i].reshape(cells, 128), mid // 128)
            v = mg[i].reshape(cells, mid) * v1[2:3] - m * (
                offset1 + slope1 * fp[i].reshape(cells, mid)
            )
            mx[i] = v.astype(BF16).reshape(slots, cols, mid)
            return c

        lax.fori_loop(0, images // 2, first_grad, 0)
        reduce_red.second(reduce_piece)
        lax.fori_loop(images // 2, images, first_grad, 0)
        out_fg = pltpu.make_async_copy(mx, fg_hbm, lsem.at[7])
        out_fg.start()
        reduce_red.third()
        split_out[...] = split_red.end()
        for copy in rows_copies:
            copy.wait()
        for p in range(n_row):
            up_out[p * up_rows : (p + 1) * up_rows] = rows_all[p, 0:up_rows]
            lines = rows_all[p, up_rows:]
            down_out[p * down_rows : (p + 1) * down_rows] = jnp.concatenate(
                [lines[:, 0:inter], lines[:, inter:]], axis=0
            )
        reduce_red.fourth()
        reduce_out[...] = reduce_red.end()
        out_fg.wait()

    pl.run_scoped(
        to_inputs,
        pltpu.VMEM((images, slots, cols, mid), F32),
        pltpu.VMEM((2, GROUP, slots, cols, ch), BF16),
        pltpu.VMEM((mid + 128, ch), F32),
        pltpu.VMEM((mid, ch), F32),
        pltpu.VMEM((9 * half, 2 * mid), F32),
    )


def reducer_sizes(n_row, ch, mid, inter):
    return [
        (mid // n_row, ch, BF16),
        (9 * (mid // 2) // n_row, 2 * mid, BF16),
        (ch // n_row, mid, BF16),
        (inter // n_row + mid // n_row // 2, mid, F32),
    ]


def call_backward(n_img, n_row, args, ch, inter):
    q = args[1]
    images, slots, cols, mid = q.shape
    half = mid // 2
    n = n_img * n_row
    cells = (images, slots, cols)
    sizes = reducer_sizes(n_row, ch, mid, inter)
    outs = [
        (sd(cells + (mid,), BF16), ANY),
        (sd((mid // n_row, ch)), VMEM),
        (sd((9 * half // n_row, 2 * mid)), VMEM),
        (sd((ch // n_row, mid)), VMEM),
        (sd((inter, mid)), VMEM),
        (sd((mid, inter)), VMEM),
        (sd((2, mid)), VMEM),
        (sd((3, 2 * mid)), VMEM),
        (sd((2, ch)), VMEM),
        (sd((2, inter)), VMEM),
    ]
    dma = pltpu.SemaphoreType.DMA
    scratch = [
        pltpu.VMEM(cells + (mid,), F32),
        pltpu.VMEM(cells + (2 * mid,), F32),
        pltpu.VMEM(cells + (mid,), BF16),
        pltpu.VMEM(cells + (mid,), BF16),
        pltpu.VMEM(cells + (128,), F32),
        pltpu.VMEM((2, mid, 9 * half), F32),
        pltpu.VMEM((n_row, sizes[3][0], mid), F32),
        pltpu.VMEM((n_row, sizes[3][0], mid), F32),
        pltpu.VMEM((GROUP, cols, 2 * mid), BF16),
        pltpu.VMEM((2, images, cols, mid), BF16),
        pltpu.VMEM((2, images, cols, mid), BF16),
        pltpu.VMEM((2, 8, mid), F32),
        pltpu.VMEM((2, 8, 2 * mid), F32),
        pltpu.VMEM((mid, mid), F32),
        pltpu.VMEM((images, mid), F32),
        pltpu.VMEM((images, mid), F32),
        pltpu.VMEM((n_img, 2, ch), F32),
        pltpu.VMEM((n_row, 2, ch), F32),
        pltpu.VMEM((n_row, images, inter), F32),
        pltpu.VMEM((n_img, 2, inter), F32),
        pltpu.VMEM((n, 3, 2 * mid), F32),
        pltpu.VMEM((n, 2, mid), F32),
        dma((8,)),
        dma((2,)),
        dma((2,)),
        dma((4,)),
        dma((2, n_row)),
        dma((2, n_img)),
        dma((2, n_row)),
        dma((2, n_img)),
        dma((2, n)),
        dma((2, n)),
        dma((2, n_row)),
    ]
    for rows, width, dtype in sizes:
        scratch += Reducer.scratch(n_img, rows, width, dtype)
    in_specs = [SMEM] + [ANY] * 9 + [VMEM] * (len(args) - 10)
    return pl.pallas_call(
        functools.partial(backward_kernel, n_img, n_row),
        out_shape=[o for o, _ in outs],
        in_specs=in_specs,
        out_specs=[s for _, s in outs],
        scratch_shapes=scratch,
        name="backward",
        compiler_params=pltpu.CompilerParams(
            collective_id=1, has_side_effects=True, vmem_limit_bytes=62 * 1024 * 1024
        ),
    )(*args)


def input_kernel(fg, sg, wr, gi):
    per, slots, cols, ch = sg.shape
    cells = per * slots * cols
    value = mm_nt(fg[...].reshape(cells, fg.shape[-1]), wr[...])
    gi[...] = (value + sg[...].reshape(cells, ch).astype(F32)).astype(BF16).reshape(gi.shape)


def call_input(fg, sg, wr):
    images, slots, cols, ch = sg.shape
    per = 4

    def cells(c):
        return pl.BlockSpec((per, slots, cols, c), lambda b: (b, 0, 0, 0))

    return pl.pallas_call(
        input_kernel,
        out_shape=sd(sg.shape, BF16),
        grid=(images // per,),
        in_specs=[cells(fg.shape[-1]), cells(ch), pl.BlockSpec(wr.shape, lambda b: (0, 0))],
        out_specs=cells(ch),
        name="input_grad",
        compiler_params=pltpu.CompilerParams(vmem_limit_bytes=48 * 1024 * 1024),
    )(fg, sg, wr)


def body(
    n_img,
    n_row,
    feature_map,
    image_group,
    row_counts,
    reduce_weight,
    gain_first,
    shift_first,
    split_weight,
    gain_second,
    shift_second,
    attn_down,
    gain_attend,
    shift_attend,
    attn_up,
    attn_bias,
    expand_weight,
    gain_third,
    shift_third,
    cotangent,
):
    images, slots, cols, ch = feature_map.shape
    mid = reduce_weight.shape[1]
    inter = attn_down.shape[1]
    half = mid // 2
    counts = row_counts[:, 0]
    heights = 12 + 2 * image_group
    area = jnp.broadcast_to((heights * heights).astype(F32)[:, None], (images, mid))
    ws = split_weight.reshape(3, 3 * half, 2 * mid)

    def line(v):
        return v[None, :]

    (
        fp, a3, sp, pd, mx, mk, xt, v1, v2, v3, v_at, at_norm, at_out, w0, w1, pooled, gw, mixed_sum,
    ) = call_forward(
        n_img,
        n_row,
        (
            counts,
            heights,
            feature_map,
            area,
            reduce_weight,
            line(gain_first),
            line(shift_first),
            ws,
            line(gain_second),
            line(shift_second),
            attn_down,
            line(gain_attend),
            line(shift_attend),
            attn_up,
            line(attn_bias),
            expand_weight,
            line(gain_third),
            line(shift_third),
        ),
        images, slots, cols, ch, mid, inter,
    )
    awe = (expand_weight.astype(F32) * v3[2:3]).astype(BF16).T
    half_terms = jnp.concatenate([0.5 * v3[2:4], jnp.zeros((6, ch), F32)], axis=0)
    block_out, sg, q, m_sum = call_third(
        counts, feature_map, cotangent, mx, mk, expand_weight, awe, half_terms
    )
    (
        fg, grad_expand, grad_split, grad_reduce, grad_up, grad_down, b1, b2, b3, b_at,
    ) = call_backward(
        n_img,
        n_row,
        (
            counts, q, fp, a3, sp, pd, mx, mk, xt, feature_map, v1, v2, v3, v_at, at_norm, at_out, w0, w1, pooled,
            gw, mixed_sum, m_sum, area, line(gain_attend), ws, attn_down, attn_up, expand_weight,
            awe,
        ),
        ch, inter,
    )
    grad_input = call_input(fg, sg, reduce_weight)
    grad_split = grad_split.reshape(3, 3, half // n_row, 2 * mid)
    grad_bias = b2[2, 0:mid]
    return (
        block_out,
        grad_input,
        grad_reduce,
        grad_split,
        grad_expand,
        grad_down,
        jnp.concatenate([grad_up, -grad_up], axis=1),
        jnp.concatenate([grad_bias, -grad_bias]),
        b1[1],
        b1[0],
        b2[1],
        b2[0],
        b_at[1],
        b_at[0],
        b3[1],
        b3[0],
    )


def solution(mesh):
    cells = P("img", "row", None, None)
    in_specs = (cells, P("img"), P("img", "row")) + (P(),) * 14 + (cells,)
    out_specs = (cells, cells, P("row", None), P(None, None, "row", None), P("row", None)) + (P(),) * 11
    return jax.shard_map(
        functools.partial(body, mesh.shape["img"], mesh.shape["row"]),
        mesh=mesh,
        in_specs=in_specs,
        out_specs=out_specs,
        check_vma=False,
    )
```

```python
import functools

import jax
import jax.numpy as jnp
from jax import lax
from jax.experimental import pallas as pl
from jax.experimental.pallas import tpu as pltpu
from jax.sharding import PartitionSpec as P

MESH = pl.DeviceIdType.MESH
HIGH = lax.Precision.HIGHEST
F32 = jnp.float32
BF16 = jnp.bfloat16
EPS = 1e-05
GROUP = 8
ANY = pl.BlockSpec(memory_space=pl.ANY)
VMEM = pl.BlockSpec(memory_space=pltpu.VMEM)
SMEM = pl.BlockSpec(memory_space=pltpu.SMEM)


def dot(a, b, dims, precision=None):
    return lax.dot_general(
        a, b, (dims, ((), ())), preferred_element_type=F32, precision=precision
    )


def mm(a, b, precision=None):
    return dot(a, b, ((1,), (0,)), precision)


def mm_nt(a, b, precision=None):
    return dot(a, b, ((1,), (1,)), precision)


def mm_tn(a, b, precision=None):
    return dot(a, b, ((0,), (0,)), precision)


def mm_terms(product, a, b, terms):
    total = None
    for _ in range(terms):
        part = a.astype(BF16)
        a = a - part.astype(F32)
        value = product(part, b)
        total = value if total is None else total + value
    return total


def sigmoid(v):
    return 0.5 * jnp.tanh(0.5 * v) + 0.5


def swish_slope(v):
    s = sigmoid(v)
    return s * (1.0 + v * (1.0 - s))


def wide(mask, times):
    return jnp.concatenate([mask] * times, axis=1)


def fold(v):
    return jnp.sum(v.reshape(v.shape[0] // 8, 8, v.shape[1]), axis=0)


def row_sum(v):
    return jnp.sum(v, axis=0, keepdims=True)


class Links:
    def __init__(self, n_img, n_row):
        self.ni, self.nr = n_img, n_row
        self.i, self.r = lax.axis_index("img"), lax.axis_index("row")

    def greet(self):
        bar = pltpu.get_barrier_semaphore()

        def go(k, c):
            pl.semaphore_signal(
                bar, inc=1, device_id=self.peer(k), device_id_type=MESH
            )
            return c

        lax.fori_loop(1, self.ni * self.nr, go, 0)

    def met(self):
        pl.semaphore_wait(pltpu.get_barrier_semaphore(), self.ni * self.nr - 1)

    def peer(self, k):
        return (lax.rem(self.i + k // self.nr, self.ni), lax.rem(self.r + k % self.nr, self.nr))

    def copy(self, buf, send, recv, me, k, target):
        return pltpu.make_async_remote_copy(
            src_ref=buf.at[me],
            dst_ref=buf.at[me],
            send_sem=send.at[k],
            recv_sem=recv.at[k],
            device_id=target,
            device_id_type=MESH,
        )

    def all_me(self):
        return self.i * self.nr + self.r

    def all_start(self, buf, sems):
        def go(k, c):
            self.copy(buf, sems.at[0], sems.at[1], self.all_me(), k, self.peer(k)).start()
            return c

        lax.fori_loop(1, self.ni * self.nr, go, 0)

    def all_wait(self, buf, sems):
        def go(k, c):
            self.copy(buf, sems.at[0], sems.at[1], self.all_me(), k, self.peer(k)).wait()
            return c

        lax.fori_loop(1, self.ni * self.nr, go, 0)
        return jnp.sum(buf[...], axis=0)

    def row_copies(self, buf, sems):
        return [
            self.copy(buf, sems.at[0], sems.at[1], self.r, k, (self.i, lax.rem(self.r + k, self.nr)))
            for k in range(1, self.nr)
        ]

    def img_copy(self, buf, sems, k):
        return self.copy(
            buf, sems.at[0], sems.at[1], self.i, k, (lax.rem(self.i + k, self.ni), self.r)
        )

    def row_total(self, buf, sems):
        copies = self.row_copies(buf, sems)
        for c in copies:
            c.start()
        for c in copies:
            c.wait()
        return jnp.sum(buf[...], axis=0)

    def img_total(self, buf, sems):
        def go(k, c):
            self.img_copy(buf, sems, k).start()
            return c

        def end(k, c):
            self.img_copy(buf, sems, k).wait()
            return c

        lax.fori_loop(1, self.ni, go, 0)
        lax.fori_loop(1, self.ni, end, 0)
        return jnp.sum(buf[...], axis=0)


class Reducer:
    @staticmethod
    def layout(n_img, rows, width, dtype):
        lane_parts = min(width // 128, n_img)
        row_parts = n_img // lane_parts
        tile = 16 if dtype == BF16 else 8
        share = -(-rows // (row_parts * tile)) * tile
        return lane_parts, share, share * row_parts

    @staticmethod
    def scratch(n_img, rows, width, dtype):
        lane_parts, share, padded = Reducer.layout(n_img, rows, width, dtype)
        lanes = width // lane_parts
        return [
            pltpu.VMEM((2, padded, width), dtype),
            pltpu.VMEM((2, padded, width), dtype),
            pltpu.VMEM((padded, width), dtype),
            pltpu.VMEM((padded, width), dtype),
            pltpu.VMEM((padded, width), F32),
            pltpu.VMEM((n_img, share, lanes), dtype),
            pltpu.VMEM((padded, width), dtype),
            pltpu.SemaphoreType.DMA((2, 2 + 2 * n_img)),
        ]

    COUNT = 8

    def __init__(self, links, rows, width, refs):
        self.links, self.rows, self.width = links, rows, width
        (self.sb1, self.rb1, self.sb2, self.rb2, self.mine, self.rb3, self.ag, self.sems) = refs
        self.dtype = self.sb1.dtype
        self.lane_parts, self.share, self.padded = Reducer.layout(links.ni, rows, width, self.dtype)
        self.lanes = width // self.lane_parts
        r = links.r
        self.one = r + 1 - 2 * lax.rem(r, 2)
        self.two = lax.rem(r + 2, 4)

    def copy(self, src, dst, k, target):
        return pltpu.make_async_remote_copy(
            src_ref=src,
            dst_ref=dst,
            send_sem=self.sems.at[0, k],
            recv_sem=self.sems.at[1, k],
            device_id=target,
            device_id_type=MESH,
        )

    def copy1(self):
        return self.copy(self.sb1, self.rb1, 0, (self.links.i, self.one))

    def copy2(self):
        return self.copy(self.sb2, self.rb2, 1, (self.links.i, self.two))

    def part(self, ref, j):
        row = pl.multiple_of((j // self.lane_parts) * self.share, self.share)
        lane = pl.multiple_of(lax.rem(j, self.lane_parts) * self.lanes, self.lanes)
        return ref.at[pl.ds(row, self.share), pl.ds(lane, self.lanes)]

    def peer(self, k):
        return lax.rem(self.links.i + k, self.links.ni)

    def copy3(self, k):
        return self.copy(
            self.part(self.sb2, self.peer(k)), self.rb3.at[self.links.i], 2 + k, (self.peer(k), self.links.r)
        )

    def copy4(self, k):
        mine = self.part(self.ag, self.links.i)
        return self.copy(mine, mine, 2 + self.links.ni + k, (self.peer(k), self.links.r))

    def each(self, make, act):
        def go(k, c):
            act(make(k))
            return c

        lax.fori_loop(1, self.links.ni, go, 0)

    def begin(self, piece):
        odd = 1 - lax.rem(self.links.r, 2)
        for k in range(2):
            self.sb1[k, 0 : self.rows] = piece(odd + 2 * k).astype(self.dtype)
        self.copy1().start()

    def second(self, piece):
        self.copy1().wait()
        r = self.links.r
        kept = self.rb1[self.two // 2, 0 : self.rows].astype(F32)
        self.sb2[0 : self.rows] = (piece(self.two) + kept).astype(self.dtype)
        self.copy2().start()
        self.mine[0 : self.rows] = piece(r) + self.rb1[r // 2, 0 : self.rows].astype(F32)

    def third(self):
        self.copy2().wait()
        total = self.mine[0 : self.rows] + self.rb2[0 : self.rows].astype(F32)
        self.mine[0 : self.rows] = total
        self.sb2[0 : self.rows] = total.astype(self.dtype)
        self.each(self.copy3, lambda c: c.start())

    def fourth(self):
        self.each(self.copy3, lambda c: c.wait())
        total = self.part(self.mine, self.links.i)[...]
        for k in range(1, self.links.ni):
            total = total + self.rb3[self.peer(k)].astype(F32)
        self.part(self.ag, self.links.i)[...] = total.astype(self.dtype)
        self.each(self.copy4, lambda c: c.start())

    def end(self):
        self.each(self.copy4, lambda c: c.wait())
        return self.ag[0 : self.rows].astype(F32)


def norm_terms(total, square, count, gain, shift):
    mean = total / count
    factor = lax.rsqrt(square / count - mean * mean + EPS)
    scale = gain * factor
    return mean, factor, scale, shift - mean * scale


def norm_back_terms(mean, factor, scale, count, s0, s1):
    slope = scale * factor * (s1 / count)
    return slope, scale * (s0 / count) - slope * mean


def forward_kernel(
    n_img,
    n_row,
    counts,
    group,
    x_hbm,
    wr,
    g1,
    h1,
    ws,
    g2,
    h2,
    down,
    g_at,
    h_at,
    up,
    bias,
    we,
    g3,
    h3,
    fp_hbm,
    a3_hbm,
    sp_hbm,
    pd_hbm,
    mx_hbm,
    mk_hbm,
    xt_hbm,
    v1,
    v2,
    v3,
    v_at,
    at_norm,
    at_out,
    w0,
    w1,
    pooled,
    area,
    gw,
    awe,
    wt,
    mixed_sum,
    fp,
    sp,
    pp,
    pd,
    mx,
    mk,
    xt,
    xbuf,
    a3,
    acc1,
    acc2,
    gram,
    bottom,
    above,
    below,
    buf1,
    buf2,
    rbuf3,
    ibuf3,
    rbuf4,
    ibuf4,
    xsem,
    osem,
    a3sem,
    hsem,
    sem1,
    sem2,
    rsem3,
    isem3,
    rsem4,
    isem4,
):
    images, slots, cols, ch = x_hbm.shape
    mid = wr.shape[1]
    half = mid // 2
    blocks = images // GROUP
    cells = slots * cols
    links = Links(n_img, n_row)
    r = links.r
    links.greet()

    def x_copy(b, slot):
        return pltpu.make_async_copy(
            x_hbm.at[pl.ds(b * GROUP, GROUP)], xbuf.at[slot], xsem.at[slot]
        )

    x_copy(0, 0).start()
    pending = []

    def first(b, c):
        slot = lax.rem(b, 2)

        @pl.when(b + 1 < blocks)
        def _():
            x_copy(b + 1, 1 - slot).start()

        x_copy(b, slot).wait()
        pre = mm(xbuf[slot].reshape(GROUP * cells, ch), wr[...])
        fp[pl.ds(b * GROUP, GROUP)] = pre.reshape(GROUP, slots, cols, mid)
        return c

    lax.fori_loop(0, blocks, first, 0)
    out_fp = pltpu.make_async_copy(fp, fp_hbm, osem.at[0])
    out_fp.start()
    pending.append(out_fp)
    acc1[...] = jnp.zeros_like(acc1)

    def first_sums(i, c):
        count, height = counts[i], 12 + 2 * group[i]
        area[pl.ds(i, 1)] = jnp.full((1, mid), 1, F32) * (height * height).astype(F32)
        rows = lax.broadcasted_iota(jnp.int32, (slots, cols, 128), 0)
        columns = lax.broadcasted_iota(jnp.int32, (slots, cols, 128), 1)
        m = jnp.where((rows < count) & (columns < height), 1.0, 0.0).astype(F32)
        mk[i] = m
        m = m.reshape(cells, 128)
        v = fp[i].reshape(cells, mid)
        w = v * wide(m, mid // 128)
        acc1[0] += fold(w)
        acc1[1] += fold(w * v)
        acc1[2, :, 0:128] += fold(m)
        bottom[i] = fp[i, jnp.maximum(count - 1, 0)]
        return c

    lax.fori_loop(0, images, first_sums, 0, unroll=2)
    out_mk = pltpu.make_async_copy(mk, mk_hbm, osem.at[1])
    out_mk.start()
    pending.append(out_mk)

    me = links.all_me()
    buf1[me, 0:1] = row_sum(acc1[0])
    buf1[me, 1:2] = row_sum(acc1[1])
    n_here = row_sum(acc1[2, :, 0:128])
    buf1[me, 2:3] = wide(n_here, mid // 128)
    buf1[me, 3:4] = jnp.zeros((1, mid), F32)

    prev_dev = (links.i, lax.rem(r + n_row - 1, n_row))
    next_dev = (links.i, lax.rem(r + 1, n_row))
    to_prev = pltpu.make_async_remote_copy(
        src_ref=fp.at[:, 0],
        dst_ref=below,
        send_sem=hsem.at[0],
        recv_sem=hsem.at[1],
        device_id=prev_dev,
        device_id_type=MESH,
    )
    to_next = pltpu.make_async_remote_copy(
        src_ref=bottom,
        dst_ref=above,
        send_sem=hsem.at[2],
        recv_sem=hsem.at[3],
        device_id=next_dev,
        device_id_type=MESH,
    )
    has_prev = r > 0
    has_next = r < n_row - 1

    links.met()
    links.all_start(buf1, sem1)

    @pl.when(has_prev)
    def _():
        to_prev.start()

    @pl.when(has_next)
    def _():
        to_next.start()

    @pl.when(jnp.logical_not(has_prev))
    def _():
        above[...] = jnp.zeros_like(above)

    @pl.when(jnp.logical_not(has_next))
    def _():
        below[...] = jnp.zeros_like(below)

    x_copy(0, 0).start()
    xt[...] = jnp.zeros_like(xt)

    def against_input(b, c):
        slot = lax.rem(b, 2)

        @pl.when(b + 1 < blocks)
        def _():
            x_copy(b + 1, 1 - slot).start()

        m = mk[pl.ds(b * GROUP, GROUP)].reshape(GROUP * cells, 128)
        v = fp[pl.ds(b * GROUP, GROUP)].reshape(GROUP * cells, mid) * wide(m, mid // 128)
        v = jnp.concatenate([v.astype(BF16), m.astype(BF16)], axis=1)
        x_copy(b, slot).wait()
        xt[...] += mm_tn(v, xbuf[slot].reshape(GROUP * cells, ch))
        return c

    lax.fori_loop(0, blocks, against_input, 0)
    out_xt = pltpu.make_async_copy(xt, xt_hbm, osem.at[5])
    out_xt.start()
    pending.append(out_xt)
    total = links.all_wait(buf1, sem1)
    n = total[2:3, 0:1]
    mean, factor, scale, offset = norm_terms(total[0:1], total[1:2], n, g1[...], h1[...])
    v1[0:1] = mean
    v1[1:2] = factor
    v1[2:3] = scale
    v1[3:4] = offset
    v1[4:5] = total[2:3]
    v1[5:8] = jnp.zeros((3, mid), F32)

    @pl.when(has_prev)
    def _():
        to_prev.wait_send()
        to_next.wait_recv()

    @pl.when(has_next)
    def _():
        to_next.wait_send()
        to_prev.wait_recv()

    prev_flag = has_prev.astype(F32)
    next_flag = has_next.astype(F32)
    ext = (slots + 2) * cols
    col_index = lax.rem(lax.broadcasted_iota(jnp.int32, (ext, mid), 0), cols)
    acc2[...] = jnp.zeros_like(acc2)

    def a3_copy(b, slot):
        return pltpu.make_async_copy(
            a3.at[slot], a3_hbm.at[pl.ds(b * GROUP, GROUP)], a3sem.at[slot]
        )

    def second(b, c):
        slot = lax.rem(b, 2)

        @pl.when(b >= 2)
        def _():
            a3_copy(b - 2, slot).wait()

        def spread(k, c):
            i = b * GROUP + k
            m = mk[i].reshape(cells, 128)
            cm = wide(m[0:cols], mid // 128)
            z = fp[i].reshape(cells, mid) * v1[2:3] + v1[3:4]
            own = z * sigmoid(z) * wide(m, mid // 128)
            z = above[i] * v1[2:3] + v1[3:4]
            top = z * sigmoid(z) * (cm * prev_flag)
            z = below[i] * v1[2:3] + v1[3:4]
            low = z * sigmoid(z) * (cm * next_flag)
            count = counts[i]
            parts = [top]
            for s in range(slots + 1):
                here = low * jnp.where(count == s, 1.0, 0.0).astype(F32)
                if s < slots:
                    here = here + own[s * cols : (s + 1) * cols]
                parts.append(here)
            full = jnp.concatenate(parts, axis=0)
            left = jnp.where(col_index == 0, 0.0, pltpu.roll(full, 1, 0)).astype(BF16)
            right = jnp.where(col_index == cols - 1, 0.0, pltpu.roll(full, ext - 1, 0)).astype(BF16)
            full = full.astype(BF16)
            pieces = []
            for g in range(2):
                for v in (left, full, right):
                    pieces.append(v[:, g * half : (g + 1) * half])
            a3[slot, k] = jnp.concatenate(pieces, axis=1).reshape(slots + 2, cols, 6 * half)
            return c

        lax.fori_loop(0, GROUP, spread, 0)
        for g in range(2):
            taps = jnp.concatenate(
                [
                    a3[slot, :, dy : dy + slots, :, g * 3 * half : (g + 1) * 3 * half].reshape(
                        GROUP * cells, 3 * half
                    )
                    for dy in range(3)
                ],
                axis=1,
            )
            value = mm(taps, ws[:, :, g * mid : (g + 1) * mid].reshape(9 * half, mid))
            sp[pl.ds(b * GROUP, GROUP), :, :, g * mid : (g + 1) * mid] = value.reshape(
                GROUP, slots, cols, mid
            )
        a3_copy(b, slot).start()
        return c

    lax.fori_loop(0, blocks, second, 0)
    pending += [a3_copy(0, 0), a3_copy(0, 1)]
    out_sp = pltpu.make_async_copy(sp, sp_hbm, osem.at[2])
    out_sp.start()
    pending.append(out_sp)

    def second_sums(i, c):
        m = wide(mk[i].reshape(cells, 128), mid // 128)
        for g in range(2):
            lanes = slice(g * mid, (g + 1) * mid)
            v = sp[i, :, :, lanes].reshape(cells, mid)
            w = v * m
            acc2[0, :, lanes] += fold(w)
            acc2[1, :, lanes] += fold(w * v)
        return c

    lax.fori_loop(0, images, second_sums, 0, unroll=2)
    buf2[me, 0:1] = row_sum(acc2[0])
    buf2[me, 1:2] = row_sum(acc2[1])
    links.all_start(buf2, sem2)
    for g in range(2):
        for dy in range(3):
            wt[g, dy * mid : (dy + 1) * mid] = jnp.transpose(ws[dy, :, g * mid : (g + 1) * mid])
    total = links.all_wait(buf2, sem2)
    mean, factor, scale, offset = norm_terms(total[0:1], total[1:2], n, g2[...], h2[...])
    v2[0:1] = mean
    v2[1:2] = factor
    v2[2:3] = scale
    v2[3:4] = offset
    v2[4:8] = jnp.zeros((4, 2 * mid), F32)

    def second_act(i, c):
        m = wide(mk[i].reshape(cells, 128), mid // 128)
        both = None
        for g in range(2):
            lanes = slice(g * mid, (g + 1) * mid)
            z = sp[i, :, :, lanes].reshape(cells, mid) * v2[2:3, lanes] + v2[3:4, lanes]
            p = z * sigmoid(z) * m
            pp[i, :, :, lanes] = p.reshape(slots, cols, mid)
            part = fold(p)
            both = part if both is None else both + part
        pooled[pl.ds(i, 1)] = row_sum(both)
        return c

    lax.fori_loop(0, images, second_act, 0, unroll=2)
    pooled[...] = pooled[...] / area[...]
    rbuf3[r] = mm(pooled[...], down[...].astype(F32), HIGH)
    squeeze = links.row_total(rbuf3, rsem3)
    ibuf3[links.i, 0:1] = row_sum(squeeze)
    ibuf3[links.i, 1:2] = row_sum(squeeze * squeeze)
    total = links.img_total(ibuf3, isem3)
    mean, factor, scale, offset = norm_terms(
        total[0:1], total[1:2], float(images * n_img), g_at[...], h_at[...]
    )
    v_at[0:1] = factor
    v_at[1:8] = jnp.zeros((7, v_at.shape[1]), F32)
    at_norm[...] = (squeeze - mean) * factor
    z = at_norm[...] * g_at[...] + h_at[...]
    at_out[...] = z
    attend = z * sigmoid(z)
    upf = up[...].astype(F32)
    lean = mm(attend, upf[:, :mid] - upf[:, mid:], HIGH) + (bias[:, :mid] - bias[:, mid:])
    w0[...] = sigmoid(lean)
    w1[...] = sigmoid(-lean)

    gram[...] = jnp.zeros_like(gram)
    mixed_sum[...] = jnp.zeros_like(mixed_sum)

    def mixing(b, c):
        def one(k, c):
            i = b * GROUP + k
            p0 = pp[i, :, :, 0:mid].reshape(cells, mid)
            p1 = pp[i, :, :, mid:].reshape(cells, mid)
            v = w0[pl.ds(i, 1)] * p0 + w1[pl.ds(i, 1)] * p1
            mx[i] = v.astype(BF16).reshape(slots, cols, mid)
            pd[i] = (p0 - p1).astype(BF16).reshape(slots, cols, mid)
            return c

        lax.fori_loop(0, GROUP, one, 0)
        v = mx[pl.ds(b * GROUP, GROUP)].reshape(GROUP * cells, mid)
        gram[...] += mm_tn(v, v)
        mixed_sum[...] += mm_tn(v, jnp.ones((GROUP * cells, 128), BF16))
        return c

    lax.fori_loop(0, blocks, mixing, 0)
    out_mx = pltpu.make_async_copy(mx, mx_hbm, osem.at[4])
    out_mx.start()
    pending.append(out_mx)
    out_pd = pltpu.make_async_copy(pd, pd_hbm, osem.at[3])
    out_pd.start()
    pending.append(out_pd)
    gw[...] = mm_terms(mm, gram[...], we[...], 3)
    wef = we[...].astype(F32)
    rbuf4[r, 0:1] = row_sum(wide(mixed_sum[...], ch // 128) * wef)
    rbuf4[r, 1:2] = row_sum(gw[...] * wef)
    ibuf4[links.i] = links.row_total(rbuf4, rsem4)
    total = links.img_total(ibuf4, isem4)
    mean, factor, scale, offset = norm_terms(total[0:1], total[1:2], n, g3[...], h3[...])
    v3[0:1] = mean
    v3[1:2] = factor
    v3[2:3] = scale
    v3[3:4] = offset
    v3[4:5] = 0.5 * scale
    v3[5:6] = 0.5 * offset
    v3[6:8] = jnp.zeros((2, ch), F32)
    awe[...] = (wef * scale).astype(BF16)

    for copy in pending:
        copy.wait()


def sd(shape, dtype=F32):
    return jax.ShapeDtypeStruct(shape, dtype)


def call_forward(n_img, n_row, args, images, slots, cols, ch, mid, inter):
    n = n_img * n_row
    cells = (images, slots, cols)
    outs = [
        (sd(cells + (mid,)), ANY),
        (sd((images, slots + 2, cols, 3 * mid), BF16), ANY),
        (sd(cells + (2 * mid,)), ANY),
        (sd(cells + (mid,), BF16), ANY),
        (sd(cells + (mid,), BF16), ANY),
        (sd(cells + (128,)), ANY),
        (sd((mid + 128, ch)), ANY),
        (sd((8, mid)), VMEM),
        (sd((8, 2 * mid)), VMEM),
        (sd((8, ch)), VMEM),
        (sd((8, inter)), VMEM),
        (sd((images, inter)), VMEM),
        (sd((images, inter)), VMEM),
        (sd((images, mid)), VMEM),
        (sd((images, mid)), VMEM),
        (sd((images, mid)), VMEM),
        (sd((images, mid)), VMEM),
        (sd((mid, ch)), VMEM),
        (sd((mid, ch), BF16), VMEM),
        (sd((2, 3 * mid, 3 * mid // 2), BF16), VMEM),
        (sd((mid, 128)), VMEM),
    ]
    dma = pltpu.SemaphoreType.DMA
    scratch = [
        pltpu.VMEM(cells + (mid,), F32),
        pltpu.VMEM(cells + (2 * mid,), F32),
        pltpu.VMEM(cells + (2 * mid,), F32),
        pltpu.VMEM(cells + (mid,), BF16),
        pltpu.VMEM(cells + (mid,), BF16),
        pltpu.VMEM(cells + (128,), F32),
        pltpu.VMEM((mid + 128, ch), F32),
        pltpu.VMEM((2, GROUP, slots, cols, ch), BF16),
        pltpu.VMEM((2, GROUP, slots + 2, cols, 3 * mid), BF16),
        pltpu.VMEM((3, 8, mid), F32),
        pltpu.VMEM((2, 8, 2 * mid), F32),
        pltpu.VMEM((mid, mid), F32),
        pltpu.VMEM((images, cols, mid), F32),
        pltpu.VMEM((images, cols, mid), F32),
        pltpu.VMEM((images, cols, mid), F32),
        pltpu.VMEM((n, 4, mid), F32),
        pltpu.VMEM((n, 2, 2 * mid), F32),
        pltpu.VMEM((n_row, images, inter), F32),
        pltpu.VMEM((n_img, 2, inter), F32),
        pltpu.VMEM((n_row, 2, ch), F32),
        pltpu.VMEM((n_img, 2, ch), F32),
        dma((2,)),
        dma((6,)),
        dma((2,)),
        dma((4,)),
        dma((2, n)),
        dma((2, n)),
        dma((2, n_row)),
        dma((2, n_img)),
        dma((2, n_row)),
        dma((2, n_img)),
    ]
    in_specs = [SMEM, SMEM, ANY] + [VMEM] * (len(args) - 3)
    return pl.pallas_call(
        functools.partial(forward_kernel, n_img, n_row),
        out_shape=[o for o, _ in outs],
        in_specs=in_specs,
        out_specs=[s for _, s in outs],
        scratch_shapes=scratch,
        name="forward",
        compiler_params=pltpu.CompilerParams(
            collective_id=0, has_side_effects=True, vmem_limit_bytes=60 * 1024 * 1024
        ),
    )(*args)


PART = 2


def third_kernel(x, cot, mx, mk, we, awe, v3, bo, sg, q, m_out, *parts):
    per, slots, cols, ch = x.shape
    mid = mx.shape[-1]
    cells = PART * slots * cols

    @pl.when(pl.program_id(0) == 0)
    def _():
        m_out[...] = jnp.zeros_like(m_out)

    def product(p):
        v = mx[p * PART : (p + 1) * PART].reshape(cells, mid)
        parts[p][...] = mm(v, we[...])

    product(0)
    for p in range(per // PART):
        if p + 1 < per // PART:
            product(p + 1)
        for k in range(PART):
            i = p * PART + k
            for s in range(slots):
                m = wide(mk[i, s], ch // 128)
                at = (k * slots + s) * cols
                half = parts[p][at : at + cols] * v3[4:5] + v3[5:6] + 0.5 * x[i, s].astype(F32)
                th = jnp.tanh(half)
                up = 1.0 + th
                act = half * up
                bo[i, s] = (act * m).astype(BF16)
                slope = up + act * (1.0 - th)
                sg[i, s] = (cot[i, s].astype(F32) * (0.5 * m) * slope).astype(BF16)
        v = sg[p * PART : (p + 1) * PART].reshape(cells, ch)
        q[p * PART : (p + 1) * PART] = mm_nt(v, awe[...]).reshape(PART, slots, cols, mid)
    v = sg[...].reshape(per * slots * cols, ch)
    m_out[0:mid] += mm_tn(mx[...].reshape(per * slots * cols, mid), v)
    m_out[mid : mid + 16] += mm(jnp.ones((16, per * slots * cols), BF16), v)


def call_third(x, cot, mx, mk, we, awe, v3):
    images, slots, cols, ch = x.shape
    mid = mx.shape[-1]
    per = 8

    def cells(c):
        return pl.BlockSpec((per, slots, cols, c), lambda b: (b, 0, 0, 0))

    def whole(a):
        return pl.BlockSpec(a.shape, lambda b: (0,) * a.ndim)

    return pl.pallas_call(
        third_kernel,
        out_shape=[
            sd(x.shape, BF16),
            sd(x.shape, BF16),
            sd((images, slots, cols, mid)),
            sd((mid + 16, ch)),
        ],
        grid=(images // per,),
        in_specs=[cells(ch), cells(ch), cells(mid), cells(128), whole(we), whole(awe), whole(v3)],
        out_specs=[
            cells(ch),
            cells(ch),
            cells(mid),
            pl.BlockSpec((mid + 16, ch), lambda b: (0, 0)),
        ],
        scratch_shapes=[pltpu.VMEM((PART * slots * cols, ch), F32)] * (per // PART),
        name="third",
        compiler_params=pltpu.CompilerParams(vmem_limit_bytes=60 * 1024 * 1024),
    )(x, cot, mx, mk, we, awe, v3)


def backward_kernel(
    n_img,
    n_row,
    counts,
    q_hbm,
    fp_hbm,
    a3_hbm,
    sp_hbm,
    pd_hbm,
    mx_hbm,
    mk_hbm,
    xt_hbm,
    x_hbm,
    v1,
    v2,
    v3,
    v_at,
    at_norm,
    at_out,
    w0,
    w1,
    pooled,
    gw,
    mixed_sum,
    m_in,
    area,
    g_at,
    wt,
    down,
    up,
    we,
    awe,
    fg_hbm,
    expand_out,
    split_out,
    reduce_out,
    up_out,
    down_out,
    bias_out,
    b1,
    b2,
    b3,
    b_at,
    mg,
    pd,
    mx,
    mk,
    split_part,
    small_part,
    rows_all,
    edge,
    ret,
    acc1,
    acc2,
    mb,
    dpart,
    pgrad,
    ibuf5,
    rbuf5,
    rbuf6,
    ibuf6,
    buf7,
    buf8,
    lsem,
    a3sem,
    hsem,
    rsem5,
    isem5,
    rsem6,
    isem6,
    sem7,
    sem8,
    rsem9,
    *reducers,
):
    images, slots, cols, mid = q_hbm.shape
    ch = we.shape[1]
    inter = down.shape[1]
    half = mid // 2
    blocks = images // GROUP
    cells = slots * cols
    links = Links(n_img, n_row)
    r, me = links.r, links.all_me()
    links.greet()
    sizes = reducer_sizes(n_row, ch, mid, inter)
    count = Reducer.COUNT
    expand_red, split_red, reduce_red, small_red = [
        Reducer(links, rows, width, reducers[k * count : (k + 1) * count])
        for k, (rows, width, _) in enumerate(sizes)
    ]
    n = v1[4:5, 0:1]
    up_rows, down_rows = inter // n_row, mid // n_row
    prev_dev = (links.i, lax.rem(r + n_row - 1, n_row))
    next_dev = (links.i, lax.rem(r + 1, n_row))
    has_prev = r > 0
    has_next = r < n_row - 1
    to_prev = pltpu.make_async_remote_copy(
        src_ref=edge.at[0],
        dst_ref=ret.at[1],
        send_sem=hsem.at[0],
        recv_sem=hsem.at[1],
        device_id=prev_dev,
        device_id_type=MESH,
    )
    to_next = pltpu.make_async_remote_copy(
        src_ref=edge.at[1],
        dst_ref=ret.at[0],
        send_sem=hsem.at[2],
        recv_sem=hsem.at[3],
        device_id=next_dev,
        device_id_type=MESH,
    )

    def columns_back(t, lines):
        col = lax.rem(lax.broadcasted_iota(jnp.int32, (lines, half), 0), cols)
        left = jnp.where(col == cols - 1, 0.0, pltpu.roll(t[:, 0:half], lines - 1, 0))
        right = jnp.where(col == 0, 0.0, pltpu.roll(t[:, 2 * half : 3 * half], 1, 0))
        return left + t[:, half : 2 * half] + right

    def small_piece(p):
        return small_part[p]

    def to_second_grads(sp):
        loads = [
            pltpu.make_async_copy(src, dst, lsem.at[k])
            for k, (src, dst) in enumerate(
                [(mx_hbm, mx), (q_hbm, mg), (pd_hbm, pd), (mk_hbm, mk), (sp_hbm, sp)]
            )
        ]
        for load in loads:
            load.start()
        pending = list(loads)

        mean3, factor3, scale3 = v3[0:1], v3[1:2], v3[2:3]
        wef = we[...].astype(F32)
        rbuf5[r, 0:1] = m_in[mid : mid + 1]
        rbuf5[r, 1:2] = factor3 * (row_sum(m_in[0:mid] * wef) - mean3 * m_in[mid : mid + 1])
        links.met()
        ibuf5[links.i] = links.row_total(rbuf5, rsem5)
        total = links.img_total(ibuf5, isem5)
        b3[...] = total
        slope3, offset3 = norm_back_terms(mean3, factor3, scale3, n, total[0:1], total[1:2])
        slope = factor3 * (total[1:2] / n)
        mb[...] = mm_terms(mm_nt, wef * slope, awe[...], 2)
        level = total[0:1] / n - slope * mean3
        ev = mm_terms(mm_nt, jnp.broadcast_to(level, (8, ch)), awe[...], 3)[0:1]

        def expand_piece(p):
            rows = pl.ds(pl.multiple_of(p * (mid // n_row), mid // n_row), mid // n_row)
            return (
                m_in[rows] * scale3 - wide(mixed_sum[rows], ch // 128) * offset3 - gw[rows] * slope3
            )

        expand_red.begin(expand_piece)

        for load in loads[:4]:
            load.wait()
        del pending[:4]

        def mix_back(b, c):
            v = mx[pl.ds(b * GROUP, GROUP)].reshape(GROUP * cells, mid)
            high = mb[...].astype(BF16)
            fix = mm(v, high) + mm(v, (mb[...] - high.astype(F32)).astype(BF16))
            mg[pl.ds(b * GROUP, GROUP)] -= fix.reshape(GROUP, slots, cols, mid)

            def one(k, c):
                i = b * GROUP + k
                m = wide(mk[i].reshape(cells, 128), mid // 128)
                v = mg[i].reshape(cells, mid) - m * ev
                mg[i] = v.reshape(slots, cols, mid)
                d = pd[i].reshape(cells, mid).astype(F32)
                dpart[pl.ds(i, 1)] = row_sum(fold(v * d))
                return c

            lax.fori_loop(0, GROUP, one, 0)
            return c

        lax.fori_loop(0, blocks, mix_back, 0)

        expand_red.second(expand_piece)
        upf = up[...].astype(F32)
        lean = dpart[...] * w0[...] * w1[...]
        rbuf6[r] = mm_nt(lean, upf[:, :mid] - upf[:, mid:], HIGH)
        z = at_out[...]
        attend = z * sigmoid(z)
        up_part = mm_tn(attend, lean, HIGH)
        bias_part = row_sum(lean)
        attend_grad = links.row_total(rbuf6, rsem6) * swish_slope(z)
        ibuf6[links.i, 0:1] = row_sum(attend_grad)
        ibuf6[links.i, 1:2] = row_sum(attend_grad * at_norm[...])
        total = links.img_total(ibuf6, isem6)
        b_at[...] = total
        count = float(images * n_img)
        squeeze_grad = (
            g_at[...]
            * v_at[0:1]
            * (attend_grad - total[0:1] / count - at_norm[...] * (total[1:2] / count))
        )
        down_part = mm_tn(pooled[...], squeeze_grad, HIGH)
        for p in range(n_row):
            lines = down_part[p * down_rows : (p + 1) * down_rows]
            small_part[p, 0:up_rows] = up_part[p * up_rows : (p + 1) * up_rows]
            small_part[p, up_rows : up_rows + down_rows // 2] = jnp.concatenate(
                [lines[: down_rows // 2], lines[down_rows // 2 :]], axis=1
            )
            small_part[p, up_rows + down_rows // 2 :] = jnp.broadcast_to(bias_part, (8, mid))

        expand_red.third()
        small_red.begin(small_piece)
        pgrad[...] = mm_nt(squeeze_grad, down[...].astype(F32), HIGH) / area[...]

        def with_second_grads(ub, a3, geb):
            loads[4].wait()
            del pending[0]
            acc2[...] = jnp.zeros_like(acc2)

            def second_back(i, c):
                m = wide(mk[i].reshape(cells, 128), mid // 128)
                v = mg[i].reshape(cells, mid)
                for g, w in enumerate((w0, w1)):
                    lanes = slice(g * mid, (g + 1) * mid)
                    s = sp[i, :, :, lanes].reshape(cells, mid)
                    z = s * v2[2:3, lanes] + v2[3:4, lanes]
                    grad = (v * w[pl.ds(i, 1)] + pgrad[pl.ds(i, 1)]) * swish_slope(z) * m
                    ub[i, :, :, lanes] = grad.reshape(slots, cols, mid)
                    acc2[0, :, lanes] += fold(grad)
                    acc2[1, :, lanes] += fold(grad * s)
                return c

            lax.fori_loop(0, images, second_back, 0, unroll=2)
            expand_red.fourth()
            small_red.second(small_piece)
            mean2, factor2, scale2 = v2[0:1], v2[1:2], v2[2:3]
            s0 = row_sum(acc2[0])
            buf7[me, 0:1] = s0
            buf7[me, 1:2] = factor2 * (row_sum(acc2[1]) - mean2 * s0)
            links.all_start(buf7, sem7)
            total = links.all_wait(buf7, sem7)
            b2[...] = total
            slope2, offset2 = norm_back_terms(mean2, factor2, scale2, n, total[0:1], total[1:2])
            expand_out[...] = expand_red.end()
            small_red.third()

            def second_grad(grad, s, m):
                return (grad * scale2 - m * (offset2 + slope2 * s)).astype(BF16)

            for side, dy in ((0, 0), (1, 2)):

                def edge_rows(i, c):
                    at = 0 if side == 0 else jnp.maximum(counts[i] - 1, 0)
                    m = wide(mk[i, 0], 2 * mid // 128)
                    geb[i] = second_grad(ub[i, at], sp[i, at], m)
                    return c

                lax.fori_loop(0, images, edge_rows, 0, unroll=2)
                for g in range(2):
                    v = geb[:, :, g * mid : (g + 1) * mid].reshape(images * cols, mid)
                    t = mm(v, wt[g, dy * mid : (dy + 1) * mid])
                    edge[side, :, :, g * half : (g + 1) * half] = (
                        columns_back(t, images * cols).astype(BF16).reshape(images, cols, half)
                    )
                if side == 0:

                    @pl.when(has_prev)
                    def _():
                        to_prev.start()

                else:

                    @pl.when(has_next)
                    def _():
                        to_next.start()

            @pl.when(jnp.logical_not(has_prev))
            def _():
                ret[0] = jnp.zeros(ret.shape[1:], BF16)

            @pl.when(jnp.logical_not(has_next))
            def _():
                ret[1] = jnp.zeros(ret.shape[1:], BF16)

            def a3_copy(b, slot):
                return pltpu.make_async_copy(
                    a3_hbm.at[pl.ds(b * GROUP, GROUP)], a3.at[slot], a3sem.at[slot]
                )

            a3_copy(0, 0).start()
            split_part[...] = jnp.zeros_like(split_part)

            def split_grads(b, c):
                slot = lax.rem(b, 2)

                @pl.when(b + 1 < blocks)
                def _():
                    a3_copy(b + 1, 1 - slot).start()

                def one(k, c):
                    i = b * GROUP + k
                    m = wide(mk[i].reshape(cells, 128), 2 * mid // 128)
                    v = second_grad(ub[i].reshape(cells, 2 * mid), sp[i].reshape(cells, 2 * mid), m)
                    mx[i] = v[:, 0:mid].reshape(slots, cols, mid)
                    pd[i] = v[:, mid:].reshape(slots, cols, mid)
                    return c

                lax.fori_loop(0, GROUP, one, 0)
                a3_copy(b, slot).wait()
                for g, grads in enumerate((mx, pd)):
                    v = grads[pl.ds(b * GROUP, GROUP)].reshape(GROUP * cells, mid)
                    taps = jnp.concatenate(
                        [
                            a3[slot, :, dy : dy + slots, :, g * 3 * half : (g + 1) * 3 * half].reshape(
                                GROUP * cells, 3 * half
                            )
                            for dy in range(3)
                        ],
                        axis=1,
                    )
                    split_part[g] += mm_tn(v, taps)
                return c

            lax.fori_loop(0, blocks, split_grads, 0)

        pl.run_scoped(
            with_second_grads,
            pltpu.VMEM((images, slots, cols, 2 * mid), F32),
            pltpu.VMEM((2, GROUP, slots + 2, cols, 3 * mid), BF16),
            pltpu.VMEM((images, cols, 2 * mid), BF16),
        )

    pl.run_scoped(to_second_grads, pltpu.VMEM((images, slots, cols, 2 * mid), F32))

    def to_inputs(fp, xs, xt, xu, split_rows):
        loads = [
            pltpu.make_async_copy(fp_hbm, fp, lsem.at[5]),
            pltpu.make_async_copy(xt_hbm, xt, lsem.at[6]),
            pltpu.make_async_copy(x_hbm, xs, lsem.at[4]),
        ]
        for load in loads:
            load.start()
        small_red.fourth()

        def split_piece(p):
            lines = []
            for tap in range(9):
                at = pl.multiple_of(tap * half + p * (half // n_row), half // n_row)
                lines.append(split_rows[pl.ds(at, half // n_row)])
            return jnp.concatenate(lines, axis=0).astype(F32)

        for g in range(2):
            for tap in range(9):
                split_rows[tap * half : (tap + 1) * half, g * mid : (g + 1) * mid] = jnp.transpose(
                    split_part[g, :, tap * half : (tap + 1) * half].astype(BF16)
                )
        split_red.begin(split_piece)

        def conv_back(b, c):
            @pl.when(b == 2)
            def _():
                split_red.second(split_piece)

            @pl.when(b == 5)
            def _():
                split_red.third()

            blank = jnp.zeros((GROUP, 1, cols, mid), BF16)
            for g, grads in enumerate((mx, pd)):
                v = grads[pl.ds(b * GROUP, GROUP)]
                moved = (
                    jnp.concatenate([v[:, 1:], blank], axis=1),
                    v,
                    jnp.concatenate([blank, v[:, : slots - 1]], axis=1),
                )
                v = jnp.concatenate(
                    [moved[dy].reshape(GROUP * cells, mid) for dy in range(3)], axis=1
                )
                value = mm(v, wt[g])
                mg[pl.ds(b * GROUP, GROUP), :, :, g * half : (g + 1) * half] = columns_back(
                    value, GROUP * cells
                ).reshape(GROUP, slots, cols, half)
            return c

        lax.fori_loop(0, blocks, conv_back, 0)
        rows_all[r] = small_red.end()
        rows_copies = links.row_copies(rows_all, rsem9)
        for copy in rows_copies:
            copy.start()
        @pl.when(has_prev)
        def _():
            to_prev.wait_send()
            to_next.wait_recv()

        @pl.when(has_next)
        def _():
            to_next.wait_send()
            to_prev.wait_recv()

        loads[0].wait()
        acc1[...] = jnp.zeros_like(acc1)

        def first_back(i, c):
            m = wide(mk[i].reshape(cells, 128), mid // 128)
            count = counts[i]
            low = ret[1, i].astype(F32)
            parts = []
            for s in range(slots):
                here = mg[i, s] + low * jnp.where(count - 1 == s, 1.0, 0.0).astype(F32)
                if s == 0:
                    here = here + ret[0, i].astype(F32)
                parts.append(here)
            v = fp[i].reshape(cells, mid)
            z = v * v1[2:3] + v1[3:4]
            grad = jnp.concatenate(parts, axis=0) * swish_slope(z) * m
            mg[i] = grad.reshape(slots, cols, mid)
            pd[i] = grad.astype(BF16).reshape(slots, cols, mid)
            acc1[0] += fold(grad)
            acc1[1] += fold(grad * v)
            return c

        lax.fori_loop(0, images, first_back, 0, unroll=2)
        s0 = row_sum(acc1[0])
        buf8[me, 0:1] = s0
        buf8[me, 1:2] = v1[1:2] * (row_sum(acc1[1]) - v1[0:1] * s0)
        links.all_start(buf8, sem8)
        loads[2].wait()
        lines = images * cells
        width = ch // 2
        for k in range(2):
            xu[:, k * width : (k + 1) * width] = mm_tn(
                pd[...].reshape(lines, mid), xs[:, :, :, k * width : (k + 1) * width].reshape(lines, width)
            )
        loads[1].wait()
        total = links.all_wait(buf8, sem8)
        b1[...] = total
        slope1, offset1 = norm_back_terms(v1[0:1], v1[1:2], v1[2:3], n, total[0:1], total[1:2])

        def column(v):
            return wide(jnp.transpose(jnp.broadcast_to(v, (128, mid))), ch // n_row // 128)

        scale_c, slope_c, offset_c = column(v1[2:3]), column(slope1), column(offset1)

        def reduce_piece(p):
            lanes = pl.ds(pl.multiple_of(p * (ch // n_row), ch // n_row), ch // n_row)
            v = xu[:, lanes] * scale_c - xt[mid : mid + 1, lanes] * offset_c - xt[0:mid, lanes] * slope_c
            return jnp.transpose(v.astype(BF16)).astype(F32)

        reduce_red.begin(reduce_piece)
        split_red.fourth()

        def first_grad(i, c):
            m = wide(mk[i].reshape(cells, 128), mid // 128)
            v = mg[i].reshape(cells, mid) * v1[2:3] - m * (
                offset1 + slope1 * fp[i].reshape(cells, mid)
            )
            mx[i] = v.astype(BF16).reshape(slots, cols, mid)
            return c

        lax.fori_loop(0, images // 2, first_grad, 0)
        reduce_red.second(reduce_piece)
        lax.fori_loop(images // 2, images, first_grad, 0)
        out_fg = pltpu.make_async_copy(mx, fg_hbm, lsem.at[7])
        out_fg.start()
        reduce_red.third()
        split_out[...] = split_red.end()
        for copy in rows_copies:
            copy.wait()
        for p in range(n_row):
            up_out[p * up_rows : (p + 1) * up_rows] = rows_all[p, 0:up_rows]
            lines = rows_all[p, up_rows : up_rows + down_rows // 2]
            down_out[p * down_rows : (p + 1) * down_rows] = jnp.concatenate(
                [lines[:, 0:inter], lines[:, inter:]], axis=0
            )
        bias_out[...] = rows_all[0, up_rows + down_rows // 2 :]
        reduce_red.fourth()
        reduce_out[...] = reduce_red.end()
        out_fg.wait()

    pl.run_scoped(
        to_inputs,
        pltpu.VMEM((images, slots, cols, mid), F32),
        pltpu.VMEM((images, slots, cols, ch), BF16),
        pltpu.VMEM((mid + 128, ch), F32),
        pltpu.VMEM((mid, ch), F32),
        pltpu.VMEM((9 * half, 2 * mid), BF16),
    )


def reducer_sizes(n_row, ch, mid, inter):
    return [
        (mid // n_row, ch, BF16),
        (9 * (mid // 2) // n_row, 2 * mid, BF16),
        (ch // n_row, mid, BF16),
        (inter // n_row + mid // n_row // 2 + 8, mid, F32),
    ]


def call_backward(n_img, n_row, args, ch, inter):
    q = args[1]
    images, slots, cols, mid = q.shape
    half = mid // 2
    n = n_img * n_row
    cells = (images, slots, cols)
    sizes = reducer_sizes(n_row, ch, mid, inter)
    outs = [
        (sd(cells + (mid,), BF16), ANY),
        (sd((mid // n_row, ch)), VMEM),
        (sd((9 * half // n_row, 2 * mid)), VMEM),
        (sd((ch // n_row, mid)), VMEM),
        (sd((inter, mid)), VMEM),
        (sd((mid, inter)), VMEM),
        (sd((8, mid)), VMEM),
        (sd((2, mid)), VMEM),
        (sd((2, 2 * mid)), VMEM),
        (sd((2, ch)), VMEM),
        (sd((2, inter)), VMEM),
    ]
    dma = pltpu.SemaphoreType.DMA
    scratch = [
        pltpu.VMEM(cells + (mid,), F32),
        pltpu.VMEM(cells + (mid,), BF16),
        pltpu.VMEM(cells + (mid,), BF16),
        pltpu.VMEM(cells + (128,), F32),
        pltpu.VMEM((2, mid, 9 * half), F32),
        pltpu.VMEM((n_row, sizes[3][0], mid), F32),
        pltpu.VMEM((n_row, sizes[3][0], mid), F32),
        pltpu.VMEM((2, images, cols, mid), BF16),
        pltpu.VMEM((2, images, cols, mid), BF16),
        pltpu.VMEM((2, 8, mid), F32),
        pltpu.VMEM((2, 8, 2 * mid), F32),
        pltpu.VMEM((mid, mid), F32),
        pltpu.VMEM((images, mid), F32),
        pltpu.VMEM((images, mid), F32),
        pltpu.VMEM((n_img, 2, ch), F32),
        pltpu.VMEM((n_row, 2, ch), F32),
        pltpu.VMEM((n_row, images, inter), F32),
        pltpu.VMEM((n_img, 2, inter), F32),
        pltpu.VMEM((n, 2, 2 * mid), F32),
        pltpu.VMEM((n, 2, mid), F32),
        dma((8,)),
        dma((2,)),
        dma((4,)),
        dma((2, n_row)),
        dma((2, n_img)),
        dma((2, n_row)),
        dma((2, n_img)),
        dma((2, n)),
        dma((2, n)),
        dma((2, n_row)),
    ]
    for rows, width, dtype in sizes:
        scratch += Reducer.scratch(n_img, rows, width, dtype)
    in_specs = [SMEM] + [ANY] * 9 + [VMEM] * (len(args) - 10)
    return pl.pallas_call(
        functools.partial(backward_kernel, n_img, n_row),
        out_shape=[o for o, _ in outs],
        in_specs=in_specs,
        out_specs=[s for _, s in outs],
        scratch_shapes=scratch,
        name="backward",
        compiler_params=pltpu.CompilerParams(
            collective_id=1, has_side_effects=True, vmem_limit_bytes=62 * 1024 * 1024
        ),
    )(*args)


def input_kernel(
    fg, sg, wr, expand, split, reduce, up, down, bias, b1, b2, b3, b_at,
    gi, expand_out, split_out, reduce_out, up_out, down_out, bias_out, *lines,
):
    per, slots, cols, ch = sg.shape
    cells = per * slots * cols
    mid = fg.shape[-1]
    value = mm_nt(fg[...].reshape(cells, mid), wr[...])
    gi[...] = (value + sg[...].reshape(cells, ch).astype(F32)).astype(BF16).reshape(gi.shape)

    @pl.when(pl.program_id(0) == 0)
    def _():
        expand_out[...] = expand[...]
        split_out[...] = split[...]
        reduce_out[...] = reduce[...]
        down_out[...] = down[...]
        up_out[:, 0:mid] = up[...]
        up_out[:, mid:] = -up[...]
        bias_out[:, 0:mid] = bias[0:1]
        bias_out[:, mid:] = -bias[0:1]
        for k, v in enumerate((b1, b2, b_at, b3)):
            lines[2 * k][...] = v[1:2]
            lines[2 * k + 1][...] = v[0:1]


def call_input(fg, sg, wr, *small):
    images, slots, cols, ch = sg.shape
    mid = fg.shape[-1]
    expand, split, reduce, up, down, _, b1, b2, b3, b_at = small
    per = 14

    def cells(c):
        return pl.BlockSpec((per, slots, cols, c), lambda b: (b, 0, 0, 0))

    def whole(a):
        return pl.BlockSpec(a.shape, lambda b: (0,) * len(a.shape))

    outs = [sd(a.shape) for a in (expand, split, reduce)]
    outs += [sd((up.shape[0], 2 * mid)), sd(down.shape), sd((1, 2 * mid))]
    for v in (b1, b2, b_at, b3):
        outs += [sd((1, v.shape[1]))] * 2
    return pl.pallas_call(
        input_kernel,
        out_shape=[sd(sg.shape, BF16)] + outs,
        grid=(images // per,),
        in_specs=[cells(mid), cells(ch), whole(wr)] + [whole(a) for a in small],
        out_specs=[cells(ch)] + [whole(a) for a in outs],
        name="input_grad",
        compiler_params=pltpu.CompilerParams(vmem_limit_bytes=60 * 1024 * 1024),
    )(fg, sg, wr, *small)


def body(
    n_img,
    n_row,
    feature_map,
    image_group,
    row_counts,
    reduce_weight,
    gain_first,
    shift_first,
    split_weight,
    gain_second,
    shift_second,
    attn_down,
    gain_attend,
    shift_attend,
    attn_up,
    attn_bias,
    expand_weight,
    gain_third,
    shift_third,
    cotangent,
):
    images, slots, cols, ch = feature_map.shape
    mid = reduce_weight.shape[1]
    inter = attn_down.shape[1]
    half = mid // 2
    counts = row_counts[:, 0]
    ws = split_weight.reshape(3, 3 * half, 2 * mid)

    def line(v):
        return v[None, :]

    (
        fp, a3, sp, pd, mx, mk, xt, v1, v2, v3, v_at, at_norm, at_out, w0, w1, pooled, area,
        gw, awe, wt, mixed_sum,
    ) = call_forward(
        n_img,
        n_row,
        (
            counts,
            image_group,
            feature_map,
            reduce_weight,
            line(gain_first),
            line(shift_first),
            ws,
            line(gain_second),
            line(shift_second),
            attn_down,
            line(gain_attend),
            line(shift_attend),
            attn_up,
            line(attn_bias),
            expand_weight,
            line(gain_third),
            line(shift_third),
        ),
        images, slots, cols, ch, mid, inter,
    )
    block_out, sg, q, m_sum = call_third(
        feature_map, cotangent, mx, mk, expand_weight, awe, v3
    )
    (
        fg, grad_expand, grad_split, grad_reduce, grad_up, grad_down, bias, b1, b2, b3, b_at,
    ) = call_backward(
        n_img,
        n_row,
        (
            counts, q, fp, a3, sp, pd, mx, mk, xt, feature_map, v1, v2, v3, v_at, at_norm, at_out, w0, w1, pooled,
            gw, mixed_sum, m_sum, area, line(gain_attend), wt, attn_down, attn_up, expand_weight,
            awe,
        ),
        ch, inter,
    )
    small = call_input(
        fg, sg, reduce_weight, grad_expand, grad_split, grad_reduce, grad_up, grad_down, bias,
        b1, b2, b3, b_at,
    )
    grad_input, grad_expand, grad_split, grad_reduce, grad_up, grad_down = small[:6]
    return (
        block_out,
        grad_input,
        grad_reduce,
        grad_split.reshape(3, 3, half // n_row, 2 * mid),
        grad_expand,
        grad_down,
        grad_up,
    ) + tuple(v.reshape(-1) for v in small[6:])


def solution(mesh):
    cells = P("img", "row", None, None)
    in_specs = (cells, P("img"), P("img", "row")) + (P(),) * 14 + (cells,)
    out_specs = (cells, cells, P("row", None), P(None, None, "row", None), P("row", None)) + (P(),) * 11
    return jax.shard_map(
        functools.partial(body, mesh.shape["img"], mesh.shape["row"]),
        mesh=mesh,
        in_specs=in_specs,
        out_specs=out_specs,
        check_vma=False,
    )
```

```python
import functools

import jax
import jax.numpy as jnp
from jax import lax
from jax.experimental import pallas as pl
from jax.experimental.pallas import tpu as pltpu
from jax.sharding import PartitionSpec as P

MESH = pl.DeviceIdType.MESH
HIGH = lax.Precision.HIGHEST
F32 = jnp.float32
BF16 = jnp.bfloat16
EPS = 1e-05
GROUP = 8
ANY = pl.BlockSpec(memory_space=pl.ANY)
VMEM = pl.BlockSpec(memory_space=pltpu.VMEM)
SMEM = pl.BlockSpec(memory_space=pltpu.SMEM)


def dot(a, b, dims, precision=None):
    return lax.dot_general(
        a, b, (dims, ((), ())), preferred_element_type=F32, precision=precision
    )


def mm(a, b, precision=None):
    return dot(a, b, ((1,), (0,)), precision)


def mm_nt(a, b, precision=None):
    return dot(a, b, ((1,), (1,)), precision)


def mm_tn(a, b, precision=None):
    return dot(a, b, ((0,), (0,)), precision)


def mm_terms(product, a, b, terms):
    total = None
    for _ in range(terms):
        part = a.astype(BF16)
        a = a - part.astype(F32)
        value = product(part, b)
        total = value if total is None else total + value
    return total


def sigmoid(v):
    return 0.5 * jnp.tanh(0.5 * v) + 0.5


def swish_slope(v):
    s = sigmoid(v)
    return s * (1.0 + v * (1.0 - s))


def wide(mask, times):
    return jnp.concatenate([mask] * times, axis=1)


def fold(v):
    return jnp.sum(v.reshape(v.shape[0] // 8, 8, v.shape[1]), axis=0)


def row_sum(v):
    return jnp.sum(v, axis=0, keepdims=True)


class Links:
    def __init__(self, n_img, n_row):
        self.ni, self.nr = n_img, n_row
        self.i, self.r = lax.axis_index("img"), lax.axis_index("row")

    def greet(self):
        bar = pltpu.get_barrier_semaphore()

        def go(k, c):
            pl.semaphore_signal(
                bar, inc=1, device_id=self.peer(k), device_id_type=MESH
            )
            return c

        lax.fori_loop(1, self.ni * self.nr, go, 0)

    def met(self):
        pl.semaphore_wait(pltpu.get_barrier_semaphore(), self.ni * self.nr - 1)

    def peer(self, k):
        return (lax.rem(self.i + k // self.nr, self.ni), lax.rem(self.r + k % self.nr, self.nr))

    def copy(self, buf, send, recv, me, k, target):
        return pltpu.make_async_remote_copy(
            src_ref=buf.at[me],
            dst_ref=buf.at[me],
            send_sem=send.at[k],
            recv_sem=recv.at[k],
            device_id=target,
            device_id_type=MESH,
        )

    def all_me(self):
        return self.i * self.nr + self.r

    def all_start(self, buf, sems):
        def go(k, c):
            self.copy(buf, sems.at[0], sems.at[1], self.all_me(), k, self.peer(k)).start()
            return c

        lax.fori_loop(1, self.ni * self.nr, go, 0)

    def all_wait(self, buf, sems):
        def go(k, c):
            self.copy(buf, sems.at[0], sems.at[1], self.all_me(), k, self.peer(k)).wait()
            return c

        lax.fori_loop(1, self.ni * self.nr, go, 0)
        return jnp.sum(buf[...], axis=0)

    def row_copies(self, buf, sems):
        return [
            self.copy(buf, sems.at[0], sems.at[1], self.r, k, (self.i, lax.rem(self.r + k, self.nr)))
            for k in range(1, self.nr)
        ]

    def img_copy(self, buf, sems, k):
        return self.copy(
            buf, sems.at[0], sems.at[1], self.i, k, (lax.rem(self.i + k, self.ni), self.r)
        )

    def row_total(self, buf, sems):
        copies = self.row_copies(buf, sems)
        for c in copies:
            c.start()
        for c in copies:
            c.wait()
        return jnp.sum(buf[...], axis=0)

    def img_total(self, buf, sems):
        def go(k, c):
            self.img_copy(buf, sems, k).start()
            return c

        def end(k, c):
            self.img_copy(buf, sems, k).wait()
            return c

        lax.fori_loop(1, self.ni, go, 0)
        lax.fori_loop(1, self.ni, end, 0)
        return jnp.sum(buf[...], axis=0)


class Reducer:
    @staticmethod
    def layout(n_img, rows, width, dtype):
        lane_parts = min(width // 128, n_img)
        row_parts = n_img // lane_parts
        tile = 16 if dtype == BF16 else 8
        share = -(-rows // (row_parts * tile)) * tile
        return lane_parts, share, share * row_parts

    @staticmethod
    def scratch(n_img, rows, width, dtype):
        lane_parts, share, padded = Reducer.layout(n_img, rows, width, dtype)
        lanes = width // lane_parts
        return [
            pltpu.VMEM((2, padded, width), dtype),
            pltpu.VMEM((2, padded, width), dtype),
            pltpu.VMEM((padded, width), dtype),
            pltpu.VMEM((padded, width), dtype),
            pltpu.VMEM((padded, width), F32),
            pltpu.VMEM((n_img, share, lanes), dtype),
            pltpu.VMEM((padded, width), dtype),
            pltpu.SemaphoreType.DMA((2, 2 + 2 * n_img)),
        ]

    COUNT = 8

    def __init__(self, links, rows, width, refs):
        self.links, self.rows, self.width = links, rows, width
        (self.sb1, self.rb1, self.sb2, self.rb2, self.mine, self.rb3, self.ag, self.sems) = refs
        self.dtype = self.sb1.dtype
        self.lane_parts, self.share, self.padded = Reducer.layout(links.ni, rows, width, self.dtype)
        self.lanes = width // self.lane_parts
        r = links.r
        self.one = r + 1 - 2 * lax.rem(r, 2)
        self.two = lax.rem(r + 2, 4)

    def copy(self, src, dst, k, target):
        return pltpu.make_async_remote_copy(
            src_ref=src,
            dst_ref=dst,
            send_sem=self.sems.at[0, k],
            recv_sem=self.sems.at[1, k],
            device_id=target,
            device_id_type=MESH,
        )

    def copy1(self):
        return self.copy(self.sb1, self.rb1, 0, (self.links.i, self.one))

    def copy2(self):
        return self.copy(self.sb2, self.rb2, 1, (self.links.i, self.two))

    def part(self, ref, j):
        row = pl.multiple_of((j // self.lane_parts) * self.share, self.share)
        lane = pl.multiple_of(lax.rem(j, self.lane_parts) * self.lanes, self.lanes)
        return ref.at[pl.ds(row, self.share), pl.ds(lane, self.lanes)]

    def peer(self, k):
        return lax.rem(self.links.i + k, self.links.ni)

    def copy3(self, k):
        return self.copy(
            self.part(self.sb2, self.peer(k)), self.rb3.at[self.links.i], 2 + k, (self.peer(k), self.links.r)
        )

    def copy4(self, k):
        mine = self.part(self.ag, self.links.i)
        return self.copy(mine, mine, 2 + self.links.ni + k, (self.peer(k), self.links.r))

    def each(self, make, act):
        def go(k, c):
            act(make(k))
            return c

        lax.fori_loop(1, self.links.ni, go, 0)

    def begin(self, piece):
        odd = 1 - lax.rem(self.links.r, 2)
        for k in range(2):
            self.sb1[k, 0 : self.rows] = piece(odd + 2 * k).astype(self.dtype)
        self.copy1().start()

    def second(self, piece):
        self.copy1().wait()
        r = self.links.r
        kept = self.rb1[self.two // 2, 0 : self.rows].astype(F32)
        self.sb2[0 : self.rows] = (piece(self.two) + kept).astype(self.dtype)
        self.copy2().start()
        self.mine[0 : self.rows] = piece(r) + self.rb1[r // 2, 0 : self.rows].astype(F32)

    def third(self):
        self.copy2().wait()
        total = self.mine[0 : self.rows] + self.rb2[0 : self.rows].astype(F32)
        self.mine[0 : self.rows] = total
        self.sb2[0 : self.rows] = total.astype(self.dtype)
        self.each(self.copy3, lambda c: c.start())

    def fourth(self):
        self.each(self.copy3, lambda c: c.wait())
        total = self.part(self.mine, self.links.i)[...]
        for k in range(1, self.links.ni):
            total = total + self.rb3[self.peer(k)].astype(F32)
        self.part(self.ag, self.links.i)[...] = total.astype(self.dtype)
        self.each(self.copy4, lambda c: c.start())

    def end(self):
        self.each(self.copy4, lambda c: c.wait())
        return self.ag[0 : self.rows].astype(F32)


def norm_terms(total, square, count, gain, shift):
    mean = total / count
    factor = lax.rsqrt(square / count - mean * mean + EPS)
    scale = gain * factor
    return mean, factor, scale, shift - mean * scale


def norm_back_terms(mean, factor, scale, count, s0, s1):
    slope = scale * factor * (s1 / count)
    return slope, scale * (s0 / count) - slope * mean


def forward_kernel(
    n_img,
    n_row,
    counts,
    group,
    x_hbm,
    wr,
    g1,
    h1,
    ws_hbm,
    g2,
    h2,
    down,
    g_at,
    h_at,
    up,
    bias,
    we_hbm,
    g3,
    h3,
    fp_hbm,
    a3_hbm,
    sp_hbm,
    pd_hbm,
    mx_hbm,
    mk_hbm,
    xt_hbm,
    v1,
    v2,
    v3,
    v_at,
    at_norm,
    at_out,
    w0,
    w1,
    pooled,
    area,
    gw_hbm,
    awe_hbm,
    wt_hbm,
    mixed_sum,
    fp,
    sp,
    pp,
    pd,
    mx,
    mk,
    xt,
    xs,
    a3,
    a3b,
    ws,
    we,
    awe,
    wt,
    acc1,
    acc2,
    gram,
    bottom,
    above,
    below,
    buf1,
    buf2,
    rbuf3,
    ibuf3,
    rbuf4,
    ibuf4,
    xsem,
    osem,
    a3sem,
    hsem,
    sem1,
    sem2,
    rsem3,
    isem3,
    rsem4,
    isem4,
):
    images, slots, cols, ch = x_hbm.shape
    mid = wr.shape[1]
    half = mid // 2
    blocks = images // GROUP
    cells = slots * cols
    links = Links(n_img, n_row)
    r = links.r
    links.greet()

    def x_copy(b):
        at = pl.ds(b * GROUP, GROUP)
        return pltpu.make_async_copy(x_hbm.at[at], xs.at[at], xsem.at[b])

    def x_start(b, c):
        x_copy(b).start()
        return c

    lax.fori_loop(0, blocks, x_start, 0)
    pending = []
    in_ws = pltpu.make_async_copy(ws_hbm, ws, osem.at[6])
    in_we = pltpu.make_async_copy(we_hbm, we, osem.at[7])
    in_ws.start()
    in_we.start()
    pending += [in_ws, in_we]

    def masks(i, c):
        count, height = counts[i], 12 + 2 * group[i]
        area[pl.ds(i, 1)] = jnp.full((1, mid), 1, F32) * (height * height).astype(F32)
        rows = lax.broadcasted_iota(jnp.int32, (slots, cols, 128), 0)
        columns = lax.broadcasted_iota(jnp.int32, (slots, cols, 128), 1)
        mk[i] = jnp.where((rows < count) & (columns < height), 1.0, 0.0).astype(F32)
        return c

    lax.fori_loop(0, images, masks, 0)
    out_mk = pltpu.make_async_copy(mk, mk_hbm, osem.at[1])
    out_mk.start()
    pending.append(out_mk)
    acc1[...] = jnp.zeros_like(acc1)
    lines = GROUP * cells

    def first(b, c):
        x_copy(b).wait()
        at = pl.ds(b * GROUP, GROUP)
        v = mm(xs[at].reshape(lines, ch), wr[...])
        fp[at] = v.reshape(GROUP, slots, cols, mid)
        m = mk[at].reshape(lines, 128)
        w = v * wide(m, mid // 128)
        mx[at] = w.astype(BF16).reshape(GROUP, slots, cols, mid)
        pd[at, :, :, 0:128] = mk[at].astype(BF16)
        acc1[0] += fold(w)
        acc1[1] += fold(w * v)
        acc1[2, :, 0:128] += fold(m)
        for k in range(GROUP):
            i = b * GROUP + k
            bottom[i] = fp[i, jnp.maximum(counts[i] - 1, 0)]
        return c

    lax.fori_loop(0, blocks, first, 0)
    out_fp = pltpu.make_async_copy(fp, fp_hbm, osem.at[0])
    out_fp.start()
    pending.append(out_fp)

    me = links.all_me()
    buf1[me, 0:1] = row_sum(acc1[0])
    buf1[me, 1:2] = row_sum(acc1[1])
    n_here = row_sum(acc1[2, :, 0:128])
    buf1[me, 2:3] = wide(n_here, mid // 128)
    buf1[me, 3:4] = jnp.zeros((1, mid), F32)

    prev_dev = (links.i, lax.rem(r + n_row - 1, n_row))
    next_dev = (links.i, lax.rem(r + 1, n_row))
    to_prev = pltpu.make_async_remote_copy(
        src_ref=fp.at[:, 0],
        dst_ref=below,
        send_sem=hsem.at[0],
        recv_sem=hsem.at[1],
        device_id=prev_dev,
        device_id_type=MESH,
    )
    to_next = pltpu.make_async_remote_copy(
        src_ref=bottom,
        dst_ref=above,
        send_sem=hsem.at[2],
        recv_sem=hsem.at[3],
        device_id=next_dev,
        device_id_type=MESH,
    )
    has_prev = r > 0
    has_next = r < n_row - 1

    links.met()
    links.all_start(buf1, sem1)

    @pl.when(has_prev)
    def _():
        to_prev.start()

    @pl.when(has_next)
    def _():
        to_next.start()

    @pl.when(jnp.logical_not(has_prev))
    def _():
        above[...] = jnp.zeros_like(above)

    @pl.when(jnp.logical_not(has_next))
    def _():
        below[...] = jnp.zeros_like(below)

    v = jnp.concatenate(
        [mx[...].reshape(images * cells, mid), pd[:, :, :, 0:128].reshape(images * cells, 128)], axis=1
    )
    width = ch // 2
    for k in range(2):
        xt[:, k * width : (k + 1) * width] = mm_tn(
            v, xs[:, :, :, k * width : (k + 1) * width].reshape(images * cells, width)
        )[0 : mid + 8]
    out_xt = pltpu.make_async_copy(xt, xt_hbm, osem.at[5])
    out_xt.start()
    pending.append(out_xt)
    total = links.all_wait(buf1, sem1)
    n = total[2:3, 0:1]
    mean, factor, scale, offset = norm_terms(total[0:1], total[1:2], n, g1[...], h1[...])
    v1[0:1] = mean
    v1[1:2] = factor
    v1[2:3] = scale
    v1[3:4] = offset
    v1[4:5] = total[2:3]
    v1[5:8] = jnp.zeros((3, mid), F32)

    @pl.when(has_prev)
    def _():
        to_prev.wait_send()
        to_next.wait_recv()

    @pl.when(has_next)
    def _():
        to_next.wait_send()
        to_prev.wait_recv()

    prev_flag = has_prev.astype(F32)
    next_flag = has_next.astype(F32)
    ext = (slots + 2) * cols
    col_index = lax.rem(lax.broadcasted_iota(jnp.int32, (ext, mid), 0), cols)
    acc2[...] = jnp.zeros_like(acc2)

    in_ws.wait()
    in_we.wait()
    del pending[:2]
    buffers = (a3, a3b)

    def a3_copy(b, slot):
        return pltpu.make_async_copy(
            buffers[slot], a3_hbm.at[pl.ds(b * GROUP, GROUP)], a3sem.at[slot]
        )

    def spread(b, slot):
        for k in range(GROUP):
            i = b * GROUP + k
            m = mk[i].reshape(cells, 128)
            cm = wide(m[0:cols], mid // 128)
            z = fp[i].reshape(cells, mid) * v1[2:3] + v1[3:4]
            own = z * sigmoid(z) * wide(m, mid // 128)
            z = above[i] * v1[2:3] + v1[3:4]
            top = z * sigmoid(z) * (cm * prev_flag)
            z = below[i] * v1[2:3] + v1[3:4]
            low = z * sigmoid(z) * (cm * next_flag)
            count = counts[i]
            parts = [top]
            for s in range(slots + 1):
                here = low * jnp.where(count == s, 1.0, 0.0).astype(F32)
                if s < slots:
                    here = here + own[s * cols : (s + 1) * cols]
                parts.append(here)
            full = jnp.concatenate(parts, axis=0)
            left = jnp.where(col_index == 0, 0.0, pltpu.roll(full, 1, 0)).astype(BF16)
            right = jnp.where(col_index == cols - 1, 0.0, pltpu.roll(full, ext - 1, 0)).astype(BF16)
            full = full.astype(BF16)
            for g in range(2):
                for d, v in enumerate((left, full, right)):
                    lanes = slice((3 * g + d) * half, (3 * g + d + 1) * half)
                    buffers[slot][k, :, :, lanes] = v[:, g * half : (g + 1) * half].reshape(
                        slots + 2, cols, half
                    )

    def convolve(b, slot):
        m = wide(mk[pl.ds(b * GROUP, GROUP)].reshape(lines, 128), mid // 128)
        for g in range(2):
            lanes = slice(g * mid, (g + 1) * mid)
            taps = jnp.concatenate(
                [
                    buffers[slot][:, dy : dy + slots, :, g * 3 * half : (g + 1) * 3 * half].reshape(
                        lines, 3 * half
                    )
                    for dy in range(3)
                ],
                axis=1,
            )
            v = mm(taps, ws[:, :, lanes].reshape(9 * half, mid))
            sp[pl.ds(b * GROUP, GROUP), :, :, lanes] = v.reshape(GROUP, slots, cols, mid)
            w = v * m
            acc2[0, :, lanes] += fold(w)
            acc2[1, :, lanes] += fold(w * v)

    def second(b, slot, more):
        a3_copy(b, slot).start()
        convolve(b, slot)
        if more:

            @pl.when(b >= 1)
            def _():
                a3_copy(b - 1, 1 - slot).wait()

            spread(b + 1, 1 - slot)

    spread(0, 0)

    def pair(j, c):
        second(2 * j, 0, True)
        second(2 * j + 1, 1, True)
        return c

    pairs = (blocks - 1) // 2
    lax.fori_loop(0, pairs, pair, 0)
    rest = blocks - 2 * pairs
    second(2 * pairs, 0, rest == 2)
    if rest == 2:
        second(2 * pairs + 1, 1, False)
    pending += [a3_copy(0, 0), a3_copy(0, 1)]
    out_sp = pltpu.make_async_copy(sp, sp_hbm, osem.at[2])
    out_sp.start()
    pending.append(out_sp)

    buf2[me, 0:1] = row_sum(acc2[0])
    buf2[me, 1:2] = row_sum(acc2[1])
    links.all_start(buf2, sem2)
    for g in range(2):
        for dy in range(3):
            wt[g, dy * mid : (dy + 1) * mid] = jnp.transpose(ws[dy, :, g * mid : (g + 1) * mid])
    total = links.all_wait(buf2, sem2)
    mean, factor, scale, offset = norm_terms(total[0:1], total[1:2], n, g2[...], h2[...])
    v2[0:1] = mean
    v2[1:2] = factor
    v2[2:3] = scale
    v2[3:4] = offset
    v2[4:8] = jnp.zeros((4, 2 * mid), F32)

    def second_act(i, c):
        m = wide(mk[i].reshape(cells, 128), mid // 128)
        both = None
        for g in range(2):
            lanes = slice(g * mid, (g + 1) * mid)
            z = sp[i, :, :, lanes].reshape(cells, mid) * v2[2:3, lanes] + v2[3:4, lanes]
            p = z * sigmoid(z) * m
            pp[i, :, :, lanes] = p.reshape(slots, cols, mid)
            part = fold(p)
            both = part if both is None else both + part
        pooled[pl.ds(i, 1)] = row_sum(both)
        return c

    lax.fori_loop(0, images, second_act, 0, unroll=2)
    pooled[...] = pooled[...] / area[...]
    rbuf3[r] = mm(pooled[...], down[...].astype(F32), HIGH)
    squeeze = links.row_total(rbuf3, rsem3)
    ibuf3[links.i, 0:1] = row_sum(squeeze)
    ibuf3[links.i, 1:2] = row_sum(squeeze * squeeze)
    total = links.img_total(ibuf3, isem3)
    mean, factor, scale, offset = norm_terms(
        total[0:1], total[1:2], float(images * n_img), g_at[...], h_at[...]
    )
    v_at[0:1] = factor
    v_at[1:8] = jnp.zeros((7, v_at.shape[1]), F32)
    at_norm[...] = (squeeze - mean) * factor
    z = at_norm[...] * g_at[...] + h_at[...]
    at_out[...] = z
    attend = z * sigmoid(z)
    upf = up[...].astype(F32)
    lean = mm(attend, upf[:, :mid] - upf[:, mid:], HIGH) + (bias[:, :mid] - bias[:, mid:])
    w0[...] = sigmoid(lean)
    w1[...] = sigmoid(-lean)


    def mixing(i, c):
        p0 = pp[i, :, :, 0:mid].reshape(cells, mid)
        p1 = pp[i, :, :, mid:].reshape(cells, mid)
        v = w0[pl.ds(i, 1)] * p0 + w1[pl.ds(i, 1)] * p1
        mx[i] = v.astype(BF16).reshape(slots, cols, mid)
        pd[i] = (p0 - p1).astype(BF16).reshape(slots, cols, mid)
        return c

    lax.fori_loop(0, images, mixing, 0, unroll=2)
    v = mx[...].reshape(images * cells, mid)
    v = mm_tn(v, jnp.concatenate([v, jnp.ones((images * cells, 128), BF16)], axis=1))
    gram[...] = v[:, 0:mid]
    mixed_sum[...] = v[:, mid:]
    out_mx = pltpu.make_async_copy(mx, mx_hbm, osem.at[4])
    out_mx.start()
    pending.append(out_mx)
    out_pd = pltpu.make_async_copy(pd, pd_hbm, osem.at[3])
    out_pd.start()
    pending.append(out_pd)
    out_xt.wait()
    pending = [c for c in pending if c is not out_xt]
    gw = xt.at[0:mid]
    gw[...] = mm_terms(mm, gram[...], we[...], 3)
    wef = we[...].astype(F32)
    rbuf4[r, 0:1] = row_sum(wide(mixed_sum[...], ch // 128) * wef)
    rbuf4[r, 1:2] = row_sum(gw[...] * wef)
    ibuf4[links.i] = links.row_total(rbuf4, rsem4)
    total = links.img_total(ibuf4, isem4)
    mean, factor, scale, offset = norm_terms(total[0:1], total[1:2], n, g3[...], h3[...])
    v3[0:1] = mean
    v3[1:2] = factor
    v3[2:3] = scale
    v3[3:4] = offset
    v3[4:5] = 0.5 * scale
    v3[5:6] = 0.5 * offset
    v3[6:8] = jnp.zeros((2, ch), F32)
    awe[...] = (wef * scale).astype(BF16)
    for k, (src, dst) in enumerate([(gw, gw_hbm), (awe, awe_hbm), (wt, wt_hbm)]):
        copy = pltpu.make_async_copy(src, dst, osem.at[6 + k])
        copy.start()
        pending.append(copy)

    for copy in pending:
        copy.wait()


def sd(shape, dtype=F32):
    return jax.ShapeDtypeStruct(shape, dtype)


def call_forward(n_img, n_row, args, images, slots, cols, ch, mid, inter):
    n = n_img * n_row
    cells = (images, slots, cols)
    outs = [
        (sd(cells + (mid,)), ANY),
        (sd((images, slots + 2, cols, 3 * mid), BF16), ANY),
        (sd(cells + (2 * mid,)), ANY),
        (sd(cells + (mid,), BF16), ANY),
        (sd(cells + (mid,), BF16), ANY),
        (sd(cells + (128,)), ANY),
        (sd((mid + 8, ch)), ANY),
        (sd((8, mid)), VMEM),
        (sd((8, 2 * mid)), VMEM),
        (sd((8, ch)), VMEM),
        (sd((8, inter)), VMEM),
        (sd((images, inter)), VMEM),
        (sd((images, inter)), VMEM),
        (sd((images, mid)), VMEM),
        (sd((images, mid)), VMEM),
        (sd((images, mid)), VMEM),
        (sd((images, mid)), VMEM),
        (sd((mid, ch)), ANY),
        (sd((mid, ch), BF16), ANY),
        (sd((2, 3 * mid, 3 * mid // 2), BF16), ANY),
        (sd((mid, 128)), VMEM),
    ]
    dma = pltpu.SemaphoreType.DMA
    scratch = [
        pltpu.VMEM(cells + (mid,), F32),
        pltpu.VMEM(cells + (2 * mid,), F32),
        pltpu.VMEM(cells + (2 * mid,), F32),
        pltpu.VMEM(cells + (mid,), BF16),
        pltpu.VMEM(cells + (mid,), BF16),
        pltpu.VMEM(cells + (128,), F32),
        pltpu.VMEM((mid + 8, ch), F32),
        pltpu.VMEM((images, slots, cols, ch), BF16),
        pltpu.VMEM((GROUP, slots + 2, cols, 3 * mid), BF16),
        pltpu.VMEM((GROUP, slots + 2, cols, 3 * mid), BF16),
        pltpu.VMEM(args[6].shape, BF16),
        pltpu.VMEM((mid, ch), BF16),
        pltpu.VMEM((mid, ch), BF16),
        pltpu.VMEM((2, 3 * mid, 3 * mid // 2), BF16),
        pltpu.VMEM((3, 8, mid), F32),
        pltpu.VMEM((2, 8, 2 * mid), F32),
        pltpu.VMEM((mid, mid), F32),
        pltpu.VMEM((images, cols, mid), F32),
        pltpu.VMEM((images, cols, mid), F32),
        pltpu.VMEM((images, cols, mid), F32),
        pltpu.VMEM((n, 4, mid), F32),
        pltpu.VMEM((n, 2, 2 * mid), F32),
        pltpu.VMEM((n_row, images, inter), F32),
        pltpu.VMEM((n_img, 2, inter), F32),
        pltpu.VMEM((n_row, 2, ch), F32),
        pltpu.VMEM((n_img, 2, ch), F32),
        dma((images // GROUP,)),
        dma((9,)),
        dma((2,)),
        dma((4,)),
        dma((2, n)),
        dma((2, n)),
        dma((2, n_row)),
        dma((2, n_img)),
        dma((2, n_row)),
        dma((2, n_img)),
    ]
    in_specs = [SMEM, SMEM, ANY] + [VMEM] * (len(args) - 3)
    for k in (6, 14):
        in_specs[k] = ANY
    return pl.pallas_call(
        functools.partial(forward_kernel, n_img, n_row),
        out_shape=[o for o, _ in outs],
        in_specs=in_specs,
        out_specs=[s for _, s in outs],
        scratch_shapes=scratch,
        name="forward",
        compiler_params=pltpu.CompilerParams(
            collective_id=0, has_side_effects=True, vmem_limit_bytes=62 * 1024 * 1024
        ),
    )(*args)


PART = 2


def third_kernel(counts, group, x, cot, mx, we, awe, v3, bo, sg, q, m_out, *parts):
    per, slots, cols, ch = x.shape
    mid = mx.shape[-1]
    cells = PART * slots * cols
    columns = lax.broadcasted_iota(jnp.int32, (cols, 128), 0)

    @pl.when(pl.program_id(0) == 0)
    def _():
        m_out[...] = jnp.zeros_like(m_out)

    def product(p):
        v = mx[p * PART : (p + 1) * PART].reshape(cells, mid)
        parts[p][...] = mm(v, we[...])

    product(0)
    for p in range(per // PART):
        if p + 1 < per // PART:
            product(p + 1)
        for k in range(PART):
            i = p * PART + k
            image = pl.program_id(0) * per + i
            inside = jnp.where(columns < 12 + 2 * group[image], 1.0, 0.0).astype(F32)
            for s in range(slots):
                held = jnp.where(s < counts[image], 1.0, 0.0).astype(F32)
                m = wide(inside * held, ch // 128)
                at = (k * slots + s) * cols
                half = parts[p][at : at + cols] * v3[4:5] + v3[5:6] + 0.5 * x[i, s].astype(F32)
                th = jnp.tanh(half)
                up = 1.0 + th
                act = half * up
                bo[i, s] = (act * m).astype(BF16)
                slope = up + act * (1.0 - th)
                sg[i, s] = (cot[i, s].astype(F32) * (0.5 * m) * slope).astype(BF16)
        v = sg[p * PART : (p + 1) * PART].reshape(cells, ch)
        q[p * PART : (p + 1) * PART] = mm_nt(v, awe[...]).reshape(PART, slots, cols, mid)
    v = sg[...].reshape(per * slots * cols, ch)
    m_out[0:mid] += mm_tn(mx[...].reshape(per * slots * cols, mid), v)
    m_out[mid : mid + 16] += mm(jnp.ones((16, per * slots * cols), BF16), v)


def call_third(counts, group, x, cot, mx, we, awe, v3):
    images, slots, cols, ch = x.shape
    mid = mx.shape[-1]
    per = 8

    def cells(c):
        return pl.BlockSpec((per, slots, cols, c), lambda b: (b, 0, 0, 0))

    def whole(a):
        return pl.BlockSpec(a.shape, lambda b: (0,) * a.ndim)

    return pl.pallas_call(
        third_kernel,
        out_shape=[
            sd(x.shape, BF16),
            sd(x.shape, BF16),
            sd((images, slots, cols, mid)),
            sd((mid + 16, ch)),
        ],
        grid=(images // per,),
        in_specs=[SMEM, SMEM, cells(ch), cells(ch), cells(mid), whole(we), whole(awe), whole(v3)],
        out_specs=[
            cells(ch),
            cells(ch),
            cells(mid),
            pl.BlockSpec((mid + 16, ch), lambda b: (0, 0)),
        ],
        scratch_shapes=[pltpu.VMEM((PART * slots * cols, ch), F32)] * (per // PART),
        name="third",
        compiler_params=pltpu.CompilerParams(vmem_limit_bytes=60 * 1024 * 1024),
    )(counts, group, x, cot, mx, we, awe, v3)


def backward_kernel(
    n_img,
    n_row,
    counts,
    q_hbm,
    fp_hbm,
    a3_hbm,
    sp_hbm,
    pd_hbm,
    mx_hbm,
    mk_hbm,
    xt_hbm,
    x_hbm,
    v1,
    v2,
    v3,
    v_at,
    at_norm,
    at_out,
    w0,
    w1,
    pooled,
    gw_hbm,
    mixed_sum,
    m_in,
    area,
    g_at,
    wt_hbm,
    down,
    up,
    we,
    awe,
    fg_hbm,
    expand_out,
    split_out,
    reduce_out,
    up_out,
    down_out,
    bias_out,
    b1,
    b2,
    b3,
    b_at,
    mg,
    pd,
    mx,
    mk,
    gw,
    wt,
    split_part,
    small_part,
    rows_all,
    edge,
    ret,
    acc1,
    acc2,
    mb,
    dpart,
    pgrad,
    ibuf5,
    rbuf5,
    rbuf6,
    ibuf6,
    buf7,
    buf8,
    lsem,
    a3sem,
    hsem,
    rsem5,
    isem5,
    rsem6,
    isem6,
    sem7,
    sem8,
    rsem9,
    *reducers,
):
    images, slots, cols, mid = q_hbm.shape
    ch = we.shape[1]
    inter = down.shape[1]
    half = mid // 2
    blocks = images // GROUP
    cells = slots * cols
    links = Links(n_img, n_row)
    r, me = links.r, links.all_me()
    links.greet()
    sizes = reducer_sizes(n_row, ch, mid, inter)
    count = Reducer.COUNT
    expand_red, split_red, reduce_red, small_red = [
        Reducer(links, rows, width, reducers[k * count : (k + 1) * count])
        for k, (rows, width, _) in enumerate(sizes)
    ]
    n = v1[4:5, 0:1]
    up_rows, down_rows = inter // n_row, mid // n_row
    prev_dev = (links.i, lax.rem(r + n_row - 1, n_row))
    next_dev = (links.i, lax.rem(r + 1, n_row))
    has_prev = r > 0
    has_next = r < n_row - 1
    to_prev = pltpu.make_async_remote_copy(
        src_ref=edge.at[0],
        dst_ref=ret.at[1],
        send_sem=hsem.at[0],
        recv_sem=hsem.at[1],
        device_id=prev_dev,
        device_id_type=MESH,
    )
    to_next = pltpu.make_async_remote_copy(
        src_ref=edge.at[1],
        dst_ref=ret.at[0],
        send_sem=hsem.at[2],
        recv_sem=hsem.at[3],
        device_id=next_dev,
        device_id_type=MESH,
    )

    def columns_back(t, lines):
        col = lax.rem(lax.broadcasted_iota(jnp.int32, (lines, half), 0), cols)
        left = jnp.where(col == cols - 1, 0.0, pltpu.roll(t[:, 0:half], lines - 1, 0))
        right = jnp.where(col == 0, 0.0, pltpu.roll(t[:, 2 * half : 3 * half], 1, 0))
        return left + t[:, half : 2 * half] + right

    def small_piece(p):
        return small_part[p]

    def to_second_grads(sp):
        loads = [
            pltpu.make_async_copy(src, dst, lsem.at[k])
            for k, (src, dst) in enumerate(
                [(mx_hbm, mx), (q_hbm, mg), (pd_hbm, pd), (mk_hbm, mk), (sp_hbm, sp)]
            )
        ]
        load_gw = pltpu.make_async_copy(gw_hbm, gw, lsem.at[5])
        load_wt = pltpu.make_async_copy(wt_hbm, wt, lsem.at[6])
        load_gw.start()
        for load in loads:
            load.start()
        load_wt.start()
        pending = list(loads)

        mean3, factor3, scale3 = v3[0:1], v3[1:2], v3[2:3]
        wef = we[...].astype(F32)
        rbuf5[r, 0:1] = m_in[mid : mid + 1]
        rbuf5[r, 1:2] = factor3 * (row_sum(m_in[0:mid] * wef) - mean3 * m_in[mid : mid + 1])
        links.met()
        ibuf5[links.i] = links.row_total(rbuf5, rsem5)
        total = links.img_total(ibuf5, isem5)
        b3[...] = total
        slope3, offset3 = norm_back_terms(mean3, factor3, scale3, n, total[0:1], total[1:2])
        slope = factor3 * (total[1:2] / n)
        level = jnp.broadcast_to(total[0:1] / n - slope * mean3, (16, ch))
        lefts = []
        for v, terms in ((wef * slope, 2), (level, 3)):
            for _ in range(terms):
                lefts.append(v.astype(BF16))
                v = v - lefts[-1].astype(F32)
        v = mm_nt(jnp.concatenate(lefts, axis=0), awe[...])
        fix = v[0:mid] + v[mid : 2 * mid]
        ev = v[2 * mid : 2 * mid + 1] + v[2 * mid + 16 : 2 * mid + 17] + v[2 * mid + 32 : 2 * mid + 33]
        high = fix.astype(BF16)
        mb[0:mid] = high
        mb[mid:] = (fix - high.astype(F32)).astype(BF16)

        def expand_piece(p):
            rows = pl.ds(pl.multiple_of(p * (mid // n_row), mid // n_row), mid // n_row)
            return (
                m_in[rows] * scale3 - wide(mixed_sum[rows], ch // 128) * offset3 - gw[rows] * slope3
            )

        load_gw.wait()
        expand_red.begin(expand_piece)

        for load in loads[:4]:
            load.wait()
        del pending[:4]

        def mix_back(b, c):
            v = mx[pl.ds(b * GROUP, GROUP)].reshape(GROUP * cells, mid)
            v = mm(jnp.concatenate([v, v], axis=1), mb[...])
            for k in range(GROUP):
                i = b * GROUP + k
                m = wide(mk[i].reshape(cells, 128), mid // 128)
                w = mg[i].reshape(cells, mid) - v[k * cells : (k + 1) * cells] - m * ev
                mg[i] = w.reshape(slots, cols, mid)
                dpart[pl.ds(i, 1)] = row_sum(fold(w * pd[i].reshape(cells, mid).astype(F32)))
            return c

        lax.fori_loop(0, blocks, mix_back, 0)

        upf = up[...].astype(F32)
        lean = dpart[...] * w0[...] * w1[...]
        rbuf6[r] = mm_nt(lean, upf[:, :mid] - upf[:, mid:], HIGH)
        z = at_out[...]
        attend = z * sigmoid(z)
        up_part = mm_tn(attend, lean, HIGH)
        bias_part = row_sum(lean)
        attend_grad = links.row_total(rbuf6, rsem6) * swish_slope(z)
        ibuf6[links.i, 0:1] = row_sum(attend_grad)
        ibuf6[links.i, 1:2] = row_sum(attend_grad * at_norm[...])
        total = links.img_total(ibuf6, isem6)
        b_at[...] = total
        count = float(images * n_img)
        squeeze_grad = (
            g_at[...]
            * v_at[0:1]
            * (attend_grad - total[0:1] / count - at_norm[...] * (total[1:2] / count))
        )
        down_part = mm_tn(pooled[...], squeeze_grad, HIGH)
        for p in range(n_row):
            lines = down_part[p * down_rows : (p + 1) * down_rows]
            small_part[p, 0:up_rows] = up_part[p * up_rows : (p + 1) * up_rows]
            small_part[p, up_rows : up_rows + down_rows // 2] = jnp.concatenate(
                [lines[: down_rows // 2], lines[down_rows // 2 :]], axis=1
            )
            small_part[p, up_rows + down_rows // 2 :] = jnp.broadcast_to(bias_part, (8, mid))

        small_red.begin(small_piece)
        expand_red.second(expand_piece)
        pgrad[...] = mm_nt(squeeze_grad, down[...].astype(F32), HIGH) / area[...]

        def with_second_grads(ub, a3, geb):
            loads[4].wait()
            load_wt.wait()
            del pending[0]
            acc2[...] = jnp.zeros_like(acc2)

            def second_back(i, c):
                m = wide(mk[i].reshape(cells, 128), mid // 128)
                v = mg[i].reshape(cells, mid)
                for g, w in enumerate((w0, w1)):
                    lanes = slice(g * mid, (g + 1) * mid)
                    s = sp[i, :, :, lanes].reshape(cells, mid)
                    z = s * v2[2:3, lanes] + v2[3:4, lanes]
                    grad = (v * w[pl.ds(i, 1)] + pgrad[pl.ds(i, 1)]) * swish_slope(z) * m
                    ub[i, :, :, lanes] = grad.reshape(slots, cols, mid)
                    acc2[0, :, lanes] += fold(grad)
                    acc2[1, :, lanes] += fold(grad * s)
                return c

            lax.fori_loop(0, images, second_back, 0, unroll=2)
            mean2, factor2, scale2 = v2[0:1], v2[1:2], v2[2:3]
            s0 = row_sum(acc2[0])
            buf7[me, 0:1] = s0
            buf7[me, 1:2] = factor2 * (row_sum(acc2[1]) - mean2 * s0)
            links.all_start(buf7, sem7)
            total = links.all_wait(buf7, sem7)
            b2[...] = total
            slope2, offset2 = norm_back_terms(mean2, factor2, scale2, n, total[0:1], total[1:2])
            expand_red.third()

            def second_grad(grad, s, m):
                return (grad * scale2 - m * (offset2 + slope2 * s)).astype(BF16)

            for side, dy in ((0, 0), (1, 2)):

                def edge_rows(i, c):
                    at = 0 if side == 0 else jnp.maximum(counts[i] - 1, 0)
                    m = wide(mk[i, 0], 2 * mid // 128)
                    geb[i] = second_grad(ub[i, at], sp[i, at], m)
                    return c

                lax.fori_loop(0, images, edge_rows, 0, unroll=2)
                for g in range(2):
                    v = geb[:, :, g * mid : (g + 1) * mid].reshape(images * cols, mid)
                    t = mm(v, wt[g, dy * mid : (dy + 1) * mid])
                    edge[side, :, :, g * half : (g + 1) * half] = (
                        columns_back(t, images * cols).astype(BF16).reshape(images, cols, half)
                    )
                if side == 0:

                    @pl.when(has_prev)
                    def _():
                        to_prev.start()

                else:

                    @pl.when(has_next)
                    def _():
                        to_next.start()

            @pl.when(jnp.logical_not(has_prev))
            def _():
                ret[0] = jnp.zeros(ret.shape[1:], BF16)

            @pl.when(jnp.logical_not(has_next))
            def _():
                ret[1] = jnp.zeros(ret.shape[1:], BF16)

            def a3_copy(b, slot):
                return pltpu.make_async_copy(
                    a3_hbm.at[pl.ds(b * GROUP, GROUP)], a3.at[slot], a3sem.at[slot]
                )

            a3_copy(0, 0).start()
            split_part[...] = jnp.zeros_like(split_part)

            def split_grads(b, c):
                slot = lax.rem(b, 2)

                @pl.when(b + 1 < blocks)
                def _():
                    a3_copy(b + 1, 1 - slot).start()

                @pl.when(b == 2)
                def _():
                    small_red.second(small_piece)

                @pl.when(b == 4)
                def _():
                    expand_red.fourth()

                @pl.when(b == 6)
                def _():
                    small_red.third()

                def one(k, c):
                    i = b * GROUP + k
                    m = wide(mk[i].reshape(cells, 128), 2 * mid // 128)
                    v = second_grad(ub[i].reshape(cells, 2 * mid), sp[i].reshape(cells, 2 * mid), m)
                    mx[i] = v[:, 0:mid].reshape(slots, cols, mid)
                    pd[i] = v[:, mid:].reshape(slots, cols, mid)
                    return c

                lax.fori_loop(0, GROUP, one, 0)
                a3_copy(b, slot).wait()
                for g, grads in enumerate((mx, pd)):
                    v = grads[pl.ds(b * GROUP, GROUP)].reshape(GROUP * cells, mid)
                    taps = jnp.concatenate(
                        [
                            a3[slot, :, dy : dy + slots, :, g * 3 * half : (g + 1) * 3 * half].reshape(
                                GROUP * cells, 3 * half
                            )
                            for dy in range(3)
                        ],
                        axis=1,
                    )
                    split_part[g] += mm_tn(v, taps)
                return c

            lax.fori_loop(0, blocks, split_grads, 0)

        pl.run_scoped(
            with_second_grads,
            pltpu.VMEM((images, slots, cols, 2 * mid), F32),
            pltpu.VMEM((2, GROUP, slots + 2, cols, 3 * mid), BF16),
            pltpu.VMEM((images, cols, 2 * mid), BF16),
        )

    pl.run_scoped(to_second_grads, pltpu.VMEM((images, slots, cols, 2 * mid), F32))

    def to_inputs(fp, xs, xt, xu, split_rows):
        loads = [
            pltpu.make_async_copy(fp_hbm, fp, lsem.at[5]),
            pltpu.make_async_copy(xt_hbm, xt, lsem.at[6]),
            pltpu.make_async_copy(x_hbm, xs, lsem.at[4]),
        ]
        for load in loads:
            load.start()

        def split_piece(p):
            lines = []
            for tap in range(9):
                at = pl.multiple_of(tap * half + p * (half // n_row), half // n_row)
                lines.append(split_rows[pl.ds(at, half // n_row)])
            return jnp.concatenate(lines, axis=0).astype(F32)

        for g in range(2):
            for tap in range(9):
                split_rows[tap * half : (tap + 1) * half, g * mid : (g + 1) * mid] = jnp.transpose(
                    split_part[g, :, tap * half : (tap + 1) * half].astype(BF16)
                )
        split_red.begin(split_piece)
        @pl.when(has_prev)
        def _():
            to_prev.wait_send()
            to_next.wait_recv()

        @pl.when(has_next)
        def _():
            to_next.wait_send()
            to_prev.wait_recv()

        loads[0].wait()
        acc1[...] = jnp.zeros_like(acc1)

        def conv_back(b, c):
            @pl.when(b == 1)
            def _():
                split_red.second(split_piece)

            @pl.when(b == 3)
            def _():
                small_red.fourth()

            @pl.when(b == 5)
            def _():
                split_red.third()

            blank = jnp.zeros((GROUP, 1, cols, mid), BF16)
            for g, grads in enumerate((mx, pd)):
                v = grads[pl.ds(b * GROUP, GROUP)]
                moved = (
                    jnp.concatenate([v[:, 1:], blank], axis=1),
                    v,
                    jnp.concatenate([blank, v[:, : slots - 1]], axis=1),
                )
                v = jnp.concatenate(
                    [moved[dy].reshape(GROUP * cells, mid) for dy in range(3)], axis=1
                )
                value = mm(v, wt[g])
                back = columns_back(value, GROUP * cells)
                lanes = slice(g * half, (g + 1) * half)
                for k in range(GROUP):
                    i = b * GROUP + k
                    m = mk[i].reshape(cells, 128)
                    low = ret[1, i, :, lanes].astype(F32)
                    parts = []
                    for s in range(slots):
                        at = k * cells + s * cols
                        here = back[at : at + cols] + low * jnp.where(counts[i] - 1 == s, 1.0, 0.0).astype(F32)
                        if s == 0:
                            here = here + ret[0, i, :, lanes].astype(F32)
                        parts.append(here)
                    v = fp[i, :, :, lanes].reshape(cells, half)
                    z = v * v1[2:3, lanes] + v1[3:4, lanes]
                    grad = jnp.concatenate(parts, axis=0) * swish_slope(z) * wide(m, half // 128)
                    mg[i, :, :, lanes] = grad.reshape(slots, cols, half)
                    acc1[0, :, lanes] += fold(grad)
                    acc1[1, :, lanes] += fold(grad * v)
            return c

        lax.fori_loop(0, blocks, conv_back, 0)
        expand_out[...] = expand_red.end()
        rows_all[r] = small_red.end()
        rows_copies = links.row_copies(rows_all, rsem9)
        s0 = row_sum(acc1[0])
        buf8[me, 0:1] = s0
        buf8[me, 1:2] = v1[1:2] * (row_sum(acc1[1]) - v1[0:1] * s0)
        links.all_start(buf8, sem8)

        def narrow(i, c):
            pd[i] = mg[i].astype(BF16)
            return c

        lax.fori_loop(0, images, narrow, 0, unroll=4)
        loads[2].wait()
        lines = images * cells
        width = ch // 2
        for k in range(2):
            xu[:, k * width : (k + 1) * width] = mm_tn(
                pd[...].reshape(lines, mid), xs[:, :, :, k * width : (k + 1) * width].reshape(lines, width)
            )
        loads[1].wait()
        total = links.all_wait(buf8, sem8)
        b1[...] = total
        slope1, offset1 = norm_back_terms(v1[0:1], v1[1:2], v1[2:3], n, total[0:1], total[1:2])

        def column(v):
            return wide(jnp.transpose(jnp.broadcast_to(v, (128, mid))), ch // n_row // 128)

        scale_c, slope_c, offset_c = column(v1[2:3]), column(slope1), column(offset1)

        def reduce_piece(p):
            lanes = pl.ds(pl.multiple_of(p * (ch // n_row), ch // n_row), ch // n_row)
            v = xu[:, lanes] * scale_c - xt[mid : mid + 1, lanes] * offset_c - xt[0:mid, lanes] * slope_c
            return jnp.transpose(v.astype(BF16)).astype(F32)

        reduce_red.begin(reduce_piece)
        for copy in rows_copies:
            copy.start()
        split_red.fourth()

        def first_grad(i, c):
            m = wide(mk[i].reshape(cells, 128), mid // 128)
            v = mg[i].reshape(cells, mid) * v1[2:3] - m * (
                offset1 + slope1 * fp[i].reshape(cells, mid)
            )
            mx[i] = v.astype(BF16).reshape(slots, cols, mid)
            return c

        lax.fori_loop(0, images // 2, first_grad, 0)
        reduce_red.second(reduce_piece)
        lax.fori_loop(images // 2, images, first_grad, 0)
        out_fg = pltpu.make_async_copy(mx, fg_hbm, lsem.at[7])
        out_fg.start()
        reduce_red.third()
        split_out[...] = split_red.end()
        for copy in rows_copies:
            copy.wait()
        for p in range(n_row):
            up_out[p * up_rows : (p + 1) * up_rows] = rows_all[p, 0:up_rows]
            lines = rows_all[p, up_rows : up_rows + down_rows // 2]
            down_out[p * down_rows : (p + 1) * down_rows] = jnp.concatenate(
                [lines[:, 0:inter], lines[:, inter:]], axis=0
            )
        bias_out[...] = rows_all[0, up_rows + down_rows // 2 :]
        reduce_red.fourth()
        reduce_out[...] = reduce_red.end()
        out_fg.wait()

    pl.run_scoped(
        to_inputs,
        pltpu.VMEM((images, slots, cols, mid), F32),
        pltpu.VMEM((images, slots, cols, ch), BF16),
        pltpu.VMEM((mid + 8, ch), F32),
        pltpu.VMEM((mid, ch), F32),
        pltpu.VMEM((9 * half, 2 * mid), BF16),
    )


def reducer_sizes(n_row, ch, mid, inter):
    return [
        (mid // n_row, ch, BF16),
        (9 * (mid // 2) // n_row, 2 * mid, BF16),
        (ch // n_row, mid, BF16),
        (inter // n_row + mid // n_row // 2 + 8, mid, F32),
    ]


def call_backward(n_img, n_row, args, gw, wt, ch, inter):
    q = args[1]
    images, slots, cols, mid = q.shape
    half = mid // 2
    n = n_img * n_row
    cells = (images, slots, cols)
    sizes = reducer_sizes(n_row, ch, mid, inter)
    outs = [
        (sd(cells + (mid,), BF16), ANY),
        (sd((mid // n_row, ch)), VMEM),
        (sd((9 * half // n_row, 2 * mid)), VMEM),
        (sd((ch // n_row, mid)), VMEM),
        (sd((inter, mid)), VMEM),
        (sd((mid, inter)), VMEM),
        (sd((8, mid)), VMEM),
        (sd((2, mid)), VMEM),
        (sd((2, 2 * mid)), VMEM),
        (sd((2, ch)), VMEM),
        (sd((2, inter)), VMEM),
    ]
    dma = pltpu.SemaphoreType.DMA
    scratch = [
        pltpu.VMEM(cells + (mid,), F32),
        pltpu.VMEM(cells + (mid,), BF16),
        pltpu.VMEM(cells + (mid,), BF16),
        pltpu.VMEM(cells + (128,), F32),
        pltpu.VMEM((mid, ch), F32),
        pltpu.VMEM((2, 3 * mid, 3 * half), BF16),
        pltpu.VMEM((2, mid, 9 * half), F32),
        pltpu.VMEM((n_row, sizes[3][0], mid), F32),
        pltpu.VMEM((n_row, sizes[3][0], mid), F32),
        pltpu.VMEM((2, images, cols, mid), BF16),
        pltpu.VMEM((2, images, cols, mid), BF16),
        pltpu.VMEM((2, 8, mid), F32),
        pltpu.VMEM((2, 8, 2 * mid), F32),
        pltpu.VMEM((2 * mid, mid), BF16),
        pltpu.VMEM((images, mid), F32),
        pltpu.VMEM((images, mid), F32),
        pltpu.VMEM((n_img, 2, ch), F32),
        pltpu.VMEM((n_row, 2, ch), F32),
        pltpu.VMEM((n_row, images, inter), F32),
        pltpu.VMEM((n_img, 2, inter), F32),
        pltpu.VMEM((n, 2, 2 * mid), F32),
        pltpu.VMEM((n, 2, mid), F32),
        dma((8,)),
        dma((2,)),
        dma((4,)),
        dma((2, n_row)),
        dma((2, n_img)),
        dma((2, n_row)),
        dma((2, n_img)),
        dma((2, n)),
        dma((2, n)),
        dma((2, n_row)),
    ]
    for rows, width, dtype in sizes:
        scratch += Reducer.scratch(n_img, rows, width, dtype)
    in_specs = [SMEM] + [ANY] * 9 + [VMEM] * (len(args) - 10)
    for k, a in enumerate(args):
        if a is gw or a is wt:
            in_specs[k] = ANY
    return pl.pallas_call(
        functools.partial(backward_kernel, n_img, n_row),
        out_shape=[o for o, _ in outs],
        in_specs=in_specs,
        out_specs=[s for _, s in outs],
        scratch_shapes=scratch,
        name="backward",
        compiler_params=pltpu.CompilerParams(
            collective_id=1, has_side_effects=True, vmem_limit_bytes=62 * 1024 * 1024
        ),
    )(*args)


def input_kernel(
    fg, sg, wr, expand, split, reduce, up, down, bias, b1, b2, b3, b_at,
    gi, expand_out, split_out, reduce_out, up_out, down_out, bias_out, *lines,
):
    per, slots, cols, ch = sg.shape
    cells = per * slots * cols
    mid = fg.shape[-1]
    value = mm_nt(fg[...].reshape(cells, mid), wr[...])
    gi[...] = (value + sg[...].reshape(cells, ch).astype(F32)).astype(BF16).reshape(gi.shape)

    @pl.when(pl.program_id(0) == 0)
    def _():
        expand_out[...] = expand[...]
        split_out[...] = split[...]
        reduce_out[...] = reduce[...]
        down_out[...] = down[...]
        up_out[:, 0:mid] = up[...]
        up_out[:, mid:] = -up[...]
        bias_out[:, 0:mid] = bias[0:1]
        bias_out[:, mid:] = -bias[0:1]
        for k, v in enumerate((b1, b2, b_at, b3)):
            lines[2 * k][...] = v[1:2]
            lines[2 * k + 1][...] = v[0:1]


def call_input(fg, sg, wr, *small):
    images, slots, cols, ch = sg.shape
    mid = fg.shape[-1]
    expand, split, reduce, up, down, _, b1, b2, b3, b_at = small
    per = 14

    def cells(c):
        return pl.BlockSpec((per, slots, cols, c), lambda b: (b, 0, 0, 0))

    def whole(a):
        return pl.BlockSpec(a.shape, lambda b: (0,) * len(a.shape))

    outs = [sd(a.shape) for a in (expand, split, reduce)]
    outs += [sd((up.shape[0], 2 * mid)), sd(down.shape), sd((1, 2 * mid))]
    for v in (b1, b2, b_at, b3):
        outs += [sd((1, v.shape[1]))] * 2
    return pl.pallas_call(
        input_kernel,
        out_shape=[sd(sg.shape, BF16)] + outs,
        grid=(images // per,),
        in_specs=[cells(mid), cells(ch), whole(wr)] + [whole(a) for a in small],
        out_specs=[cells(ch)] + [whole(a) for a in outs],
        name="input_grad",
        compiler_params=pltpu.CompilerParams(vmem_limit_bytes=60 * 1024 * 1024),
    )(fg, sg, wr, *small)


def body(
    n_img,
    n_row,
    feature_map,
    image_group,
    row_counts,
    reduce_weight,
    gain_first,
    shift_first,
    split_weight,
    gain_second,
    shift_second,
    attn_down,
    gain_attend,
    shift_attend,
    attn_up,
    attn_bias,
    expand_weight,
    gain_third,
    shift_third,
    cotangent,
):
    images, slots, cols, ch = feature_map.shape
    mid = reduce_weight.shape[1]
    inter = attn_down.shape[1]
    half = mid // 2
    counts = row_counts[:, 0]
    ws = split_weight.reshape(3, 3 * half, 2 * mid)

    def line(v):
        return v[None, :]

    (
        fp, a3, sp, pd, mx, mk, xt, v1, v2, v3, v_at, at_norm, at_out, w0, w1, pooled, area,
        gw, awe, wt, mixed_sum,
    ) = call_forward(
        n_img,
        n_row,
        (
            counts,
            image_group,
            feature_map,
            reduce_weight,
            line(gain_first),
            line(shift_first),
            ws,
            line(gain_second),
            line(shift_second),
            attn_down,
            line(gain_attend),
            line(shift_attend),
            attn_up,
            line(attn_bias),
            expand_weight,
            line(gain_third),
            line(shift_third),
        ),
        images, slots, cols, ch, mid, inter,
    )
    block_out, sg, q, m_sum = call_third(
        counts, image_group, feature_map, cotangent, mx, expand_weight, awe, v3
    )
    (
        fg, grad_expand, grad_split, grad_reduce, grad_up, grad_down, bias, b1, b2, b3, b_at,
    ) = call_backward(
        n_img,
        n_row,
        (
            counts, q, fp, a3, sp, pd, mx, mk, xt, feature_map, v1, v2, v3, v_at, at_norm, at_out, w0, w1, pooled,
            gw, mixed_sum, m_sum, area, line(gain_attend), wt, attn_down, attn_up, expand_weight,
            awe,
        ),
        gw, wt, ch, inter,
    )
    small = call_input(
        fg, sg, reduce_weight, grad_expand, grad_split, grad_reduce, grad_up, grad_down, bias,
        b1, b2, b3, b_at,
    )
    grad_input, grad_expand, grad_split, grad_reduce, grad_up, grad_down = small[:6]
    return (
        block_out,
        grad_input,
        grad_reduce,
        grad_split.reshape(3, 3, half // n_row, 2 * mid),
        grad_expand,
        grad_down,
        grad_up,
    ) + tuple(v.reshape(-1) for v in small[6:])


def solution(mesh):
    cells = P("img", "row", None, None)
    in_specs = (cells, P("img"), P("img", "row")) + (P(),) * 14 + (cells,)
    out_specs = (cells, cells, P("row", None), P(None, None, "row", None), P("row", None)) + (P(),) * 11
    return jax.shard_map(
        functools.partial(body, mesh.shape["img"], mesh.shape["row"]),
        mesh=mesh,
        in_specs=in_specs,
        out_specs=out_specs,
        check_vma=False,
    )
```

```python
import functools

import jax
import jax.numpy as jnp
from jax import lax
from jax.experimental import pallas as pl
from jax.experimental.pallas import tpu as pltpu
from jax.sharding import PartitionSpec as P

MESH = pl.DeviceIdType.MESH
HIGH = lax.Precision.HIGHEST
F32 = jnp.float32
BF16 = jnp.bfloat16
EPS = 1e-05
GROUP = 8
ANY = pl.BlockSpec(memory_space=pl.ANY)
VMEM = pl.BlockSpec(memory_space=pltpu.VMEM)
SMEM = pl.BlockSpec(memory_space=pltpu.SMEM)


def dot(a, b, dims, precision=None):
    return lax.dot_general(
        a, b, (dims, ((), ())), preferred_element_type=F32, precision=precision
    )


def mm(a, b, precision=None):
    return dot(a, b, ((1,), (0,)), precision)


def mm_nt(a, b, precision=None):
    return dot(a, b, ((1,), (1,)), precision)


def mm_tn(a, b, precision=None):
    return dot(a, b, ((0,), (0,)), precision)


def mm_terms(product, a, b, terms):
    total = None
    for _ in range(terms):
        part = a.astype(BF16)
        a = a - part.astype(F32)
        value = product(part, b)
        total = value if total is None else total + value
    return total


def sigmoid(v):
    return 0.5 * jnp.tanh(0.5 * v) + 0.5


def swish_slope(v):
    s = sigmoid(v)
    return s * (1.0 + v * (1.0 - s))


def wide(mask, times):
    return jnp.concatenate([mask] * times, axis=1)


def fold(v):
    return jnp.sum(v.reshape(v.shape[0] // 8, 8, v.shape[1]), axis=0)


def row_sum(v):
    return jnp.sum(v, axis=0, keepdims=True)


class Links:
    def __init__(self, n_img, n_row):
        self.ni, self.nr = n_img, n_row
        self.i, self.r = lax.axis_index("img"), lax.axis_index("row")

    def greet(self):
        bar = pltpu.get_barrier_semaphore()

        def go(k, c):
            pl.semaphore_signal(
                bar, inc=1, device_id=self.peer(k), device_id_type=MESH
            )
            return c

        lax.fori_loop(1, self.ni * self.nr, go, 0)

    def met(self):
        pl.semaphore_wait(pltpu.get_barrier_semaphore(), self.ni * self.nr - 1)

    def peer(self, k):
        return (lax.rem(self.i + k // self.nr, self.ni), lax.rem(self.r + k % self.nr, self.nr))

    def copy(self, buf, send, recv, me, k, target):
        return pltpu.make_async_remote_copy(
            src_ref=buf.at[me],
            dst_ref=buf.at[me],
            send_sem=send.at[k],
            recv_sem=recv.at[k],
            device_id=target,
            device_id_type=MESH,
        )

    def all_me(self):
        return self.i * self.nr + self.r

    def all_start(self, buf, sems):
        def go(k, c):
            self.copy(buf, sems.at[0], sems.at[1], self.all_me(), k, self.peer(k)).start()
            return c

        lax.fori_loop(1, self.ni * self.nr, go, 0)

    def all_wait(self, buf, sems):
        def go(k, c):
            self.copy(buf, sems.at[0], sems.at[1], self.all_me(), k, self.peer(k)).wait()
            return c

        lax.fori_loop(1, self.ni * self.nr, go, 0)
        return jnp.sum(buf[...], axis=0)

    def row_copies(self, buf, sems):
        return [
            self.copy(buf, sems.at[0], sems.at[1], self.r, k, (self.i, lax.rem(self.r + k, self.nr)))
            for k in range(1, self.nr)
        ]

    def img_copy(self, buf, sems, k):
        return self.copy(
            buf, sems.at[0], sems.at[1], self.i, k, (lax.rem(self.i + k, self.ni), self.r)
        )

    def row_start(self, buf, sems):
        copies = self.row_copies(buf, sems)
        for c in copies:
            c.start()
        return copies

    def row_end(self, buf, copies):
        for c in copies:
            c.wait()
        return jnp.sum(buf[...], axis=0)

    def row_total(self, buf, sems):
        return self.row_end(buf, self.row_start(buf, sems))

    def img_start(self, buf, sems):
        def go(k, c):
            self.img_copy(buf, sems, k).start()
            return c

        lax.fori_loop(1, self.ni, go, 0)

    def img_end(self, buf, sems):
        def end(k, c):
            self.img_copy(buf, sems, k).wait()
            return c

        lax.fori_loop(1, self.ni, end, 0)
        return jnp.sum(buf[...], axis=0)

    def img_total(self, buf, sems):
        self.img_start(buf, sems)
        return self.img_end(buf, sems)


class Reducer:
    @staticmethod
    def layout(n_img, rows, width, dtype):
        lane_parts = min(width // 128, n_img)
        row_parts = n_img // lane_parts
        tile = 16 if dtype == BF16 else 8
        share = -(-rows // (row_parts * tile)) * tile
        return lane_parts, share, share * row_parts

    @staticmethod
    def scratch(n_img, rows, width, dtype):
        lane_parts, share, padded = Reducer.layout(n_img, rows, width, dtype)
        lanes = width // lane_parts
        return [
            pltpu.VMEM((2, padded, width), dtype),
            pltpu.VMEM((2, padded, width), dtype),
            pltpu.VMEM((padded, width), dtype),
            pltpu.VMEM((padded, width), dtype),
            pltpu.VMEM((padded, width), F32),
            pltpu.VMEM((n_img, share, lanes), dtype),
            pltpu.VMEM((padded, width), dtype),
            pltpu.SemaphoreType.DMA((2, 2 + 2 * n_img)),
        ]

    COUNT = 8

    def __init__(self, links, rows, width, refs):
        self.links, self.rows, self.width = links, rows, width
        (self.sb1, self.rb1, self.sb2, self.rb2, self.mine, self.rb3, self.ag, self.sems) = refs
        self.dtype = self.sb1.dtype
        self.lane_parts, self.share, self.padded = Reducer.layout(links.ni, rows, width, self.dtype)
        self.lanes = width // self.lane_parts
        r = links.r
        self.one = r + 1 - 2 * lax.rem(r, 2)
        self.two = lax.rem(r + 2, 4)

    def copy(self, src, dst, k, target):
        return pltpu.make_async_remote_copy(
            src_ref=src,
            dst_ref=dst,
            send_sem=self.sems.at[0, k],
            recv_sem=self.sems.at[1, k],
            device_id=target,
            device_id_type=MESH,
        )

    def copy1(self):
        return self.copy(self.sb1, self.rb1, 0, (self.links.i, self.one))

    def copy2(self):
        return self.copy(self.sb2, self.rb2, 1, (self.links.i, self.two))

    def part(self, ref, j):
        row = pl.multiple_of((j // self.lane_parts) * self.share, self.share)
        lane = pl.multiple_of(lax.rem(j, self.lane_parts) * self.lanes, self.lanes)
        return ref.at[pl.ds(row, self.share), pl.ds(lane, self.lanes)]

    def peer(self, k):
        return lax.rem(self.links.i + k, self.links.ni)

    def copy3(self, k):
        return self.copy(
            self.part(self.sb2, self.peer(k)), self.rb3.at[self.links.i], 2 + k, (self.peer(k), self.links.r)
        )

    def copy4(self, k):
        mine = self.part(self.ag, self.links.i)
        return self.copy(mine, mine, 2 + self.links.ni + k, (self.peer(k), self.links.r))

    def each(self, make, act):
        def go(k, c):
            act(make(k))
            return c

        lax.fori_loop(1, self.links.ni, go, 0)

    def begin(self, piece):
        odd = 1 - lax.rem(self.links.r, 2)
        for k in range(2):
            self.sb1[k, 0 : self.rows] = piece(odd + 2 * k).astype(self.dtype)
        self.copy1().start()

    def second(self, piece):
        self.copy1().wait()
        r = self.links.r
        kept = self.rb1[self.two // 2, 0 : self.rows].astype(F32)
        self.sb2[0 : self.rows] = (piece(self.two) + kept).astype(self.dtype)
        self.copy2().start()
        self.mine[0 : self.rows] = piece(r) + self.rb1[r // 2, 0 : self.rows].astype(F32)

    def third(self):
        self.copy2().wait()
        total = self.mine[0 : self.rows] + self.rb2[0 : self.rows].astype(F32)
        self.mine[0 : self.rows] = total
        self.sb2[0 : self.rows] = total.astype(self.dtype)
        self.each(self.copy3, lambda c: c.start())

    def fourth(self):
        self.each(self.copy3, lambda c: c.wait())
        total = self.part(self.mine, self.links.i)[...]
        for k in range(1, self.links.ni):
            total = total + self.rb3[self.peer(k)].astype(F32)
        self.part(self.ag, self.links.i)[...] = total.astype(self.dtype)
        self.each(self.copy4, lambda c: c.start())

    def end(self):
        self.each(self.copy4, lambda c: c.wait())
        return self.ag[0 : self.rows].astype(F32)


def norm_terms(total, square, count, gain, shift):
    mean = total / count
    factor = lax.rsqrt(square / count - mean * mean + EPS)
    scale = gain * factor
    return mean, factor, scale, shift - mean * scale


def norm_back_terms(mean, factor, scale, count, s0, s1):
    slope = scale * factor * (s1 / count)
    return slope, scale * (s0 / count) - slope * mean


def forward_kernel(
    n_img,
    n_row,
    counts,
    group,
    x_hbm,
    wr,
    g1,
    h1,
    ws_hbm,
    g2,
    h2,
    down,
    g_at,
    h_at,
    up,
    bias,
    we_hbm,
    g3,
    h3,
    fp_hbm,
    a3_hbm,
    sp_hbm,
    pd_hbm,
    mx_hbm,
    mk_hbm,
    xt_hbm,
    v1,
    v2,
    v3,
    v_at,
    at_norm,
    at_out,
    w0,
    w1,
    pooled,
    area,
    gw_hbm,
    awe_hbm,
    wt_hbm,
    mixed_sum,
    fp,
    sp,
    pp,
    pd,
    mx,
    mk,
    xt,
    xs,
    a3,
    a3b,
    ws,
    we,
    awe,
    wt,
    acc1,
    acc2,
    gram,
    bottom,
    above,
    below,
    buf1,
    buf2,
    rbuf3,
    ibuf3,
    rbuf4,
    ibuf4,
    xsem,
    osem,
    a3sem,
    hsem,
    sem1,
    sem2,
    rsem3,
    isem3,
    rsem4,
    isem4,
):
    images, slots, cols, ch = x_hbm.shape
    mid = wr.shape[1]
    half = mid // 2
    blocks = images // GROUP
    cells = slots * cols
    links = Links(n_img, n_row)
    r = links.r
    links.greet()

    def x_copy(b):
        at = pl.ds(b * GROUP, GROUP)
        return pltpu.make_async_copy(x_hbm.at[at], xs.at[at], xsem.at[b])

    def x_start(b, c):
        x_copy(b).start()
        return c

    lax.fori_loop(0, blocks, x_start, 0)
    pending = []
    in_ws = pltpu.make_async_copy(ws_hbm, ws, osem.at[6])
    in_we = pltpu.make_async_copy(we_hbm, we, osem.at[7])

    def masks(i, c):
        count, height = counts[i], 12 + 2 * group[i]
        area[pl.ds(i, 1)] = jnp.full((1, mid), 1, F32) * (height * height).astype(F32)
        rows = lax.broadcasted_iota(jnp.int32, (slots, cols, 128), 0)
        columns = lax.broadcasted_iota(jnp.int32, (slots, cols, 128), 1)
        mk[i] = jnp.where((rows < count) & (columns < height), 1.0, 0.0).astype(F32)
        return c

    lax.fori_loop(0, images, masks, 0)
    acc1[...] = jnp.zeros_like(acc1)
    lines = GROUP * cells

    def first(b, c):
        x_copy(b).wait()
        at = pl.ds(b * GROUP, GROUP)
        v = mm(xs[at].reshape(lines, ch), wr[...])
        fp[at] = v.reshape(GROUP, slots, cols, mid)
        m = mk[at].reshape(lines, 128)
        w = v * wide(m, mid // 128)
        mx[at] = w.astype(BF16).reshape(GROUP, slots, cols, mid)
        pd[at, :, :, 0:128] = mk[at].astype(BF16)
        acc1[0] += fold(w)
        acc1[1] += fold(w * v)
        acc1[2, :, 0:128] += fold(m)
        for k in range(GROUP):
            i = b * GROUP + k
            bottom[i] = fp[i, jnp.maximum(counts[i] - 1, 0)]
        return c

    lax.fori_loop(0, blocks, first, 0)
    in_ws.start()
    in_we.start()
    pending += [in_ws, in_we]
    out_mk = pltpu.make_async_copy(mk, mk_hbm, osem.at[1])
    out_mk.start()
    pending.append(out_mk)
    out_fp = pltpu.make_async_copy(fp, fp_hbm, osem.at[0])
    out_fp.start()
    pending.append(out_fp)

    me = links.all_me()
    buf1[me, 0:1] = row_sum(acc1[0])
    buf1[me, 1:2] = row_sum(acc1[1])
    n_here = row_sum(acc1[2, :, 0:128])
    buf1[me, 2:3] = wide(n_here, mid // 128)
    buf1[me, 3:4] = jnp.zeros((1, mid), F32)

    prev_dev = (links.i, lax.rem(r + n_row - 1, n_row))
    next_dev = (links.i, lax.rem(r + 1, n_row))
    to_prev = pltpu.make_async_remote_copy(
        src_ref=fp.at[:, 0],
        dst_ref=below,
        send_sem=hsem.at[0],
        recv_sem=hsem.at[1],
        device_id=prev_dev,
        device_id_type=MESH,
    )
    to_next = pltpu.make_async_remote_copy(
        src_ref=bottom,
        dst_ref=above,
        send_sem=hsem.at[2],
        recv_sem=hsem.at[3],
        device_id=next_dev,
        device_id_type=MESH,
    )
    has_prev = r > 0
    has_next = r < n_row - 1

    links.met()
    links.all_start(buf1, sem1)

    @pl.when(has_prev)
    def _():
        to_prev.start()

    @pl.when(has_next)
    def _():
        to_next.start()

    @pl.when(jnp.logical_not(has_prev))
    def _():
        above[...] = jnp.zeros_like(above)

    @pl.when(jnp.logical_not(has_next))
    def _():
        below[...] = jnp.zeros_like(below)

    v = jnp.concatenate(
        [mx[...].reshape(images * cells, mid), pd[:, :, :, 0:128].reshape(images * cells, 128)], axis=1
    )
    width = ch // 2
    for k in range(2):
        xt[:, k * width : (k + 1) * width] = mm_tn(
            v, xs[:, :, :, k * width : (k + 1) * width].reshape(images * cells, width)
        )[0 : mid + 8]
    out_xt = pltpu.make_async_copy(xt, xt_hbm, osem.at[5])
    out_xt.start()
    pending.append(out_xt)
    total = links.all_wait(buf1, sem1)
    n = total[2:3, 0:1]
    mean, factor, scale, offset = norm_terms(total[0:1], total[1:2], n, g1[...], h1[...])
    v1[0:1] = mean
    v1[1:2] = factor
    v1[2:3] = scale
    v1[3:4] = offset
    v1[4:5] = total[2:3]
    v1[5:8] = jnp.zeros((3, mid), F32)

    @pl.when(has_prev)
    def _():
        to_prev.wait_send()
        to_next.wait_recv()

    @pl.when(has_next)
    def _():
        to_next.wait_send()
        to_prev.wait_recv()

    prev_flag = has_prev.astype(F32)
    next_flag = has_next.astype(F32)
    ext = (slots + 2) * cols
    col_index = lax.rem(lax.broadcasted_iota(jnp.int32, (ext, mid), 0), cols)
    acc2[...] = jnp.zeros_like(acc2)

    in_ws.wait()
    in_we.wait()
    del pending[:2]
    buffers = (a3, a3b)

    def a3_copy(b, slot):
        return pltpu.make_async_copy(
            buffers[slot], a3_hbm.at[pl.ds(b * GROUP, GROUP)], a3sem.at[slot]
        )

    def spread(b, slot):
        for k in range(GROUP):
            i = b * GROUP + k
            m = mk[i].reshape(cells, 128)
            cm = wide(m[0:cols], mid // 128)
            z = fp[i].reshape(cells, mid) * v1[2:3] + v1[3:4]
            own = z * sigmoid(z) * wide(m, mid // 128)
            z = above[i] * v1[2:3] + v1[3:4]
            top = z * sigmoid(z) * (cm * prev_flag)
            z = below[i] * v1[2:3] + v1[3:4]
            low = z * sigmoid(z) * (cm * next_flag)
            count = counts[i]
            parts = [top]
            for s in range(slots + 1):
                here = low * jnp.where(count == s, 1.0, 0.0).astype(F32)
                if s < slots:
                    here = here + own[s * cols : (s + 1) * cols]
                parts.append(here)
            full = jnp.concatenate(parts, axis=0)
            left = jnp.where(col_index == 0, 0.0, pltpu.roll(full, 1, 0)).astype(BF16)
            right = jnp.where(col_index == cols - 1, 0.0, pltpu.roll(full, ext - 1, 0)).astype(BF16)
            full = full.astype(BF16)
            for g in range(2):
                for d, v in enumerate((left, full, right)):
                    lanes = slice((3 * g + d) * half, (3 * g + d + 1) * half)
                    buffers[slot][k, :, :, lanes] = v[:, g * half : (g + 1) * half].reshape(
                        slots + 2, cols, half
                    )

    def convolve(b, slot):
        m = wide(mk[pl.ds(b * GROUP, GROUP)].reshape(lines, 128), mid // 128)
        for g in range(2):
            lanes = slice(g * mid, (g + 1) * mid)
            taps = jnp.concatenate(
                [
                    buffers[slot][:, dy : dy + slots, :, g * 3 * half : (g + 1) * 3 * half].reshape(
                        lines, 3 * half
                    )
                    for dy in range(3)
                ],
                axis=1,
            )
            v = mm(taps, ws[:, :, lanes].reshape(9 * half, mid))
            sp[pl.ds(b * GROUP, GROUP), :, :, lanes] = v.reshape(GROUP, slots, cols, mid)
            w = v * m
            acc2[0, :, lanes] += fold(w)
            acc2[1, :, lanes] += fold(w * v)

    def second(b, slot, more):
        a3_copy(b, slot).start()
        convolve(b, slot)
        if more:

            @pl.when(b >= 1)
            def _():
                a3_copy(b - 1, 1 - slot).wait()

            spread(b + 1, 1 - slot)

    spread(0, 0)

    def pair(j, c):
        second(2 * j, 0, True)
        second(2 * j + 1, 1, True)
        return c

    pairs = (blocks - 1) // 2
    lax.fori_loop(0, pairs, pair, 0)
    rest = blocks - 2 * pairs
    second(2 * pairs, 0, rest == 2)
    if rest == 2:
        second(2 * pairs + 1, 1, False)
    pending += [a3_copy(0, 0), a3_copy(0, 1)]
    out_sp = pltpu.make_async_copy(sp, sp_hbm, osem.at[2])
    out_sp.start()
    pending.append(out_sp)

    buf2[me, 0:1] = row_sum(acc2[0])
    buf2[me, 1:2] = row_sum(acc2[1])
    links.all_start(buf2, sem2)
    for g in range(2):
        for dy in range(3):
            wt[g, dy * mid : (dy + 1) * mid] = jnp.transpose(ws[dy, :, g * mid : (g + 1) * mid])
    total = links.all_wait(buf2, sem2)
    mean, factor, scale, offset = norm_terms(total[0:1], total[1:2], n, g2[...], h2[...])
    v2[0:1] = mean
    v2[1:2] = factor
    v2[2:3] = scale
    v2[3:4] = offset
    v2[4:8] = jnp.zeros((4, 2 * mid), F32)

    def second_act(i, c):
        m = wide(mk[i].reshape(cells, 128), mid // 128)
        acts = []
        for g in range(2):
            lanes = slice(g * mid, (g + 1) * mid)
            z = sp[i, :, :, lanes].reshape(cells, mid) * v2[2:3, lanes] + v2[3:4, lanes]
            acts.append(z * sigmoid(z) * m)
        pp[i, :, :, 0:mid] = (acts[0] - acts[1]).reshape(slots, cols, mid)
        pp[i, :, :, mid:] = acts[1].reshape(slots, cols, mid)
        pooled[pl.ds(i, 1)] = row_sum(fold(acts[0] + acts[1]))
        return c

    lax.fori_loop(0, images, second_act, 0, unroll=2)
    pooled[...] = pooled[...] / area[...]
    rbuf3[r] = mm(pooled[...], down[...].astype(F32), HIGH)
    copies = links.row_start(rbuf3, rsem3)

    def difference(i, c):
        pd[i] = pp[i, :, :, 0:mid].astype(BF16)
        return c

    lax.fori_loop(0, images, difference, 0, unroll=4)
    out_pd = pltpu.make_async_copy(pd, pd_hbm, osem.at[3])
    out_pd.start()
    pending.append(out_pd)
    squeeze = links.row_end(rbuf3, copies)
    ibuf3[links.i, 0:1] = row_sum(squeeze)
    ibuf3[links.i, 1:2] = row_sum(squeeze * squeeze)
    total = links.img_total(ibuf3, isem3)
    mean, factor, scale, offset = norm_terms(
        total[0:1], total[1:2], float(images * n_img), g_at[...], h_at[...]
    )
    v_at[0:1] = factor
    v_at[1:8] = jnp.zeros((7, v_at.shape[1]), F32)
    at_norm[...] = (squeeze - mean) * factor
    z = at_norm[...] * g_at[...] + h_at[...]
    at_out[...] = z
    attend = z * sigmoid(z)
    upf = up[...].astype(F32)
    lean = mm(attend, upf[:, :mid] - upf[:, mid:], HIGH) + (bias[:, :mid] - bias[:, mid:])
    w0[...] = sigmoid(lean)
    w1[...] = sigmoid(-lean)


    def mixing(i, c):
        v = w0[pl.ds(i, 1)] * pp[i, :, :, 0:mid].reshape(cells, mid)
        v = v + pp[i, :, :, mid:].reshape(cells, mid)
        mx[i] = v.astype(BF16).reshape(slots, cols, mid)
        return c

    lax.fori_loop(0, images, mixing, 0, unroll=2)
    v = mx[...].reshape(images * cells, mid)
    v = mm_tn(v, jnp.concatenate([v, jnp.ones((images * cells, 128), BF16)], axis=1))
    gram[...] = v[:, 0:mid]
    mixed_sum[...] = v[:, mid:]
    out_mx = pltpu.make_async_copy(mx, mx_hbm, osem.at[4])
    out_mx.start()
    pending.append(out_mx)
    out_xt.wait()
    pending = [c for c in pending if c is not out_xt]
    gw = xt.at[0:mid]
    gw[...] = mm_terms(mm, gram[...], we[...], 3)
    wef = we[...].astype(F32)
    rbuf4[r, 0:1] = row_sum(wide(mixed_sum[...], ch // 128) * wef)
    rbuf4[r, 1:2] = row_sum(gw[...] * wef)
    ibuf4[links.i] = links.row_total(rbuf4, rsem4)
    total = links.img_total(ibuf4, isem4)
    mean, factor, scale, offset = norm_terms(total[0:1], total[1:2], n, g3[...], h3[...])
    v3[0:1] = mean
    v3[1:2] = factor
    v3[2:3] = scale
    v3[3:4] = offset
    v3[4:5] = 0.5 * scale
    v3[5:6] = 0.5 * offset
    v3[6:8] = jnp.zeros((2, ch), F32)
    awe[...] = (wef * scale).astype(BF16)
    for k, (src, dst) in enumerate([(gw, gw_hbm), (awe, awe_hbm), (wt, wt_hbm)]):
        copy = pltpu.make_async_copy(src, dst, osem.at[6 + k])
        copy.start()
        pending.append(copy)

    for copy in pending:
        copy.wait()


def sd(shape, dtype=F32):
    return jax.ShapeDtypeStruct(shape, dtype)


def call_forward(n_img, n_row, args, images, slots, cols, ch, mid, inter):
    n = n_img * n_row
    cells = (images, slots, cols)
    outs = [
        (sd(cells + (mid,)), ANY),
        (sd((images, slots + 2, cols, 3 * mid), BF16), ANY),
        (sd(cells + (2 * mid,)), ANY),
        (sd(cells + (mid,), BF16), ANY),
        (sd(cells + (mid,), BF16), ANY),
        (sd(cells + (128,)), ANY),
        (sd((mid + 8, ch)), ANY),
        (sd((8, mid)), VMEM),
        (sd((8, 2 * mid)), VMEM),
        (sd((8, ch)), VMEM),
        (sd((8, inter)), VMEM),
        (sd((images, inter)), VMEM),
        (sd((images, inter)), VMEM),
        (sd((images, mid)), VMEM),
        (sd((images, mid)), VMEM),
        (sd((images, mid)), VMEM),
        (sd((images, mid)), VMEM),
        (sd((mid, ch)), ANY),
        (sd((mid, ch), BF16), ANY),
        (sd((2, 3 * mid, 3 * mid // 2), BF16), ANY),
        (sd((mid, 128)), VMEM),
    ]
    dma = pltpu.SemaphoreType.DMA
    scratch = [
        pltpu.VMEM(cells + (mid,), F32),
        pltpu.VMEM(cells + (2 * mid,), F32),
        pltpu.VMEM(cells + (2 * mid,), F32),
        pltpu.VMEM(cells + (mid,), BF16),
        pltpu.VMEM(cells + (mid,), BF16),
        pltpu.VMEM(cells + (128,), F32),
        pltpu.VMEM((mid + 8, ch), F32),
        pltpu.VMEM((images, slots, cols, ch), BF16),
        pltpu.VMEM((GROUP, slots + 2, cols, 3 * mid), BF16),
        pltpu.VMEM((GROUP, slots + 2, cols, 3 * mid), BF16),
        pltpu.VMEM(args[6].shape, BF16),
        pltpu.VMEM((mid, ch), BF16),
        pltpu.VMEM((mid, ch), BF16),
        pltpu.VMEM((2, 3 * mid, 3 * mid // 2), BF16),
        pltpu.VMEM((3, 8, mid), F32),
        pltpu.VMEM((2, 8, 2 * mid), F32),
        pltpu.VMEM((mid, mid), F32),
        pltpu.VMEM((images, cols, mid), F32),
        pltpu.VMEM((images, cols, mid), F32),
        pltpu.VMEM((images, cols, mid), F32),
        pltpu.VMEM((n, 4, mid), F32),
        pltpu.VMEM((n, 2, 2 * mid), F32),
        pltpu.VMEM((n_row, images, inter), F32),
        pltpu.VMEM((n_img, 2, inter), F32),
        pltpu.VMEM((n_row, 2, ch), F32),
        pltpu.VMEM((n_img, 2, ch), F32),
        dma((images // GROUP,)),
        dma((9,)),
        dma((2,)),
        dma((4,)),
        dma((2, n)),
        dma((2, n)),
        dma((2, n_row)),
        dma((2, n_img)),
        dma((2, n_row)),
        dma((2, n_img)),
    ]
    in_specs = [SMEM, SMEM, ANY] + [VMEM] * (len(args) - 3)
    for k in (6, 14):
        in_specs[k] = ANY
    return pl.pallas_call(
        functools.partial(forward_kernel, n_img, n_row),
        out_shape=[o for o, _ in outs],
        in_specs=in_specs,
        out_specs=[s for _, s in outs],
        scratch_shapes=scratch,
        name="forward",
        compiler_params=pltpu.CompilerParams(
            collective_id=0, has_side_effects=True, vmem_limit_bytes=62 * 1024 * 1024
        ),
    )(*args)


PART = 2


def third_kernel(counts, group, x, cot, mx, we, awe, v3, bo, sg, q, m_out, *parts):
    per, slots, cols, ch = x.shape
    mid = mx.shape[-1]
    cells = PART * slots * cols
    columns = lax.broadcasted_iota(jnp.int32, (cols, 128), 0)

    @pl.when(pl.program_id(0) == 0)
    def _():
        m_out[...] = jnp.zeros_like(m_out)

    def product(p):
        v = mx[p * PART : (p + 1) * PART].reshape(cells, mid)
        parts[p][...] = mm(v, we[...])

    product(0)
    for p in range(per // PART):
        if p + 1 < per // PART:
            product(p + 1)
        for k in range(PART):
            i = p * PART + k
            image = pl.program_id(0) * per + i
            inside = jnp.where(columns < 12 + 2 * group[image], 1.0, 0.0).astype(F32)
            for s in range(slots):
                held = jnp.where(s < counts[image], 1.0, 0.0).astype(F32)
                m = wide(inside * held, ch // 128)
                at = (k * slots + s) * cols
                half = parts[p][at : at + cols] * v3[4:5] + v3[5:6] + 0.5 * x[i, s].astype(F32)
                th = jnp.tanh(half)
                up = 1.0 + th
                act = half * up
                bo[i, s] = (act * m).astype(BF16)
                slope = up + act * (1.0 - th)
                sg[i, s] = (cot[i, s].astype(F32) * (0.5 * m) * slope).astype(BF16)
        v = sg[p * PART : (p + 1) * PART].reshape(cells, ch)
        q[p * PART : (p + 1) * PART] = mm_nt(v, awe[...]).reshape(PART, slots, cols, mid)
    v = sg[...].reshape(per * slots * cols, ch)
    m_out[0:mid] += mm_tn(mx[...].reshape(per * slots * cols, mid), v)
    m_out[mid : mid + 16] += mm(jnp.ones((16, per * slots * cols), BF16), v)


def call_third(counts, group, x, cot, mx, we, awe, v3):
    images, slots, cols, ch = x.shape
    mid = mx.shape[-1]
    per = 8

    def cells(c):
        return pl.BlockSpec((per, slots, cols, c), lambda b: (b, 0, 0, 0))

    def whole(a):
        return pl.BlockSpec(a.shape, lambda b: (0,) * a.ndim)

    return pl.pallas_call(
        third_kernel,
        out_shape=[
            sd(x.shape, BF16),
            sd(x.shape, BF16),
            sd((images, slots, cols, mid)),
            sd((mid + 16, ch)),
        ],
        grid=(images // per,),
        in_specs=[SMEM, SMEM, cells(ch), cells(ch), cells(mid), whole(we), whole(awe), whole(v3)],
        out_specs=[
            cells(ch),
            cells(ch),
            cells(mid),
            pl.BlockSpec((mid + 16, ch), lambda b: (0, 0)),
        ],
        scratch_shapes=[pltpu.VMEM((PART * slots * cols, ch), F32)] * (per // PART),
        name="third",
        compiler_params=pltpu.CompilerParams(vmem_limit_bytes=60 * 1024 * 1024),
    )(counts, group, x, cot, mx, we, awe, v3)


def backward_kernel(
    n_img,
    n_row,
    counts,
    q_hbm,
    fp_hbm,
    a3_hbm,
    sp_hbm,
    pd_hbm,
    mx_hbm,
    mk_hbm,
    xt_hbm,
    x_hbm,
    v1,
    v2,
    v3,
    v_at,
    at_norm,
    at_out,
    w0,
    w1,
    pooled,
    gw_hbm,
    mixed_sum,
    m_in,
    area,
    g_at,
    wt_hbm,
    down,
    up,
    we,
    awe,
    fg_hbm,
    expand_out,
    split_out,
    reduce_out,
    up_out,
    down_out,
    bias_out,
    b1,
    b2,
    b3,
    b_at,
    mg,
    pd,
    mx,
    mk,
    gw,
    wt,
    split_part,
    small_part,
    rows_all,
    edge,
    ret,
    acc1,
    acc2,
    mb,
    dpart,
    pgrad,
    ibuf5,
    rbuf5,
    rbuf6,
    ibuf6,
    buf7,
    buf8,
    lsem,
    a3sem,
    hsem,
    rsem5,
    isem5,
    rsem6,
    isem6,
    sem7,
    sem8,
    rsem9,
    *reducers,
):
    images, slots, cols, mid = q_hbm.shape
    ch = we.shape[1]
    inter = down.shape[1]
    half = mid // 2
    blocks = images // GROUP
    cells = slots * cols
    links = Links(n_img, n_row)
    r, me = links.r, links.all_me()
    links.greet()
    sizes = reducer_sizes(n_row, ch, mid, inter)
    count = Reducer.COUNT
    expand_red, split_red, reduce_red, small_red = [
        Reducer(links, rows, width, reducers[k * count : (k + 1) * count])
        for k, (rows, width, _) in enumerate(sizes)
    ]
    n = v1[4:5, 0:1]
    up_rows, down_rows = inter // n_row, mid // n_row
    prev_dev = (links.i, lax.rem(r + n_row - 1, n_row))
    next_dev = (links.i, lax.rem(r + 1, n_row))
    has_prev = r > 0
    has_next = r < n_row - 1
    to_prev = pltpu.make_async_remote_copy(
        src_ref=edge.at[0],
        dst_ref=ret.at[1],
        send_sem=hsem.at[0],
        recv_sem=hsem.at[1],
        device_id=prev_dev,
        device_id_type=MESH,
    )
    to_next = pltpu.make_async_remote_copy(
        src_ref=edge.at[1],
        dst_ref=ret.at[0],
        send_sem=hsem.at[2],
        recv_sem=hsem.at[3],
        device_id=next_dev,
        device_id_type=MESH,
    )

    def columns_back(t, lines):
        col = lax.rem(lax.broadcasted_iota(jnp.int32, (lines, half), 0), cols)
        left = jnp.where(col == cols - 1, 0.0, pltpu.roll(t[:, 0:half], lines - 1, 0))
        right = jnp.where(col == 0, 0.0, pltpu.roll(t[:, 2 * half : 3 * half], 1, 0))
        return left + t[:, half : 2 * half] + right

    def small_piece(p):
        return small_part[p]

    def to_second_grads(sp, ub):
        loads = [
            pltpu.make_async_copy(src, dst, lsem.at[k])
            for k, (src, dst) in enumerate(
                [(mx_hbm, mx), (q_hbm, mg), (pd_hbm, pd), (mk_hbm, mk), (sp_hbm, sp)]
            )
        ]
        load_gw = pltpu.make_async_copy(gw_hbm, gw, lsem.at[5])
        load_wt = pltpu.make_async_copy(wt_hbm, wt, lsem.at[6])
        load_gw.start()
        for load in loads:
            load.start()
        load_wt.start()
        pending = list(loads)

        mean3, factor3, scale3 = v3[0:1], v3[1:2], v3[2:3]
        wef = we[...].astype(F32)
        rbuf5[r, 0:1] = m_in[mid : mid + 1]
        rbuf5[r, 1:2] = factor3 * (row_sum(m_in[0:mid] * wef) - mean3 * m_in[mid : mid + 1])
        links.met()
        ibuf5[links.i] = links.row_total(rbuf5, rsem5)
        total = links.img_total(ibuf5, isem5)
        b3[...] = total
        slope3, offset3 = norm_back_terms(mean3, factor3, scale3, n, total[0:1], total[1:2])
        slope = factor3 * (total[1:2] / n)
        level = jnp.broadcast_to(total[0:1] / n - slope * mean3, (16, ch))
        lefts = []
        for v, terms in ((wef * slope, 2), (level, 3)):
            for _ in range(terms):
                lefts.append(v.astype(BF16))
                v = v - lefts[-1].astype(F32)
        v = mm_nt(jnp.concatenate(lefts, axis=0), awe[...])
        fix = v[0:mid] + v[mid : 2 * mid]
        ev = v[2 * mid : 2 * mid + 1] + v[2 * mid + 16 : 2 * mid + 17] + v[2 * mid + 32 : 2 * mid + 33]
        high = fix.astype(BF16)
        mb[0:mid] = high
        mb[mid:] = (fix - high.astype(F32)).astype(BF16)

        def expand_piece(p):
            rows = pl.ds(pl.multiple_of(p * (mid // n_row), mid // n_row), mid // n_row)
            return (
                m_in[rows] * scale3 - wide(mixed_sum[rows], ch // 128) * offset3 - gw[rows] * slope3
            )

        load_gw.wait()
        expand_red.begin(expand_piece)

        for load in loads[:4]:
            load.wait()
        del pending[:4]

        def mix_back(b, c):
            v = mx[pl.ds(b * GROUP, GROUP)].reshape(GROUP * cells, mid)
            v = mm(jnp.concatenate([v, v], axis=1), mb[...])
            for k in range(GROUP):
                i = b * GROUP + k
                m = wide(mk[i].reshape(cells, 128), mid // 128)
                w = mg[i].reshape(cells, mid) - v[k * cells : (k + 1) * cells] - m * ev
                mg[i] = w.reshape(slots, cols, mid)
                dpart[pl.ds(i, 1)] = row_sum(fold(w * pd[i].reshape(cells, mid).astype(F32)))
            return c

        lax.fori_loop(0, blocks, mix_back, 0)

        upf = up[...].astype(F32)
        lean = dpart[...] * w0[...] * w1[...]
        rbuf6[r] = mm_nt(lean, upf[:, :mid] - upf[:, mid:], HIGH)
        copies = links.row_start(rbuf6, rsem6)
        z = at_out[...]
        attend = z * sigmoid(z)
        up_part = mm_tn(attend, lean, HIGH)
        bias_part = row_sum(lean)
        loads[4].wait()
        del pending[0]

        def slopes(i, c):
            m = wide(mk[i].reshape(cells, 128), mid // 128)
            for g in range(2):
                lanes = slice(g * mid, (g + 1) * mid)
                v = sp[i, :, :, lanes].reshape(cells, mid) * v2[2:3, lanes] + v2[3:4, lanes]
                ub[i, :, :, lanes] = (swish_slope(v) * m).reshape(slots, cols, mid)
            return c

        lax.fori_loop(0, images * 2 // 5, slopes, 0, unroll=2)
        attend_grad = links.row_end(rbuf6, copies) * swish_slope(z)
        ibuf6[links.i, 0:1] = row_sum(attend_grad)
        ibuf6[links.i, 1:2] = row_sum(attend_grad * at_norm[...])
        links.img_start(ibuf6, isem6)
        lax.fori_loop(images * 2 // 5, images, slopes, 0, unroll=2)
        total = links.img_end(ibuf6, isem6)
        b_at[...] = total
        count = float(images * n_img)
        squeeze_grad = (
            g_at[...]
            * v_at[0:1]
            * (attend_grad - total[0:1] / count - at_norm[...] * (total[1:2] / count))
        )
        down_part = mm_tn(pooled[...], squeeze_grad, HIGH)
        for p in range(n_row):
            lines = down_part[p * down_rows : (p + 1) * down_rows]
            small_part[p, 0:up_rows] = up_part[p * up_rows : (p + 1) * up_rows]
            small_part[p, up_rows : up_rows + down_rows // 2] = jnp.concatenate(
                [lines[: down_rows // 2], lines[down_rows // 2 :]], axis=1
            )
            small_part[p, up_rows + down_rows // 2 :] = jnp.broadcast_to(bias_part, (8, mid))

        small_red.begin(small_piece)
        expand_red.second(expand_piece)
        pgrad[...] = mm_nt(squeeze_grad, down[...].astype(F32), HIGH) / area[...]

        def with_second_grads(a3, geb):
            load_wt.wait()
            acc2[...] = jnp.zeros_like(acc2)

            def second_back(i, c):
                v = mg[i].reshape(cells, mid)
                for g, w in enumerate((w0, w1)):
                    lanes = slice(g * mid, (g + 1) * mid)
                    s = sp[i, :, :, lanes].reshape(cells, mid)
                    grad = v * w[pl.ds(i, 1)] + pgrad[pl.ds(i, 1)]
                    grad = grad * ub[i, :, :, lanes].reshape(cells, mid)
                    ub[i, :, :, lanes] = grad.reshape(slots, cols, mid)
                    acc2[0, :, lanes] += fold(grad)
                    acc2[1, :, lanes] += fold(grad * s)
                return c

            lax.fori_loop(0, images, second_back, 0, unroll=2)
            mean2, factor2, scale2 = v2[0:1], v2[1:2], v2[2:3]
            s0 = row_sum(acc2[0])
            buf7[me, 0:1] = s0
            buf7[me, 1:2] = factor2 * (row_sum(acc2[1]) - mean2 * s0)
            links.all_start(buf7, sem7)
            total = links.all_wait(buf7, sem7)
            b2[...] = total
            slope2, offset2 = norm_back_terms(mean2, factor2, scale2, n, total[0:1], total[1:2])
            expand_red.third()

            def second_grad(grad, s, m):
                return (grad * scale2 - m * (offset2 + slope2 * s)).astype(BF16)

            for side, dy in ((0, 0), (1, 2)):

                def edge_rows(i, c):
                    at = 0 if side == 0 else jnp.maximum(counts[i] - 1, 0)
                    m = wide(mk[i, 0], 2 * mid // 128)
                    geb[i] = second_grad(ub[i, at], sp[i, at], m)
                    return c

                lax.fori_loop(0, images, edge_rows, 0, unroll=2)
                for g in range(2):
                    v = geb[:, :, g * mid : (g + 1) * mid].reshape(images * cols, mid)
                    t = mm(v, wt[g, dy * mid : (dy + 1) * mid])
                    edge[side, :, :, g * half : (g + 1) * half] = (
                        columns_back(t, images * cols).astype(BF16).reshape(images, cols, half)
                    )
                if side == 0:

                    @pl.when(has_prev)
                    def _():
                        to_prev.start()

                else:

                    @pl.when(has_next)
                    def _():
                        to_next.start()

            @pl.when(jnp.logical_not(has_prev))
            def _():
                ret[0] = jnp.zeros(ret.shape[1:], BF16)

            @pl.when(jnp.logical_not(has_next))
            def _():
                ret[1] = jnp.zeros(ret.shape[1:], BF16)

            def a3_copy(b, slot):
                return pltpu.make_async_copy(
                    a3_hbm.at[pl.ds(b * GROUP, GROUP)], a3.at[slot], a3sem.at[slot]
                )

            a3_copy(0, 0).start()
            split_part[...] = jnp.zeros_like(split_part)

            def split_grads(b, c):
                slot = lax.rem(b, 2)

                @pl.when(b + 1 < blocks)
                def _():
                    a3_copy(b + 1, 1 - slot).start()

                @pl.when(b == 2)
                def _():
                    small_red.second(small_piece)

                @pl.when(b == 4)
                def _():
                    expand_red.fourth()

                @pl.when(b == 6)
                def _():
                    small_red.third()

                def one(k, c):
                    i = b * GROUP + k
                    m = wide(mk[i].reshape(cells, 128), 2 * mid // 128)
                    v = second_grad(ub[i].reshape(cells, 2 * mid), sp[i].reshape(cells, 2 * mid), m)
                    mx[i] = v[:, 0:mid].reshape(slots, cols, mid)
                    pd[i] = v[:, mid:].reshape(slots, cols, mid)
                    return c

                lax.fori_loop(0, GROUP, one, 0)
                a3_copy(b, slot).wait()
                for g, grads in enumerate((mx, pd)):
                    v = grads[pl.ds(b * GROUP, GROUP)].reshape(GROUP * cells, mid)
                    taps = jnp.concatenate(
                        [
                            a3[slot, :, dy : dy + slots, :, g * 3 * half : (g + 1) * 3 * half].reshape(
                                GROUP * cells, 3 * half
                            )
                            for dy in range(3)
                        ],
                        axis=1,
                    )
                    split_part[g] += mm_tn(v, taps)
                return c

            lax.fori_loop(0, blocks, split_grads, 0)

        pl.run_scoped(
            with_second_grads,
            pltpu.VMEM((2, GROUP, slots + 2, cols, 3 * mid), BF16),
            pltpu.VMEM((images, cols, 2 * mid), BF16),
        )

    pl.run_scoped(
        to_second_grads,
        pltpu.VMEM((images, slots, cols, 2 * mid), F32),
        pltpu.VMEM((images, slots, cols, 2 * mid), F32),
    )

    def to_inputs(fp, xs, xt, xu, split_rows):
        loads = [
            pltpu.make_async_copy(fp_hbm, fp, lsem.at[5]),
            pltpu.make_async_copy(xt_hbm, xt, lsem.at[6]),
            pltpu.make_async_copy(x_hbm, xs, lsem.at[4]),
        ]
        for load in loads:
            load.start()

        def split_piece(p):
            lines = []
            for tap in range(9):
                at = pl.multiple_of(tap * half + p * (half // n_row), half // n_row)
                lines.append(split_rows[pl.ds(at, half // n_row)])
            return jnp.concatenate(lines, axis=0).astype(F32)

        for g in range(2):
            for tap in range(9):
                split_rows[tap * half : (tap + 1) * half, g * mid : (g + 1) * mid] = jnp.transpose(
                    split_part[g, :, tap * half : (tap + 1) * half].astype(BF16)
                )
        split_red.begin(split_piece)
        @pl.when(has_prev)
        def _():
            to_prev.wait_send()
            to_next.wait_recv()

        @pl.when(has_next)
        def _():
            to_next.wait_send()
            to_prev.wait_recv()

        loads[0].wait()
        acc1[...] = jnp.zeros_like(acc1)

        def conv_back(b, c):
            @pl.when(b == 1)
            def _():
                split_red.second(split_piece)

            @pl.when(b == 3)
            def _():
                small_red.fourth()

            @pl.when(b == 5)
            def _():
                split_red.third()

            blank = jnp.zeros((GROUP, 1, cols, mid), BF16)
            for g, grads in enumerate((mx, pd)):
                v = grads[pl.ds(b * GROUP, GROUP)]
                moved = (
                    jnp.concatenate([v[:, 1:], blank], axis=1),
                    v,
                    jnp.concatenate([blank, v[:, : slots - 1]], axis=1),
                )
                v = jnp.concatenate(
                    [moved[dy].reshape(GROUP * cells, mid) for dy in range(3)], axis=1
                )
                value = mm(v, wt[g])
                back = columns_back(value, GROUP * cells)
                lanes = slice(g * half, (g + 1) * half)
                for k in range(GROUP):
                    i = b * GROUP + k
                    m = mk[i].reshape(cells, 128)
                    low = ret[1, i, :, lanes].astype(F32)
                    parts = []
                    for s in range(slots):
                        at = k * cells + s * cols
                        here = back[at : at + cols] + low * jnp.where(counts[i] - 1 == s, 1.0, 0.0).astype(F32)
                        if s == 0:
                            here = here + ret[0, i, :, lanes].astype(F32)
                        parts.append(here)
                    v = fp[i, :, :, lanes].reshape(cells, half)
                    z = v * v1[2:3, lanes] + v1[3:4, lanes]
                    grad = jnp.concatenate(parts, axis=0) * swish_slope(z) * wide(m, half // 128)
                    mg[i, :, :, lanes] = grad.reshape(slots, cols, half)
                    acc1[0, :, lanes] += fold(grad)
                    acc1[1, :, lanes] += fold(grad * v)
            return c

        lax.fori_loop(0, blocks, conv_back, 0)
        expand_out[...] = expand_red.end()
        rows_all[r] = small_red.end()
        rows_copies = links.row_copies(rows_all, rsem9)
        s0 = row_sum(acc1[0])
        buf8[me, 0:1] = s0
        buf8[me, 1:2] = v1[1:2] * (row_sum(acc1[1]) - v1[0:1] * s0)
        links.all_start(buf8, sem8)

        def narrow(i, c):
            pd[i] = mg[i].astype(BF16)
            return c

        lax.fori_loop(0, images, narrow, 0, unroll=4)
        loads[2].wait()
        lines = images * cells
        width = ch // 2
        for k in range(2):
            xu[:, k * width : (k + 1) * width] = mm_tn(
                pd[...].reshape(lines, mid), xs[:, :, :, k * width : (k + 1) * width].reshape(lines, width)
            )
        loads[1].wait()
        total = links.all_wait(buf8, sem8)
        b1[...] = total
        slope1, offset1 = norm_back_terms(v1[0:1], v1[1:2], v1[2:3], n, total[0:1], total[1:2])

        def column(v):
            return wide(jnp.transpose(jnp.broadcast_to(v, (128, mid))), ch // n_row // 128)

        scale_c, slope_c, offset_c = column(v1[2:3]), column(slope1), column(offset1)

        def reduce_piece(p):
            lanes = pl.ds(pl.multiple_of(p * (ch // n_row), ch // n_row), ch // n_row)
            v = xu[:, lanes] * scale_c - xt[mid : mid + 1, lanes] * offset_c - xt[0:mid, lanes] * slope_c
            return jnp.transpose(v.astype(BF16)).astype(F32)

        reduce_red.begin(reduce_piece)
        for copy in rows_copies:
            copy.start()
        split_red.fourth()

        def first_grad(i, c):
            m = wide(mk[i].reshape(cells, 128), mid // 128)
            v = mg[i].reshape(cells, mid) * v1[2:3] - m * (
                offset1 + slope1 * fp[i].reshape(cells, mid)
            )
            mx[i] = v.astype(BF16).reshape(slots, cols, mid)
            return c

        lax.fori_loop(0, images // 2, first_grad, 0)
        reduce_red.second(reduce_piece)
        lax.fori_loop(images // 2, images, first_grad, 0)
        out_fg = pltpu.make_async_copy(mx, fg_hbm, lsem.at[7])
        out_fg.start()
        reduce_red.third()
        split_out[...] = split_red.end()
        for copy in rows_copies:
            copy.wait()
        for p in range(n_row):
            up_out[p * up_rows : (p + 1) * up_rows] = rows_all[p, 0:up_rows]
            lines = rows_all[p, up_rows : up_rows + down_rows // 2]
            down_out[p * down_rows : (p + 1) * down_rows] = jnp.concatenate(
                [lines[:, 0:inter], lines[:, inter:]], axis=0
            )
        bias_out[...] = rows_all[0, up_rows + down_rows // 2 :]
        reduce_red.fourth()
        reduce_out[...] = reduce_red.end()
        out_fg.wait()

    pl.run_scoped(
        to_inputs,
        pltpu.VMEM((images, slots, cols, mid), F32),
        pltpu.VMEM((images, slots, cols, ch), BF16),
        pltpu.VMEM((mid + 8, ch), F32),
        pltpu.VMEM((mid, ch), F32),
        pltpu.VMEM((9 * half, 2 * mid), BF16),
    )


def reducer_sizes(n_row, ch, mid, inter):
    return [
        (mid // n_row, ch, BF16),
        (9 * (mid // 2) // n_row, 2 * mid, BF16),
        (ch // n_row, mid, BF16),
        (inter // n_row + mid // n_row // 2 + 8, mid, F32),
    ]


def call_backward(n_img, n_row, args, gw, wt, ch, inter):
    q = args[1]
    images, slots, cols, mid = q.shape
    half = mid // 2
    n = n_img * n_row
    cells = (images, slots, cols)
    sizes = reducer_sizes(n_row, ch, mid, inter)
    outs = [
        (sd(cells + (mid,), BF16), ANY),
        (sd((mid // n_row, ch)), VMEM),
        (sd((9 * half // n_row, 2 * mid)), VMEM),
        (sd((ch // n_row, mid)), VMEM),
        (sd((inter, mid)), VMEM),
        (sd((mid, inter)), VMEM),
        (sd((8, mid)), VMEM),
        (sd((2, mid)), VMEM),
        (sd((2, 2 * mid)), VMEM),
        (sd((2, ch)), VMEM),
        (sd((2, inter)), VMEM),
    ]
    dma = pltpu.SemaphoreType.DMA
    scratch = [
        pltpu.VMEM(cells + (mid,), F32),
        pltpu.VMEM(cells + (mid,), BF16),
        pltpu.VMEM(cells + (mid,), BF16),
        pltpu.VMEM(cells + (128,), F32),
        pltpu.VMEM((mid, ch), F32),
        pltpu.VMEM((2, 3 * mid, 3 * half), BF16),
        pltpu.VMEM((2, mid, 9 * half), F32),
        pltpu.VMEM((n_row, sizes[3][0], mid), F32),
        pltpu.VMEM((n_row, sizes[3][0], mid), F32),
        pltpu.VMEM((2, images, cols, mid), BF16),
        pltpu.VMEM((2, images, cols, mid), BF16),
        pltpu.VMEM((2, 8, mid), F32),
        pltpu.VMEM((2, 8, 2 * mid), F32),
        pltpu.VMEM((2 * mid, mid), BF16),
        pltpu.VMEM((images, mid), F32),
        pltpu.VMEM((images, mid), F32),
        pltpu.VMEM((n_img, 2, ch), F32),
        pltpu.VMEM((n_row, 2, ch), F32),
        pltpu.VMEM((n_row, images, inter), F32),
        pltpu.VMEM((n_img, 2, inter), F32),
        pltpu.VMEM((n, 2, 2 * mid), F32),
        pltpu.VMEM((n, 2, mid), F32),
        dma((8,)),
        dma((2,)),
        dma((4,)),
        dma((2, n_row)),
        dma((2, n_img)),
        dma((2, n_row)),
        dma((2, n_img)),
        dma((2, n)),
        dma((2, n)),
        dma((2, n_row)),
    ]
    for rows, width, dtype in sizes:
        scratch += Reducer.scratch(n_img, rows, width, dtype)
    in_specs = [SMEM] + [ANY] * 9 + [VMEM] * (len(args) - 10)
    for k, a in enumerate(args):
        if a is gw or a is wt:
            in_specs[k] = ANY
    return pl.pallas_call(
        functools.partial(backward_kernel, n_img, n_row),
        out_shape=[o for o, _ in outs],
        in_specs=in_specs,
        out_specs=[s for _, s in outs],
        scratch_shapes=scratch,
        name="backward",
        compiler_params=pltpu.CompilerParams(
            collective_id=1, has_side_effects=True, vmem_limit_bytes=62 * 1024 * 1024
        ),
    )(*args)


def input_kernel(
    fg, sg, wr, expand, split, reduce, up, down, bias, b1, b2, b3, b_at,
    gi, expand_out, split_out, reduce_out, up_out, down_out, bias_out, *lines,
):
    per, slots, cols, ch = sg.shape
    cells = per * slots * cols
    mid = fg.shape[-1]
    value = mm_nt(fg[...].reshape(cells, mid), wr[...])
    gi[...] = (value + sg[...].reshape(cells, ch).astype(F32)).astype(BF16).reshape(gi.shape)

    @pl.when(pl.program_id(0) == 0)
    def _():
        expand_out[...] = expand[...]
        split_out[...] = split[...]
        reduce_out[...] = reduce[...]
        down_out[...] = down[...]
        up_out[:, 0:mid] = up[...]
        up_out[:, mid:] = -up[...]
        bias_out[:, 0:mid] = bias[0:1]
        bias_out[:, mid:] = -bias[0:1]
        for k, v in enumerate((b1, b2, b_at, b3)):
            lines[2 * k][...] = v[1:2]
            lines[2 * k + 1][...] = v[0:1]


def call_input(fg, sg, wr, *small):
    images, slots, cols, ch = sg.shape
    mid = fg.shape[-1]
    expand, split, reduce, up, down, _, b1, b2, b3, b_at = small
    per = 14

    def cells(c):
        return pl.BlockSpec((per, slots, cols, c), lambda b: (b, 0, 0, 0))

    def whole(a):
        return pl.BlockSpec(a.shape, lambda b: (0,) * len(a.shape))

    outs = [sd(a.shape) for a in (expand, split, reduce)]
    outs += [sd((up.shape[0], 2 * mid)), sd(down.shape), sd((1, 2 * mid))]
    for v in (b1, b2, b_at, b3):
        outs += [sd((1, v.shape[1]))] * 2
    return pl.pallas_call(
        input_kernel,
        out_shape=[sd(sg.shape, BF16)] + outs,
        grid=(images // per,),
        in_specs=[cells(mid), cells(ch), whole(wr)] + [whole(a) for a in small],
        out_specs=[cells(ch)] + [whole(a) for a in outs],
        name="input_grad",
        compiler_params=pltpu.CompilerParams(vmem_limit_bytes=60 * 1024 * 1024),
    )(fg, sg, wr, *small)


def body(
    n_img,
    n_row,
    feature_map,
    image_group,
    row_counts,
    reduce_weight,
    gain_first,
    shift_first,
    split_weight,
    gain_second,
    shift_second,
    attn_down,
    gain_attend,
    shift_attend,
    attn_up,
    attn_bias,
    expand_weight,
    gain_third,
    shift_third,
    cotangent,
):
    images, slots, cols, ch = feature_map.shape
    mid = reduce_weight.shape[1]
    inter = attn_down.shape[1]
    half = mid // 2
    counts = row_counts[:, 0]
    ws = split_weight.reshape(3, 3 * half, 2 * mid)

    def line(v):
        return v[None, :]

    (
        fp, a3, sp, pd, mx, mk, xt, v1, v2, v3, v_at, at_norm, at_out, w0, w1, pooled, area,
        gw, awe, wt, mixed_sum,
    ) = call_forward(
        n_img,
        n_row,
        (
            counts,
            image_group,
            feature_map,
            reduce_weight,
            line(gain_first),
            line(shift_first),
            ws,
            line(gain_second),
            line(shift_second),
            attn_down,
            line(gain_attend),
            line(shift_attend),
            attn_up,
            line(attn_bias),
            expand_weight,
            line(gain_third),
            line(shift_third),
        ),
        images, slots, cols, ch, mid, inter,
    )
    block_out, sg, q, m_sum = call_third(
        counts, image_group, feature_map, cotangent, mx, expand_weight, awe, v3
    )
    (
        fg, grad_expand, grad_split, grad_reduce, grad_up, grad_down, bias, b1, b2, b3, b_at,
    ) = call_backward(
        n_img,
        n_row,
        (
            counts, q, fp, a3, sp, pd, mx, mk, xt, feature_map, v1, v2, v3, v_at, at_norm, at_out, w0, w1, pooled,
            gw, mixed_sum, m_sum, area, line(gain_attend), wt, attn_down, attn_up, expand_weight,
            awe,
        ),
        gw, wt, ch, inter,
    )
    small = call_input(
        fg, sg, reduce_weight, grad_expand, grad_split, grad_reduce, grad_up, grad_down, bias,
        b1, b2, b3, b_at,
    )
    grad_input, grad_expand, grad_split, grad_reduce, grad_up, grad_down = small[:6]
    return (
        block_out,
        grad_input,
        grad_reduce,
        grad_split.reshape(3, 3, half // n_row, 2 * mid),
        grad_expand,
        grad_down,
        grad_up,
    ) + tuple(v.reshape(-1) for v in small[6:])


def solution(mesh):
    cells = P("img", "row", None, None)
    in_specs = (cells, P("img"), P("img", "row")) + (P(),) * 14 + (cells,)
    out_specs = (cells, cells, P("row", None), P(None, None, "row", None), P("row", None)) + (P(),) * 11
    return jax.shard_map(
        functools.partial(body, mesh.shape["img"], mesh.shape["row"]),
        mesh=mesh,
        in_specs=in_specs,
        out_specs=out_specs,
        check_vma=False,
    )
```

```python
import functools

import jax
import jax.numpy as jnp
from jax import lax
from jax.experimental import pallas as pl
from jax.experimental.pallas import tpu as pltpu
from jax.sharding import PartitionSpec as P

MESH = pl.DeviceIdType.MESH
HIGH = lax.Precision.HIGHEST
F32 = jnp.float32
BF16 = jnp.bfloat16
EPS = 1e-05
GROUP = 8
ANY = pl.BlockSpec(memory_space=pl.ANY)
VMEM = pl.BlockSpec(memory_space=pltpu.VMEM)
SMEM = pl.BlockSpec(memory_space=pltpu.SMEM)


def dot(a, b, dims, precision=None):
    return lax.dot_general(
        a, b, (dims, ((), ())), preferred_element_type=F32, precision=precision
    )


def mm(a, b, precision=None):
    return dot(a, b, ((1,), (0,)), precision)


def mm_nt(a, b, precision=None):
    return dot(a, b, ((1,), (1,)), precision)


def mm_tn(a, b, precision=None):
    return dot(a, b, ((0,), (0,)), precision)


def mm_terms(product, a, b, terms):
    total = None
    for _ in range(terms):
        part = a.astype(BF16)
        a = a - part.astype(F32)
        value = product(part, b)
        total = value if total is None else total + value
    return total


def sigmoid(v):
    return 0.5 * jnp.tanh(0.5 * v) + 0.5


def swish_slope(v):
    s = sigmoid(v)
    return s * (1.0 + v * (1.0 - s))


def wide(mask, times):
    return jnp.concatenate([mask] * times, axis=1)


def fold(v):
    return jnp.sum(v.reshape(v.shape[0] // 8, 8, v.shape[1]), axis=0)


def row_sum(v):
    return jnp.sum(v, axis=0, keepdims=True)


class Links:
    def __init__(self, n_img, n_row):
        self.ni, self.nr = n_img, n_row
        self.i, self.r = lax.axis_index("img"), lax.axis_index("row")

    def greet(self):
        bar = pltpu.get_barrier_semaphore()

        def go(k, c):
            pl.semaphore_signal(
                bar, inc=1, device_id=self.peer(k), device_id_type=MESH
            )
            return c

        lax.fori_loop(1, self.ni * self.nr, go, 0)

    def met(self):
        pl.semaphore_wait(pltpu.get_barrier_semaphore(), self.ni * self.nr - 1)

    def peer(self, k):
        return (lax.rem(self.i + k // self.nr, self.ni), lax.rem(self.r + k % self.nr, self.nr))

    def copy(self, buf, send, recv, me, k, target):
        return pltpu.make_async_remote_copy(
            src_ref=buf.at[me],
            dst_ref=buf.at[me],
            send_sem=send.at[k],
            recv_sem=recv.at[k],
            device_id=target,
            device_id_type=MESH,
        )

    def all_me(self):
        return self.i * self.nr + self.r

    def all_start(self, buf, sems):
        def go(k, c):
            self.copy(buf, sems.at[0], sems.at[1], self.all_me(), k, self.peer(k)).start()
            return c

        lax.fori_loop(1, self.ni * self.nr, go, 0)

    def all_wait(self, buf, sems):
        def go(k, c):
            self.copy(buf, sems.at[0], sems.at[1], self.all_me(), k, self.peer(k)).wait()
            return c

        lax.fori_loop(1, self.ni * self.nr, go, 0)
        return jnp.sum(buf[...], axis=0)

    def row_copies(self, buf, sems):
        return [
            self.copy(buf, sems.at[0], sems.at[1], self.r, k, (self.i, lax.rem(self.r + k, self.nr)))
            for k in range(1, self.nr)
        ]

    def img_copy(self, buf, sems, k):
        return self.copy(
            buf, sems.at[0], sems.at[1], self.i, k, (lax.rem(self.i + k, self.ni), self.r)
        )

    def row_start(self, buf, sems):
        copies = self.row_copies(buf, sems)
        for c in copies:
            c.start()
        return copies

    def row_end(self, buf, copies):
        for c in copies:
            c.wait()
        return jnp.sum(buf[...], axis=0)

    def row_total(self, buf, sems):
        return self.row_end(buf, self.row_start(buf, sems))

    def img_start(self, buf, sems):
        def go(k, c):
            self.img_copy(buf, sems, k).start()
            return c

        lax.fori_loop(1, self.ni, go, 0)

    def img_end(self, buf, sems):
        def end(k, c):
            self.img_copy(buf, sems, k).wait()
            return c

        lax.fori_loop(1, self.ni, end, 0)
        return jnp.sum(buf[...], axis=0)

    def img_total(self, buf, sems):
        self.img_start(buf, sems)
        return self.img_end(buf, sems)


class Reducer:
    @staticmethod
    def layout(n_img, rows, width, dtype):
        lane_parts = min(width // 128, n_img)
        row_parts = n_img // lane_parts
        tile = 16 if dtype == BF16 else 8
        share = -(-rows // (row_parts * tile)) * tile
        return lane_parts, share, share * row_parts

    @staticmethod
    def scratch(n_img, rows, width, dtype):
        lane_parts, share, padded = Reducer.layout(n_img, rows, width, dtype)
        lanes = width // lane_parts
        return [
            pltpu.VMEM((2, padded, width), dtype),
            pltpu.VMEM((2, padded, width), dtype),
            pltpu.VMEM((padded, width), dtype),
            pltpu.VMEM((padded, width), dtype),
            pltpu.VMEM((padded, width), F32),
            pltpu.VMEM((n_img, share, lanes), dtype),
            pltpu.VMEM((padded, width), dtype),
            pltpu.SemaphoreType.DMA((2, 2 + 2 * n_img)),
        ]

    COUNT = 8

    def __init__(self, links, rows, width, refs):
        self.links, self.rows, self.width = links, rows, width
        (self.sb1, self.rb1, self.sb2, self.rb2, self.mine, self.rb3, self.ag, self.sems) = refs
        self.dtype = self.sb1.dtype
        self.lane_parts, self.share, self.padded = Reducer.layout(links.ni, rows, width, self.dtype)
        self.lanes = width // self.lane_parts
        r = links.r
        self.one = r + 1 - 2 * lax.rem(r, 2)
        self.two = lax.rem(r + 2, 4)

    def copy(self, src, dst, k, target):
        return pltpu.make_async_remote_copy(
            src_ref=src,
            dst_ref=dst,
            send_sem=self.sems.at[0, k],
            recv_sem=self.sems.at[1, k],
            device_id=target,
            device_id_type=MESH,
        )

    def copy1(self):
        return self.copy(self.sb1, self.rb1, 0, (self.links.i, self.one))

    def copy2(self):
        return self.copy(self.sb2, self.rb2, 1, (self.links.i, self.two))

    def part(self, ref, j):
        row = pl.multiple_of((j // self.lane_parts) * self.share, self.share)
        lane = pl.multiple_of(lax.rem(j, self.lane_parts) * self.lanes, self.lanes)
        return ref.at[pl.ds(row, self.share), pl.ds(lane, self.lanes)]

    def peer(self, k):
        return lax.rem(self.links.i + k, self.links.ni)

    def copy3(self, k):
        return self.copy(
            self.part(self.sb2, self.peer(k)), self.rb3.at[self.links.i], 2 + k, (self.peer(k), self.links.r)
        )

    def copy4(self, k):
        mine = self.part(self.ag, self.links.i)
        return self.copy(mine, mine, 2 + self.links.ni + k, (self.peer(k), self.links.r))

    def each(self, make, act):
        def go(k, c):
            act(make(k))
            return c

        lax.fori_loop(1, self.links.ni, go, 0)

    def begin(self, piece):
        odd = 1 - lax.rem(self.links.r, 2)
        for k in range(2):
            self.sb1[k, 0 : self.rows] = piece(odd + 2 * k).astype(self.dtype)
        self.copy1().start()

    def second(self, piece):
        self.copy1().wait()
        r = self.links.r
        kept = self.rb1[self.two // 2, 0 : self.rows].astype(F32)
        self.sb2[0 : self.rows] = (piece(self.two) + kept).astype(self.dtype)
        self.copy2().start()
        self.mine[0 : self.rows] = piece(r) + self.rb1[r // 2, 0 : self.rows].astype(F32)

    def third(self):
        self.copy2().wait()
        total = self.mine[0 : self.rows] + self.rb2[0 : self.rows].astype(F32)
        self.mine[0 : self.rows] = total
        self.sb2[0 : self.rows] = total.astype(self.dtype)
        self.each(self.copy3, lambda c: c.start())

    def fourth(self):
        self.each(self.copy3, lambda c: c.wait())
        total = self.part(self.mine, self.links.i)[...]
        for k in range(1, self.links.ni):
            total = total + self.rb3[self.peer(k)].astype(F32)
        self.part(self.ag, self.links.i)[...] = total.astype(self.dtype)
        self.each(self.copy4, lambda c: c.start())

    def end(self):
        self.each(self.copy4, lambda c: c.wait())
        return self.ag[0 : self.rows].astype(F32)


def norm_terms(total, square, count, gain, shift):
    mean = total / count
    factor = lax.rsqrt(square / count - mean * mean + EPS)
    scale = gain * factor
    return mean, factor, scale, shift - mean * scale


def norm_back_terms(mean, factor, scale, count, s0, s1):
    slope = scale * factor * (s1 / count)
    return slope, scale * (s0 / count) - slope * mean


def forward_kernel(
    n_img,
    n_row,
    counts,
    group,
    x_hbm,
    wr,
    g1,
    h1,
    ws_hbm,
    g2,
    h2,
    down,
    g_at,
    h_at,
    up,
    bias,
    we_hbm,
    g3,
    h3,
    fp_hbm,
    a3_hbm,
    sp_hbm,
    pd_hbm,
    mx_hbm,
    mk_hbm,
    xt_hbm,
    v1,
    v2,
    v3,
    v_at,
    at_norm,
    at_out,
    w0,
    w1,
    pooled,
    area,
    gw_hbm,
    awe_hbm,
    wt_hbm,
    mixed_sum,
    fp,
    sp,
    pp,
    pd,
    mx,
    mk,
    xt,
    xs,
    a3,
    a3b,
    ws,
    we,
    awe,
    wt,
    acc1,
    acc2,
    gram,
    bottom,
    above,
    below,
    buf1,
    buf2,
    rbuf3,
    ibuf3,
    rbuf4,
    ibuf4,
    xsem,
    osem,
    a3sem,
    hsem,
    sem1,
    sem2,
    rsem3,
    isem3,
    rsem4,
    isem4,
):
    images, slots, cols, ch = x_hbm.shape
    mid = wr.shape[1]
    half = mid // 2
    blocks = images // GROUP
    cells = slots * cols
    links = Links(n_img, n_row)
    r = links.r
    links.greet()

    def x_copy(b):
        at = pl.ds(b * GROUP, GROUP)
        return pltpu.make_async_copy(x_hbm.at[at], xs.at[at], xsem.at[b])

    def x_start(b, c):
        x_copy(b).start()
        return c

    lax.fori_loop(0, blocks, x_start, 0)
    pending = []
    in_ws = pltpu.make_async_copy(ws_hbm, ws, osem.at[6])
    in_we = pltpu.make_async_copy(we_hbm, we, osem.at[7])

    def masks(i, c):
        count, height = counts[i], 12 + 2 * group[i]
        area[pl.ds(i, 1)] = jnp.full((1, mid), 1, F32) * (height * height).astype(F32)
        rows = lax.broadcasted_iota(jnp.int32, (slots, cols, 128), 0)
        columns = lax.broadcasted_iota(jnp.int32, (slots, cols, 128), 1)
        mk[i] = jnp.where((rows < count) & (columns < height), 1.0, 0.0).astype(F32)
        return c

    lax.fori_loop(0, images, masks, 0)
    acc1[...] = jnp.zeros_like(acc1)
    lines = GROUP * cells

    def first(b, c):
        x_copy(b).wait()
        at = pl.ds(b * GROUP, GROUP)
        v = mm(xs[at].reshape(lines, ch), wr[...])
        fp[at] = v.reshape(GROUP, slots, cols, mid)
        m = mk[at].reshape(lines, 128)
        w = v * wide(m, mid // 128)
        mx[at] = w.astype(BF16).reshape(GROUP, slots, cols, mid)
        pd[at, :, :, 0:128] = mk[at].astype(BF16)
        acc1[0] += fold(w)
        acc1[1] += fold(w * v)
        acc1[2, :, 0:128] += fold(m)
        for k in range(GROUP):
            i = b * GROUP + k
            bottom[i] = fp[i, jnp.maximum(counts[i] - 1, 0)]
        return c

    lax.fori_loop(0, blocks, first, 0)
    in_ws.start()
    in_we.start()
    pending += [in_ws, in_we]
    out_mk = pltpu.make_async_copy(mk, mk_hbm, osem.at[1])
    out_mk.start()
    pending.append(out_mk)
    out_fp = pltpu.make_async_copy(fp, fp_hbm, osem.at[0])
    out_fp.start()
    pending.append(out_fp)

    me = links.all_me()
    buf1[me, 0:1] = row_sum(acc1[0])
    buf1[me, 1:2] = row_sum(acc1[1])
    n_here = row_sum(acc1[2, :, 0:128])
    buf1[me, 2:3] = wide(n_here, mid // 128)
    buf1[me, 3:4] = jnp.zeros((1, mid), F32)

    prev_dev = (links.i, lax.rem(r + n_row - 1, n_row))
    next_dev = (links.i, lax.rem(r + 1, n_row))
    to_prev = pltpu.make_async_remote_copy(
        src_ref=fp.at[:, 0],
        dst_ref=below,
        send_sem=hsem.at[0],
        recv_sem=hsem.at[1],
        device_id=prev_dev,
        device_id_type=MESH,
    )
    to_next = pltpu.make_async_remote_copy(
        src_ref=bottom,
        dst_ref=above,
        send_sem=hsem.at[2],
        recv_sem=hsem.at[3],
        device_id=next_dev,
        device_id_type=MESH,
    )
    has_prev = r > 0
    has_next = r < n_row - 1

    links.met()
    links.all_start(buf1, sem1)

    @pl.when(has_prev)
    def _():
        to_prev.start()

    @pl.when(has_next)
    def _():
        to_next.start()

    @pl.when(jnp.logical_not(has_prev))
    def _():
        above[...] = jnp.zeros_like(above)

    @pl.when(jnp.logical_not(has_next))
    def _():
        below[...] = jnp.zeros_like(below)

    v = jnp.concatenate(
        [mx[...].reshape(images * cells, mid), pd[:, :, :, 0:128].reshape(images * cells, 128)], axis=1
    )
    width = ch // 2
    for k in range(2):
        xt[:, k * width : (k + 1) * width] = mm_tn(
            v, xs[:, :, :, k * width : (k + 1) * width].reshape(images * cells, width)
        )[0 : mid + 8]
    out_xt = pltpu.make_async_copy(xt, xt_hbm, osem.at[5])
    out_xt.start()
    pending.append(out_xt)
    total = links.all_wait(buf1, sem1)
    n = total[2:3, 0:1]
    mean, factor, scale, offset = norm_terms(total[0:1], total[1:2], n, g1[...], h1[...])
    v1[0:1] = mean
    v1[1:2] = factor
    v1[2:3] = scale
    v1[3:4] = offset
    v1[4:5] = total[2:3]
    v1[5:8] = jnp.zeros((3, mid), F32)

    @pl.when(has_prev)
    def _():
        to_prev.wait_send()
        to_next.wait_recv()

    @pl.when(has_next)
    def _():
        to_next.wait_send()
        to_prev.wait_recv()

    prev_flag = has_prev.astype(F32)
    next_flag = has_next.astype(F32)
    ext = (slots + 2) * cols
    col_index = lax.rem(lax.broadcasted_iota(jnp.int32, (ext, mid), 0), cols)
    acc2[...] = jnp.zeros_like(acc2)

    in_ws.wait()
    in_we.wait()
    del pending[:2]
    buffers = (a3, a3b)

    def a3_copy(b, slot):
        return pltpu.make_async_copy(
            buffers[slot], a3_hbm.at[pl.ds(b * GROUP, GROUP)], a3sem.at[slot]
        )

    def spread(b, slot):
        for k in range(GROUP):
            i = b * GROUP + k
            m = mk[i].reshape(cells, 128)
            cm = wide(m[0:cols], mid // 128)
            z = fp[i].reshape(cells, mid) * v1[2:3] + v1[3:4]
            own = z * sigmoid(z) * wide(m, mid // 128)
            z = above[i] * v1[2:3] + v1[3:4]
            top = z * sigmoid(z) * (cm * prev_flag)
            z = below[i] * v1[2:3] + v1[3:4]
            low = z * sigmoid(z) * (cm * next_flag)
            count = counts[i]
            parts = [top]
            for s in range(slots + 1):
                here = low * jnp.where(count == s, 1.0, 0.0).astype(F32)
                if s < slots:
                    here = here + own[s * cols : (s + 1) * cols]
                parts.append(here)
            full = jnp.concatenate(parts, axis=0)
            left = jnp.where(col_index == 0, 0.0, pltpu.roll(full, 1, 0)).astype(BF16)
            right = jnp.where(col_index == cols - 1, 0.0, pltpu.roll(full, ext - 1, 0)).astype(BF16)
            full = full.astype(BF16)
            for g in range(2):
                for d, v in enumerate((left, full, right)):
                    lanes = slice((3 * g + d) * half, (3 * g + d + 1) * half)
                    buffers[slot][k, :, :, lanes] = v[:, g * half : (g + 1) * half].reshape(
                        slots + 2, cols, half
                    )

    def convolve(b, slot):
        m = wide(mk[pl.ds(b * GROUP, GROUP)].reshape(lines, 128), mid // 128)
        for g in range(2):
            lanes = slice(g * mid, (g + 1) * mid)
            taps = jnp.concatenate(
                [
                    buffers[slot][:, dy : dy + slots, :, g * 3 * half : (g + 1) * 3 * half].reshape(
                        lines, 3 * half
                    )
                    for dy in range(3)
                ],
                axis=1,
            )
            v = mm(taps, ws[:, :, lanes].reshape(9 * half, mid))
            sp[pl.ds(b * GROUP, GROUP), :, :, lanes] = v.reshape(GROUP, slots, cols, mid)
            w = v * m
            acc2[0, :, lanes] += fold(w)
            acc2[1, :, lanes] += fold(w * v)

    def second(b, slot, more):
        a3_copy(b, slot).start()
        convolve(b, slot)
        if more:

            @pl.when(b >= 1)
            def _():
                a3_copy(b - 1, 1 - slot).wait()

            spread(b + 1, 1 - slot)

    spread(0, 0)

    def pair(j, c):
        second(2 * j, 0, True)
        second(2 * j + 1, 1, True)
        return c

    pairs = (blocks - 1) // 2
    lax.fori_loop(0, pairs, pair, 0)
    rest = blocks - 2 * pairs
    second(2 * pairs, 0, rest == 2)
    if rest == 2:
        second(2 * pairs + 1, 1, False)
    pending += [a3_copy(0, 0), a3_copy(0, 1)]
    out_sp = pltpu.make_async_copy(sp, sp_hbm, osem.at[2])
    out_sp.start()
    pending.append(out_sp)

    buf2[me, 0:1] = row_sum(acc2[0])
    buf2[me, 1:2] = row_sum(acc2[1])
    links.all_start(buf2, sem2)
    for g in range(2):
        for dy in range(3):
            wt[g, dy * mid : (dy + 1) * mid] = jnp.transpose(ws[dy, :, g * mid : (g + 1) * mid])
    total = links.all_wait(buf2, sem2)
    mean, factor, scale, offset = norm_terms(total[0:1], total[1:2], n, g2[...], h2[...])
    v2[0:1] = mean
    v2[1:2] = factor
    v2[2:3] = scale
    v2[3:4] = offset
    v2[4:8] = jnp.zeros((4, 2 * mid), F32)

    def second_act(i, c):
        m = wide(mk[i].reshape(cells, 128), mid // 128)
        acts = []
        for g in range(2):
            lanes = slice(g * mid, (g + 1) * mid)
            z = sp[i, :, :, lanes].reshape(cells, mid) * v2[2:3, lanes] + v2[3:4, lanes]
            acts.append(z * sigmoid(z) * m)
        pp[i, :, :, 0:mid] = (acts[0] - acts[1]).reshape(slots, cols, mid)
        pp[i, :, :, mid:] = acts[1].reshape(slots, cols, mid)
        pooled[pl.ds(i, 1)] = row_sum(fold(acts[0] + acts[1]))
        return c

    lax.fori_loop(0, images, second_act, 0, unroll=2)
    pooled[...] = pooled[...] / area[...]
    rbuf3[r] = mm(pooled[...], down[...].astype(F32), HIGH)
    copies = links.row_start(rbuf3, rsem3)

    def difference(i, c):
        pd[i] = pp[i, :, :, 0:mid].astype(BF16)
        return c

    lax.fori_loop(0, images, difference, 0, unroll=4)
    out_pd = pltpu.make_async_copy(pd, pd_hbm, osem.at[3])
    out_pd.start()
    pending.append(out_pd)
    squeeze = links.row_end(rbuf3, copies)
    ibuf3[links.i, 0:1] = row_sum(squeeze)
    ibuf3[links.i, 1:2] = row_sum(squeeze * squeeze)
    total = links.img_total(ibuf3, isem3)
    mean, factor, scale, offset = norm_terms(
        total[0:1], total[1:2], float(images * n_img), g_at[...], h_at[...]
    )
    v_at[0:1] = factor
    v_at[1:8] = jnp.zeros((7, v_at.shape[1]), F32)
    at_norm[...] = (squeeze - mean) * factor
    z = at_norm[...] * g_at[...] + h_at[...]
    at_out[...] = z
    attend = z * sigmoid(z)
    upf = up[...].astype(F32)
    lean = mm(attend, upf[:, :mid] - upf[:, mid:], HIGH) + (bias[:, :mid] - bias[:, mid:])
    w0[...] = sigmoid(lean)
    w1[...] = sigmoid(-lean)


    def mixing(i, c):
        v = w0[pl.ds(i, 1)] * pp[i, :, :, 0:mid].reshape(cells, mid)
        v = v + pp[i, :, :, mid:].reshape(cells, mid)
        mx[i] = v.astype(BF16).reshape(slots, cols, mid)
        return c

    lax.fori_loop(0, images, mixing, 0, unroll=2)
    v = mx[...].reshape(images * cells, mid)
    v = mm_tn(v, jnp.concatenate([v, jnp.ones((images * cells, 128), BF16)], axis=1))
    gram[...] = v[:, 0:mid]
    mixed_sum[...] = v[:, mid:]
    out_mx = pltpu.make_async_copy(mx, mx_hbm, osem.at[4])
    out_mx.start()
    pending.append(out_mx)
    out_xt.wait()
    pending = [c for c in pending if c is not out_xt]
    gw = xt.at[0:mid]
    gw[...] = mm_terms(mm, gram[...], we[...], 3)
    wef = we[...].astype(F32)
    rbuf4[r, 0:1] = row_sum(wide(mixed_sum[...], ch // 128) * wef)
    rbuf4[r, 1:2] = row_sum(gw[...] * wef)
    ibuf4[links.i] = links.row_total(rbuf4, rsem4)
    total = links.img_total(ibuf4, isem4)
    mean, factor, scale, offset = norm_terms(total[0:1], total[1:2], n, g3[...], h3[...])
    v3[0:1] = mean
    v3[1:2] = factor
    v3[2:3] = scale
    v3[3:4] = offset
    v3[4:5] = 0.5 * scale
    v3[5:6] = 0.5 * offset
    v3[6:8] = jnp.zeros((2, ch), F32)
    awe[...] = (wef * scale).astype(BF16)
    for k, (src, dst) in enumerate([(gw, gw_hbm), (awe, awe_hbm), (wt, wt_hbm)]):
        copy = pltpu.make_async_copy(src, dst, osem.at[6 + k])
        copy.start()
        pending.append(copy)

    for copy in pending:
        copy.wait()


def sd(shape, dtype=F32):
    return jax.ShapeDtypeStruct(shape, dtype)


def call_forward(n_img, n_row, args, images, slots, cols, ch, mid, inter):
    n = n_img * n_row
    cells = (images, slots, cols)
    outs = [
        (sd(cells + (mid,)), ANY),
        (sd((images, slots + 2, cols, 3 * mid), BF16), ANY),
        (sd(cells + (2 * mid,)), ANY),
        (sd(cells + (mid,), BF16), ANY),
        (sd(cells + (mid,), BF16), ANY),
        (sd(cells + (128,)), ANY),
        (sd((mid + 8, ch)), ANY),
        (sd((8, mid)), VMEM),
        (sd((8, 2 * mid)), VMEM),
        (sd((8, ch)), VMEM),
        (sd((8, inter)), VMEM),
        (sd((images, inter)), VMEM),
        (sd((images, inter)), VMEM),
        (sd((images, mid)), VMEM),
        (sd((images, mid)), VMEM),
        (sd((images, mid)), VMEM),
        (sd((images, mid)), VMEM),
        (sd((mid, ch)), ANY),
        (sd((mid, ch), BF16), ANY),
        (sd((2, 3 * mid, 3 * mid // 2), BF16), ANY),
        (sd((mid, 128)), VMEM),
    ]
    dma = pltpu.SemaphoreType.DMA
    scratch = [
        pltpu.VMEM(cells + (mid,), F32),
        pltpu.VMEM(cells + (2 * mid,), F32),
        pltpu.VMEM(cells + (2 * mid,), F32),
        pltpu.VMEM(cells + (mid,), BF16),
        pltpu.VMEM(cells + (mid,), BF16),
        pltpu.VMEM(cells + (128,), F32),
        pltpu.VMEM((mid + 8, ch), F32),
        pltpu.VMEM((images, slots, cols, ch), BF16),
        pltpu.VMEM((GROUP, slots + 2, cols, 3 * mid), BF16),
        pltpu.VMEM((GROUP, slots + 2, cols, 3 * mid), BF16),
        pltpu.VMEM(args[6].shape, BF16),
        pltpu.VMEM((mid, ch), BF16),
        pltpu.VMEM((mid, ch), BF16),
        pltpu.VMEM((2, 3 * mid, 3 * mid // 2), BF16),
        pltpu.VMEM((3, 8, mid), F32),
        pltpu.VMEM((2, 8, 2 * mid), F32),
        pltpu.VMEM((mid, mid), F32),
        pltpu.VMEM((images, cols, mid), F32),
        pltpu.VMEM((images, cols, mid), F32),
        pltpu.VMEM((images, cols, mid), F32),
        pltpu.VMEM((n, 4, mid), F32),
        pltpu.VMEM((n, 2, 2 * mid), F32),
        pltpu.VMEM((n_row, images, inter), F32),
        pltpu.VMEM((n_img, 2, inter), F32),
        pltpu.VMEM((n_row, 2, ch), F32),
        pltpu.VMEM((n_img, 2, ch), F32),
        dma((images // GROUP,)),
        dma((9,)),
        dma((2,)),
        dma((4,)),
        dma((2, n)),
        dma((2, n)),
        dma((2, n_row)),
        dma((2, n_img)),
        dma((2, n_row)),
        dma((2, n_img)),
    ]
    in_specs = [SMEM, SMEM, ANY] + [VMEM] * (len(args) - 3)
    for k in (6, 14):
        in_specs[k] = ANY
    return pl.pallas_call(
        functools.partial(forward_kernel, n_img, n_row),
        out_shape=[o for o, _ in outs],
        in_specs=in_specs,
        out_specs=[s for _, s in outs],
        scratch_shapes=scratch,
        name="forward",
        compiler_params=pltpu.CompilerParams(
            collective_id=0, has_side_effects=True, vmem_limit_bytes=62 * 1024 * 1024
        ),
    )(*args)


PART = 4


def third_kernel(counts, group, x, cot, mx, we, awe, v3, bo, sg, q, m_out, *parts):
    per, slots, cols, ch = x.shape
    mid = mx.shape[-1]
    cells = PART * slots * cols
    columns = lax.broadcasted_iota(jnp.int32, (cols, 128), 0)

    @pl.when(pl.program_id(0) == 0)
    def _():
        m_out[...] = jnp.zeros_like(m_out)

    def product(p):
        v = mx[p * PART : (p + 1) * PART].reshape(cells, mid)
        parts[p][...] = mm(v, we[...])

    product(0)
    for p in range(per // PART):
        if p + 1 < per // PART:
            product(p + 1)
        for k in range(PART):
            i = p * PART + k
            image = pl.program_id(0) * per + i
            inside = jnp.where(columns < 12 + 2 * group[image], 1.0, 0.0).astype(F32)
            for s in range(slots):
                held = jnp.where(s < counts[image], 1.0, 0.0).astype(F32)
                m = wide(inside * held, ch // 128)
                at = (k * slots + s) * cols
                half = parts[p][at : at + cols] * v3[4:5] + v3[5:6] + 0.5 * x[i, s].astype(F32)
                th = jnp.tanh(half)
                up = 1.0 + th
                act = half * up
                bo[i, s] = (act * m).astype(BF16)
                slope = up + act * (1.0 - th)
                sg[i, s] = (cot[i, s].astype(F32) * (0.5 * m) * slope).astype(BF16)
        v = sg[p * PART : (p + 1) * PART].reshape(cells, ch)
        q[p * PART : (p + 1) * PART] = mm_nt(v, awe[...]).reshape(PART, slots, cols, mid)
    v = sg[...].reshape(per * slots * cols, ch)
    m_out[0:mid] += mm_tn(mx[...].reshape(per * slots * cols, mid), v)
    m_out[mid : mid + 16] += mm(jnp.ones((16, per * slots * cols), BF16), v)


def call_third(counts, group, x, cot, mx, we, awe, v3):
    images, slots, cols, ch = x.shape
    mid = mx.shape[-1]
    per = 8

    def cells(c):
        return pl.BlockSpec((per, slots, cols, c), lambda b: (b, 0, 0, 0))

    def whole(a):
        return pl.BlockSpec(a.shape, lambda b: (0,) * a.ndim)

    return pl.pallas_call(
        third_kernel,
        out_shape=[
            sd(x.shape, BF16),
            sd(x.shape, BF16),
            sd((images, slots, cols, mid)),
            sd((mid + 16, ch)),
        ],
        grid=(images // per,),
        in_specs=[SMEM, SMEM, cells(ch), cells(ch), cells(mid), whole(we), whole(awe), whole(v3)],
        out_specs=[
            cells(ch),
            cells(ch),
            cells(mid),
            pl.BlockSpec((mid + 16, ch), lambda b: (0, 0)),
        ],
        scratch_shapes=[pltpu.VMEM((PART * slots * cols, ch), F32)] * (per // PART),
        name="third",
        compiler_params=pltpu.CompilerParams(vmem_limit_bytes=60 * 1024 * 1024),
    )(counts, group, x, cot, mx, we, awe, v3)


def backward_kernel(
    n_img,
    n_row,
    counts,
    q_hbm,
    fp_hbm,
    a3_hbm,
    sp_hbm,
    pd_hbm,
    mx_hbm,
    mk_hbm,
    xt_hbm,
    x_hbm,
    v1,
    v2,
    v3,
    v_at,
    at_norm,
    at_out,
    w0,
    w1,
    pooled,
    gw_hbm,
    mixed_sum,
    m_in,
    area,
    g_at,
    wt_hbm,
    down,
    up,
    we,
    awe,
    fg_hbm,
    expand_out,
    split_out,
    reduce_out,
    up_out,
    down_out,
    bias_out,
    b1,
    b2,
    b3,
    b_at,
    mg,
    pd,
    mx,
    mk,
    gw,
    wt,
    split_part,
    small_part,
    rows_all,
    edge,
    ret,
    acc1,
    acc2,
    mb,
    dpart,
    pgrad,
    ibuf5,
    rbuf5,
    rbuf6,
    ibuf6,
    buf7,
    buf8,
    lsem,
    a3sem,
    hsem,
    rsem5,
    isem5,
    rsem6,
    isem6,
    sem7,
    sem8,
    rsem9,
    *reducers,
):
    images, slots, cols, mid = q_hbm.shape
    ch = we.shape[1]
    inter = down.shape[1]
    half = mid // 2
    blocks = images // GROUP
    cells = slots * cols
    links = Links(n_img, n_row)
    r, me = links.r, links.all_me()
    links.greet()
    sizes = reducer_sizes(n_row, ch, mid, inter)
    count = Reducer.COUNT
    expand_red, split_red, reduce_red, small_red = [
        Reducer(links, rows, width, reducers[k * count : (k + 1) * count])
        for k, (rows, width, _) in enumerate(sizes)
    ]
    n = v1[4:5, 0:1]
    up_rows, down_rows = inter // n_row, mid // n_row
    prev_dev = (links.i, lax.rem(r + n_row - 1, n_row))
    next_dev = (links.i, lax.rem(r + 1, n_row))
    has_prev = r > 0
    has_next = r < n_row - 1
    to_prev = pltpu.make_async_remote_copy(
        src_ref=edge.at[0],
        dst_ref=ret.at[1],
        send_sem=hsem.at[0],
        recv_sem=hsem.at[1],
        device_id=prev_dev,
        device_id_type=MESH,
    )
    to_next = pltpu.make_async_remote_copy(
        src_ref=edge.at[1],
        dst_ref=ret.at[0],
        send_sem=hsem.at[2],
        recv_sem=hsem.at[3],
        device_id=next_dev,
        device_id_type=MESH,
    )

    def columns_back(t, lines):
        col = lax.rem(lax.broadcasted_iota(jnp.int32, (lines, half), 0), cols)
        left = jnp.where(col == cols - 1, 0.0, pltpu.roll(t[:, 0:half], lines - 1, 0))
        right = jnp.where(col == 0, 0.0, pltpu.roll(t[:, 2 * half : 3 * half], 1, 0))
        return left + t[:, half : 2 * half] + right

    def small_piece(p):
        return small_part[p]

    def to_second_grads(sp, ub):
        loads = [
            pltpu.make_async_copy(src, dst, lsem.at[k])
            for k, (src, dst) in enumerate(
                [(mx_hbm, mx), (q_hbm, mg), (pd_hbm, pd), (mk_hbm, mk), (sp_hbm, sp)]
            )
        ]
        load_gw = pltpu.make_async_copy(gw_hbm, gw, lsem.at[5])
        load_wt = pltpu.make_async_copy(wt_hbm, wt, lsem.at[6])
        load_gw.start()
        for load in loads:
            load.start()
        load_wt.start()
        pending = list(loads)

        mean3, factor3, scale3 = v3[0:1], v3[1:2], v3[2:3]
        wef = we[...].astype(F32)
        rbuf5[r, 0:1] = m_in[mid : mid + 1]
        rbuf5[r, 1:2] = factor3 * (row_sum(m_in[0:mid] * wef) - mean3 * m_in[mid : mid + 1])
        links.met()
        ibuf5[links.i] = links.row_total(rbuf5, rsem5)
        total = links.img_total(ibuf5, isem5)
        b3[...] = total
        slope3, offset3 = norm_back_terms(mean3, factor3, scale3, n, total[0:1], total[1:2])
        slope = factor3 * (total[1:2] / n)
        level = jnp.broadcast_to(total[0:1] / n - slope * mean3, (16, ch))
        lefts = []
        for v, terms in ((wef * slope, 2), (level, 3)):
            for _ in range(terms):
                lefts.append(v.astype(BF16))
                v = v - lefts[-1].astype(F32)
        v = mm_nt(jnp.concatenate(lefts, axis=0), awe[...])
        fix = v[0:mid] + v[mid : 2 * mid]
        ev = v[2 * mid : 2 * mid + 1] + v[2 * mid + 16 : 2 * mid + 17] + v[2 * mid + 32 : 2 * mid + 33]
        high = fix.astype(BF16)
        mb[0:mid] = high
        mb[mid:] = (fix - high.astype(F32)).astype(BF16)

        def expand_piece(p):
            rows = pl.ds(pl.multiple_of(p * (mid // n_row), mid // n_row), mid // n_row)
            return (
                m_in[rows] * scale3 - wide(mixed_sum[rows], ch // 128) * offset3 - gw[rows] * slope3
            )

        load_gw.wait()
        expand_red.begin(expand_piece)

        for load in loads[:4]:
            load.wait()
        del pending[:4]

        def mix_back(b, c):
            v = mx[pl.ds(b * GROUP, GROUP)].reshape(GROUP * cells, mid)
            v = mm(jnp.concatenate([v, v], axis=1), mb[...])
            for k in range(GROUP):
                i = b * GROUP + k
                m = wide(mk[i].reshape(cells, 128), mid // 128)
                w = mg[i].reshape(cells, mid) - v[k * cells : (k + 1) * cells] - m * ev
                mg[i] = w.reshape(slots, cols, mid)
                dpart[pl.ds(i, 1)] = row_sum(fold(w * pd[i].reshape(cells, mid).astype(F32)))
            return c

        lax.fori_loop(0, blocks, mix_back, 0)

        upf = up[...].astype(F32)
        lean = dpart[...] * w0[...] * w1[...]
        rbuf6[r] = mm_nt(lean, upf[:, :mid] - upf[:, mid:], HIGH)
        copies = links.row_start(rbuf6, rsem6)
        z = at_out[...]
        attend = z * sigmoid(z)
        up_part = mm_tn(attend, lean, HIGH)
        bias_part = row_sum(lean)
        loads[4].wait()
        del pending[0]

        def slopes(i, c):
            m = wide(mk[i].reshape(cells, 128), mid // 128)
            for g in range(2):
                lanes = slice(g * mid, (g + 1) * mid)
                v = sp[i, :, :, lanes].reshape(cells, mid) * v2[2:3, lanes] + v2[3:4, lanes]
                ub[i, :, :, lanes] = (swish_slope(v) * m).reshape(slots, cols, mid)
            return c

        lax.fori_loop(0, images * 2 // 5, slopes, 0, unroll=2)
        attend_grad = links.row_end(rbuf6, copies) * swish_slope(z)
        ibuf6[links.i, 0:1] = row_sum(attend_grad)
        ibuf6[links.i, 1:2] = row_sum(attend_grad * at_norm[...])
        links.img_start(ibuf6, isem6)
        lax.fori_loop(images * 2 // 5, images, slopes, 0, unroll=2)
        total = links.img_end(ibuf6, isem6)
        b_at[...] = total
        count = float(images * n_img)
        squeeze_grad = (
            g_at[...]
            * v_at[0:1]
            * (attend_grad - total[0:1] / count - at_norm[...] * (total[1:2] / count))
        )
        pgrad[...] = mm_nt(squeeze_grad, down[...].astype(F32), HIGH) / area[...]

        def with_second_grads(a3, geb):
            load_wt.wait()
            acc2[...] = jnp.zeros_like(acc2)

            def second_back(i, c):
                v = mg[i].reshape(cells, mid)
                for g, w in enumerate((w0, w1)):
                    lanes = slice(g * mid, (g + 1) * mid)
                    s = sp[i, :, :, lanes].reshape(cells, mid)
                    grad = v * w[pl.ds(i, 1)] + pgrad[pl.ds(i, 1)]
                    grad = grad * ub[i, :, :, lanes].reshape(cells, mid)
                    ub[i, :, :, lanes] = grad.reshape(slots, cols, mid)
                    acc2[0, :, lanes] += fold(grad)
                    acc2[1, :, lanes] += fold(grad * s)
                return c

            lax.fori_loop(0, images, second_back, 0, unroll=2)
            mean2, factor2, scale2 = v2[0:1], v2[1:2], v2[2:3]
            s0 = row_sum(acc2[0])
            buf7[me, 0:1] = s0
            buf7[me, 1:2] = factor2 * (row_sum(acc2[1]) - mean2 * s0)
            links.all_start(buf7, sem7)
            down_part = mm_tn(pooled[...], squeeze_grad, HIGH)
            for p in range(n_row):
                lines = down_part[p * down_rows : (p + 1) * down_rows]
                small_part[p, 0:up_rows] = up_part[p * up_rows : (p + 1) * up_rows]
                small_part[p, up_rows : up_rows + down_rows // 2] = jnp.concatenate(
                    [lines[: down_rows // 2], lines[down_rows // 2 :]], axis=1
                )
                small_part[p, up_rows + down_rows // 2 :] = jnp.broadcast_to(bias_part, (8, mid))

            small_red.begin(small_piece)
            total = links.all_wait(buf7, sem7)
            expand_red.second(expand_piece)
            b2[...] = total
            slope2, offset2 = norm_back_terms(mean2, factor2, scale2, n, total[0:1], total[1:2])

            def second_grad(grad, s, m):
                return (grad * scale2 - m * (offset2 + slope2 * s)).astype(BF16)

            for side, dy in ((0, 0), (1, 2)):

                def edge_rows(i, c):
                    at = 0 if side == 0 else jnp.maximum(counts[i] - 1, 0)
                    m = wide(mk[i, 0], 2 * mid // 128)
                    geb[i] = second_grad(ub[i, at], sp[i, at], m)
                    return c

                lax.fori_loop(0, images, edge_rows, 0, unroll=2)
                for g in range(2):
                    v = geb[:, :, g * mid : (g + 1) * mid].reshape(images * cols, mid)
                    t = mm(v, wt[g, dy * mid : (dy + 1) * mid])
                    edge[side, :, :, g * half : (g + 1) * half] = (
                        columns_back(t, images * cols).astype(BF16).reshape(images, cols, half)
                    )
                if side == 0:

                    @pl.when(has_prev)
                    def _():
                        to_prev.start()

                else:

                    @pl.when(has_next)
                    def _():
                        to_next.start()

            @pl.when(jnp.logical_not(has_prev))
            def _():
                ret[0] = jnp.zeros(ret.shape[1:], BF16)

            @pl.when(jnp.logical_not(has_next))
            def _():
                ret[1] = jnp.zeros(ret.shape[1:], BF16)

            def a3_copy(b, slot):
                return pltpu.make_async_copy(
                    a3_hbm.at[pl.ds(b * GROUP, GROUP)], a3.at[slot], a3sem.at[slot]
                )

            a3_copy(0, 0).start()
            split_part[...] = jnp.zeros_like(split_part)

            def split_grads(b, c):
                slot = lax.rem(b, 2)

                @pl.when(b + 1 < blocks)
                def _():
                    a3_copy(b + 1, 1 - slot).start()

                @pl.when(b == 2)
                def _():
                    small_red.second(small_piece)

                @pl.when(b == 1)
                def _():
                    expand_red.third()

                @pl.when(b == 5)
                def _():
                    expand_red.fourth()

                @pl.when(b == 6)
                def _():
                    small_red.third()

                def one(k, c):
                    i = b * GROUP + k
                    m = wide(mk[i].reshape(cells, 128), 2 * mid // 128)
                    v = second_grad(ub[i].reshape(cells, 2 * mid), sp[i].reshape(cells, 2 * mid), m)
                    mx[i] = v[:, 0:mid].reshape(slots, cols, mid)
                    pd[i] = v[:, mid:].reshape(slots, cols, mid)
                    return c

                lax.fori_loop(0, GROUP, one, 0)
                a3_copy(b, slot).wait()
                for g, grads in enumerate((mx, pd)):
                    v = grads[pl.ds(b * GROUP, GROUP)].reshape(GROUP * cells, mid)
                    taps = jnp.concatenate(
                        [
                            a3[slot, :, dy : dy + slots, :, g * 3 * half : (g + 1) * 3 * half].reshape(
                                GROUP * cells, 3 * half
                            )
                            for dy in range(3)
                        ],
                        axis=1,
                    )
                    split_part[g] += mm_tn(v, taps)
                return c

            lax.fori_loop(0, blocks, split_grads, 0)

        pl.run_scoped(
            with_second_grads,
            pltpu.VMEM((2, GROUP, slots + 2, cols, 3 * mid), BF16),
            pltpu.VMEM((images, cols, 2 * mid), BF16),
        )

    pl.run_scoped(
        to_second_grads,
        pltpu.VMEM((images, slots, cols, 2 * mid), F32),
        pltpu.VMEM((images, slots, cols, 2 * mid), F32),
    )

    def to_inputs(fp, xs, xt, xu, split_rows):
        loads = [
            pltpu.make_async_copy(fp_hbm, fp, lsem.at[5]),
            pltpu.make_async_copy(xt_hbm, xt, lsem.at[6]),
            pltpu.make_async_copy(x_hbm, xs, lsem.at[4]),
        ]
        for load in loads:
            load.start()

        def split_piece(p):
            lines = []
            for tap in range(9):
                at = pl.multiple_of(tap * half + p * (half // n_row), half // n_row)
                lines.append(split_rows[pl.ds(at, half // n_row)])
            return jnp.concatenate(lines, axis=0).astype(F32)

        for g in range(2):
            for tap in range(9):
                split_rows[tap * half : (tap + 1) * half, g * mid : (g + 1) * mid] = jnp.transpose(
                    split_part[g, :, tap * half : (tap + 1) * half].astype(BF16)
                )
        split_red.begin(split_piece)
        @pl.when(has_prev)
        def _():
            to_prev.wait_send()
            to_next.wait_recv()

        @pl.when(has_next)
        def _():
            to_next.wait_send()
            to_prev.wait_recv()

        loads[0].wait()
        acc1[...] = jnp.zeros_like(acc1)

        def conv_back(b, c):
            @pl.when(b == 1)
            def _():
                split_red.second(split_piece)

            @pl.when(b == 3)
            def _():
                small_red.fourth()

            @pl.when(b == 5)
            def _():
                split_red.third()

            blank = jnp.zeros((GROUP, 1, cols, mid), BF16)
            for g, grads in enumerate((mx, pd)):
                v = grads[pl.ds(b * GROUP, GROUP)]
                moved = (
                    jnp.concatenate([v[:, 1:], blank], axis=1),
                    v,
                    jnp.concatenate([blank, v[:, : slots - 1]], axis=1),
                )
                v = jnp.concatenate(
                    [moved[dy].reshape(GROUP * cells, mid) for dy in range(3)], axis=1
                )
                value = mm(v, wt[g])
                back = columns_back(value, GROUP * cells)
                lanes = slice(g * half, (g + 1) * half)
                for k in range(GROUP):
                    i = b * GROUP + k
                    m = mk[i].reshape(cells, 128)
                    low = ret[1, i, :, lanes].astype(F32)
                    parts = []
                    for s in range(slots):
                        at = k * cells + s * cols
                        here = back[at : at + cols] + low * jnp.where(counts[i] - 1 == s, 1.0, 0.0).astype(F32)
                        if s == 0:
                            here = here + ret[0, i, :, lanes].astype(F32)
                        parts.append(here)
                    v = fp[i, :, :, lanes].reshape(cells, half)
                    z = v * v1[2:3, lanes] + v1[3:4, lanes]
                    grad = jnp.concatenate(parts, axis=0) * swish_slope(z) * wide(m, half // 128)
                    mg[i, :, :, lanes] = grad.reshape(slots, cols, half)
                    acc1[0, :, lanes] += fold(grad)
                    acc1[1, :, lanes] += fold(grad * v)
            return c

        lax.fori_loop(0, blocks, conv_back, 0)
        expand_out[...] = expand_red.end()
        rows_all[r] = small_red.end()
        rows_copies = links.row_copies(rows_all, rsem9)
        s0 = row_sum(acc1[0])
        buf8[me, 0:1] = s0
        buf8[me, 1:2] = v1[1:2] * (row_sum(acc1[1]) - v1[0:1] * s0)
        links.all_start(buf8, sem8)

        def narrow(i, c):
            pd[i] = mg[i].astype(BF16)
            return c

        lax.fori_loop(0, images, narrow, 0, unroll=4)
        loads[2].wait()
        lines = images * cells
        width = ch // 2
        for k in range(2):
            xu[:, k * width : (k + 1) * width] = mm_tn(
                pd[...].reshape(lines, mid), xs[:, :, :, k * width : (k + 1) * width].reshape(lines, width)
            )
        loads[1].wait()
        total = links.all_wait(buf8, sem8)
        b1[...] = total
        slope1, offset1 = norm_back_terms(v1[0:1], v1[1:2], v1[2:3], n, total[0:1], total[1:2])

        def column(v):
            return wide(jnp.transpose(jnp.broadcast_to(v, (128, mid))), ch // n_row // 128)

        scale_c, slope_c, offset_c = column(v1[2:3]), column(slope1), column(offset1)

        def reduce_piece(p):
            lanes = pl.ds(pl.multiple_of(p * (ch // n_row), ch // n_row), ch // n_row)
            v = xu[:, lanes] * scale_c - xt[mid : mid + 1, lanes] * offset_c - xt[0:mid, lanes] * slope_c
            return jnp.transpose(v.astype(BF16)).astype(F32)

        reduce_red.begin(reduce_piece)
        for copy in rows_copies:
            copy.start()
        split_red.fourth()

        def first_grad(i, c):
            m = wide(mk[i].reshape(cells, 128), mid // 128)
            v = mg[i].reshape(cells, mid) * v1[2:3] - m * (
                offset1 + slope1 * fp[i].reshape(cells, mid)
            )
            mx[i] = v.astype(BF16).reshape(slots, cols, mid)
            return c

        lax.fori_loop(0, images // 2, first_grad, 0)
        reduce_red.second(reduce_piece)
        lax.fori_loop(images // 2, images, first_grad, 0)
        out_fg = pltpu.make_async_copy(mx, fg_hbm, lsem.at[7])
        out_fg.start()
        reduce_red.third()
        split_out[...] = split_red.end()
        for copy in rows_copies:
            copy.wait()
        for p in range(n_row):
            up_out[p * up_rows : (p + 1) * up_rows] = rows_all[p, 0:up_rows]
            lines = rows_all[p, up_rows : up_rows + down_rows // 2]
            down_out[p * down_rows : (p + 1) * down_rows] = jnp.concatenate(
                [lines[:, 0:inter], lines[:, inter:]], axis=0
            )
        bias_out[...] = rows_all[0, up_rows + down_rows // 2 :]
        reduce_red.fourth()
        reduce_out[...] = reduce_red.end()
        out_fg.wait()

    pl.run_scoped(
        to_inputs,
        pltpu.VMEM((images, slots, cols, mid), F32),
        pltpu.VMEM((images, slots, cols, ch), BF16),
        pltpu.VMEM((mid + 8, ch), F32),
        pltpu.VMEM((mid, ch), F32),
        pltpu.VMEM((9 * half, 2 * mid), BF16),
    )


def reducer_sizes(n_row, ch, mid, inter):
    return [
        (mid // n_row, ch, BF16),
        (9 * (mid // 2) // n_row, 2 * mid, BF16),
        (ch // n_row, mid, BF16),
        (inter // n_row + mid // n_row // 2 + 8, mid, F32),
    ]


def call_backward(n_img, n_row, args, gw, wt, ch, inter):
    q = args[1]
    images, slots, cols, mid = q.shape
    half = mid // 2
    n = n_img * n_row
    cells = (images, slots, cols)
    sizes = reducer_sizes(n_row, ch, mid, inter)
    outs = [
        (sd(cells + (mid,), BF16), ANY),
        (sd((mid // n_row, ch)), VMEM),
        (sd((9 * half // n_row, 2 * mid)), VMEM),
        (sd((ch // n_row, mid)), VMEM),
        (sd((inter, mid)), VMEM),
        (sd((mid, inter)), VMEM),
        (sd((8, mid)), VMEM),
        (sd((2, mid)), VMEM),
        (sd((2, 2 * mid)), VMEM),
        (sd((2, ch)), VMEM),
        (sd((2, inter)), VMEM),
    ]
    dma = pltpu.SemaphoreType.DMA
    scratch = [
        pltpu.VMEM(cells + (mid,), F32),
        pltpu.VMEM(cells + (mid,), BF16),
        pltpu.VMEM(cells + (mid,), BF16),
        pltpu.VMEM(cells + (128,), F32),
        pltpu.VMEM((mid, ch), F32),
        pltpu.VMEM((2, 3 * mid, 3 * half), BF16),
        pltpu.VMEM((2, mid, 9 * half), F32),
        pltpu.VMEM((n_row, sizes[3][0], mid), F32),
        pltpu.VMEM((n_row, sizes[3][0], mid), F32),
        pltpu.VMEM((2, images, cols, mid), BF16),
        pltpu.VMEM((2, images, cols, mid), BF16),
        pltpu.VMEM((2, 8, mid), F32),
        pltpu.VMEM((2, 8, 2 * mid), F32),
        pltpu.VMEM((2 * mid, mid), BF16),
        pltpu.VMEM((images, mid), F32),
        pltpu.VMEM((images, mid), F32),
        pltpu.VMEM((n_img, 2, ch), F32),
        pltpu.VMEM((n_row, 2, ch), F32),
        pltpu.VMEM((n_row, images, inter), F32),
        pltpu.VMEM((n_img, 2, inter), F32),
        pltpu.VMEM((n, 2, 2 * mid), F32),
        pltpu.VMEM((n, 2, mid), F32),
        dma((8,)),
        dma((2,)),
        dma((4,)),
        dma((2, n_row)),
        dma((2, n_img)),
        dma((2, n_row)),
        dma((2, n_img)),
        dma((2, n)),
        dma((2, n)),
        dma((2, n_row)),
    ]
    for rows, width, dtype in sizes:
        scratch += Reducer.scratch(n_img, rows, width, dtype)
    in_specs = [SMEM] + [ANY] * 9 + [VMEM] * (len(args) - 10)
    for k, a in enumerate(args):
        if a is gw or a is wt:
            in_specs[k] = ANY
    return pl.pallas_call(
        functools.partial(backward_kernel, n_img, n_row),
        out_shape=[o for o, _ in outs],
        in_specs=in_specs,
        out_specs=[s for _, s in outs],
        scratch_shapes=scratch,
        name="backward",
        compiler_params=pltpu.CompilerParams(
            collective_id=1, has_side_effects=True, vmem_limit_bytes=62 * 1024 * 1024
        ),
    )(*args)


def input_kernel(
    fg, sg, wr, expand, split, reduce, up, down, bias, b1, b2, b3, b_at,
    gi, expand_out, split_out, reduce_out, up_out, down_out, bias_out, *lines,
):
    per, slots, cols, ch = sg.shape
    cells = per * slots * cols
    mid = fg.shape[-1]
    value = mm_nt(fg[...].reshape(cells, mid), wr[...])
    gi[...] = (value + sg[...].reshape(cells, ch).astype(F32)).astype(BF16).reshape(gi.shape)

    @pl.when(pl.program_id(0) == 0)
    def _():
        expand_out[...] = expand[...]
        split_out[...] = split[...]
        reduce_out[...] = reduce[...]
        down_out[...] = down[...]
        up_out[:, 0:mid] = up[...]
        up_out[:, mid:] = -up[...]
        bias_out[:, 0:mid] = bias[0:1]
        bias_out[:, mid:] = -bias[0:1]
        for k, v in enumerate((b1, b2, b_at, b3)):
            lines[2 * k][...] = v[1:2]
            lines[2 * k + 1][...] = v[0:1]


def call_input(fg, sg, wr, *small):
    images, slots, cols, ch = sg.shape
    mid = fg.shape[-1]
    expand, split, reduce, up, down, _, b1, b2, b3, b_at = small
    per = 14

    def cells(c):
        return pl.BlockSpec((per, slots, cols, c), lambda b: (b, 0, 0, 0))

    def whole(a):
        return pl.BlockSpec(a.shape, lambda b: (0,) * len(a.shape))

    outs = [sd(a.shape) for a in (expand, split, reduce)]
    outs += [sd((up.shape[0], 2 * mid)), sd(down.shape), sd((1, 2 * mid))]
    for v in (b1, b2, b_at, b3):
        outs += [sd((1, v.shape[1]))] * 2
    return pl.pallas_call(
        input_kernel,
        out_shape=[sd(sg.shape, BF16)] + outs,
        grid=(images // per,),
        in_specs=[cells(mid), cells(ch), whole(wr)] + [whole(a) for a in small],
        out_specs=[cells(ch)] + [whole(a) for a in outs],
        name="input_grad",
        compiler_params=pltpu.CompilerParams(vmem_limit_bytes=60 * 1024 * 1024),
    )(fg, sg, wr, *small)


def body(
    n_img,
    n_row,
    feature_map,
    image_group,
    row_counts,
    reduce_weight,
    gain_first,
    shift_first,
    split_weight,
    gain_second,
    shift_second,
    attn_down,
    gain_attend,
    shift_attend,
    attn_up,
    attn_bias,
    expand_weight,
    gain_third,
    shift_third,
    cotangent,
):
    images, slots, cols, ch = feature_map.shape
    mid = reduce_weight.shape[1]
    inter = attn_down.shape[1]
    half = mid // 2
    counts = row_counts[:, 0]
    ws = split_weight.reshape(3, 3 * half, 2 * mid)

    def line(v):
        return v[None, :]

    (
        fp, a3, sp, pd, mx, mk, xt, v1, v2, v3, v_at, at_norm, at_out, w0, w1, pooled, area,
        gw, awe, wt, mixed_sum,
    ) = call_forward(
        n_img,
        n_row,
        (
            counts,
            image_group,
            feature_map,
            reduce_weight,
            line(gain_first),
            line(shift_first),
            ws,
            line(gain_second),
            line(shift_second),
            attn_down,
            line(gain_attend),
            line(shift_attend),
            attn_up,
            line(attn_bias),
            expand_weight,
            line(gain_third),
            line(shift_third),
        ),
        images, slots, cols, ch, mid, inter,
    )
    block_out, sg, q, m_sum = call_third(
        counts, image_group, feature_map, cotangent, mx, expand_weight, awe, v3
    )
    (
        fg, grad_expand, grad_split, grad_reduce, grad_up, grad_down, bias, b1, b2, b3, b_at,
    ) = call_backward(
        n_img,
        n_row,
        (
            counts, q, fp, a3, sp, pd, mx, mk, xt, feature_map, v1, v2, v3, v_at, at_norm, at_out, w0, w1, pooled,
            gw, mixed_sum, m_sum, area, line(gain_attend), wt, attn_down, attn_up, expand_weight,
            awe,
        ),
        gw, wt, ch, inter,
    )
    small = call_input(
        fg, sg, reduce_weight, grad_expand, grad_split, grad_reduce, grad_up, grad_down, bias,
        b1, b2, b3, b_at,
    )
    grad_input, grad_expand, grad_split, grad_reduce, grad_up, grad_down = small[:6]
    return (
        block_out,
        grad_input,
        grad_reduce,
        grad_split.reshape(3, 3, half // n_row, 2 * mid),
        grad_expand,
        grad_down,
        grad_up,
    ) + tuple(v.reshape(-1) for v in small[6:])


def solution(mesh):
    cells = P("img", "row", None, None)
    in_specs = (cells, P("img"), P("img", "row")) + (P(),) * 14 + (cells,)
    out_specs = (cells, cells, P("row", None), P(None, None, "row", None), P("row", None)) + (P(),) * 11
    return jax.shard_map(
        functools.partial(body, mesh.shape["img"], mesh.shape["row"]),
        mesh=mesh,
        in_specs=in_specs,
        out_specs=out_specs,
        check_vma=False,
    )
```

```python
import functools

import jax
import jax.numpy as jnp
from jax import lax
from jax.experimental import pallas as pl
from jax.experimental.pallas import tpu as pltpu
from jax.sharding import PartitionSpec as P

MESH = pl.DeviceIdType.MESH
HIGH = lax.Precision.HIGHEST
F32 = jnp.float32
BF16 = jnp.bfloat16
EPS = 1e-05
GROUP = 8
ANY = pl.BlockSpec(memory_space=pl.ANY)
VMEM = pl.BlockSpec(memory_space=pltpu.VMEM)
SMEM = pl.BlockSpec(memory_space=pltpu.SMEM)


def dot(a, b, dims, precision=None):
    return lax.dot_general(
        a, b, (dims, ((), ())), preferred_element_type=F32, precision=precision
    )


def mm(a, b, precision=None):
    return dot(a, b, ((1,), (0,)), precision)


def mm_nt(a, b, precision=None):
    return dot(a, b, ((1,), (1,)), precision)


def mm_tn(a, b, precision=None):
    return dot(a, b, ((0,), (0,)), precision)


def mm_terms(product, a, b, terms):
    total = None
    for _ in range(terms):
        part = a.astype(BF16)
        a = a - part.astype(F32)
        value = product(part, b)
        total = value if total is None else total + value
    return total


def sigmoid(v):
    return 0.5 * jnp.tanh(0.5 * v) + 0.5


def swish_slope(v):
    s = sigmoid(v)
    return s * (1.0 + v * (1.0 - s))


def wide(mask, times):
    return jnp.concatenate([mask] * times, axis=1)


def fold(v):
    return jnp.sum(v.reshape(v.shape[0] // 8, 8, v.shape[1]), axis=0)


def row_sum(v):
    return jnp.sum(v, axis=0, keepdims=True)


class Links:
    def __init__(self, n_img, n_row):
        self.ni, self.nr = n_img, n_row
        self.i, self.r = lax.axis_index("img"), lax.axis_index("row")

    def greet(self):
        bar = pltpu.get_barrier_semaphore()

        def go(k, c):
            pl.semaphore_signal(
                bar, inc=1, device_id=self.peer(k), device_id_type=MESH
            )
            return c

        lax.fori_loop(1, self.ni * self.nr, go, 0)

    def met(self):
        pl.semaphore_wait(pltpu.get_barrier_semaphore(), self.ni * self.nr - 1)

    def peer(self, k):
        return (lax.rem(self.i + k // self.nr, self.ni), lax.rem(self.r + k % self.nr, self.nr))

    def copy(self, buf, send, recv, me, k, target):
        return pltpu.make_async_remote_copy(
            src_ref=buf.at[me],
            dst_ref=buf.at[me],
            send_sem=send.at[k],
            recv_sem=recv.at[k],
            device_id=target,
            device_id_type=MESH,
        )

    def all_me(self):
        return self.i * self.nr + self.r

    def all_start(self, buf, sems):
        def go(k, c):
            self.copy(buf, sems.at[0], sems.at[1], self.all_me(), k, self.peer(k)).start()
            return c

        lax.fori_loop(1, self.ni * self.nr, go, 0)

    def all_wait(self, buf, sems):
        def go(k, c):
            self.copy(buf, sems.at[0], sems.at[1], self.all_me(), k, self.peer(k)).wait()
            return c

        lax.fori_loop(1, self.ni * self.nr, go, 0)
        return jnp.sum(buf[...], axis=0)

    def row_copies(self, buf, sems):
        return [
            self.copy(buf, sems.at[0], sems.at[1], self.r, k, (self.i, lax.rem(self.r + k, self.nr)))
            for k in range(1, self.nr)
        ]

    def img_copy(self, buf, sems, k):
        return self.copy(
            buf, sems.at[0], sems.at[1], self.i, k, (lax.rem(self.i + k, self.ni), self.r)
        )

    def row_start(self, buf, sems):
        copies = self.row_copies(buf, sems)
        for c in copies:
            c.start()
        return copies

    def row_end(self, buf, copies):
        for c in copies:
            c.wait()
        return jnp.sum(buf[...], axis=0)

    def row_total(self, buf, sems):
        return self.row_end(buf, self.row_start(buf, sems))

    def img_start(self, buf, sems):
        def go(k, c):
            self.img_copy(buf, sems, k).start()
            return c

        lax.fori_loop(1, self.ni, go, 0)

    def img_end(self, buf, sems):
        def end(k, c):
            self.img_copy(buf, sems, k).wait()
            return c

        lax.fori_loop(1, self.ni, end, 0)
        return jnp.sum(buf[...], axis=0)

    def img_total(self, buf, sems):
        self.img_start(buf, sems)
        return self.img_end(buf, sems)


class Reducer:
    @staticmethod
    def layout(n_img, rows, width, dtype):
        lane_parts = min(width // 128, n_img)
        row_parts = n_img // lane_parts
        tile = 16 if dtype == BF16 else 8
        share = -(-rows // (row_parts * tile)) * tile
        return lane_parts, share, share * row_parts

    @staticmethod
    def scratch(n_img, rows, width, dtype):
        lane_parts, share, padded = Reducer.layout(n_img, rows, width, dtype)
        lanes = width // lane_parts
        return [
            pltpu.VMEM((2, padded, width), dtype),
            pltpu.VMEM((2, padded, width), dtype),
            pltpu.VMEM((padded, width), dtype),
            pltpu.VMEM((padded, width), dtype),
            pltpu.VMEM((padded, width), F32),
            pltpu.VMEM((n_img, share, lanes), dtype),
            pltpu.VMEM((padded, width), dtype),
            pltpu.SemaphoreType.DMA((2, 2 + 2 * n_img)),
        ]

    COUNT = 8

    def __init__(self, links, rows, width, refs):
        self.links, self.rows, self.width = links, rows, width
        (self.sb1, self.rb1, self.sb2, self.rb2, self.mine, self.rb3, self.ag, self.sems) = refs
        self.dtype = self.sb1.dtype
        self.lane_parts, self.share, self.padded = Reducer.layout(links.ni, rows, width, self.dtype)
        self.lanes = width // self.lane_parts
        r = links.r
        self.one = r + 1 - 2 * lax.rem(r, 2)
        self.two = lax.rem(r + 2, 4)

    def copy(self, src, dst, k, target):
        return pltpu.make_async_remote_copy(
            src_ref=src,
            dst_ref=dst,
            send_sem=self.sems.at[0, k],
            recv_sem=self.sems.at[1, k],
            device_id=target,
            device_id_type=MESH,
        )

    def copy1(self):
        return self.copy(self.sb1, self.rb1, 0, (self.links.i, self.one))

    def copy2(self):
        return self.copy(self.sb2, self.rb2, 1, (self.links.i, self.two))

    def part(self, ref, j):
        row = pl.multiple_of((j // self.lane_parts) * self.share, self.share)
        lane = pl.multiple_of(lax.rem(j, self.lane_parts) * self.lanes, self.lanes)
        return ref.at[pl.ds(row, self.share), pl.ds(lane, self.lanes)]

    def peer(self, k):
        return lax.rem(self.links.i + k, self.links.ni)

    def copy3(self, k):
        return self.copy(
            self.part(self.sb2, self.peer(k)), self.rb3.at[self.links.i], 2 + k, (self.peer(k), self.links.r)
        )

    def copy4(self, k):
        mine = self.part(self.ag, self.links.i)
        return self.copy(mine, mine, 2 + self.links.ni + k, (self.peer(k), self.links.r))

    def each(self, make, act):
        def go(k, c):
            act(make(k))
            return c

        lax.fori_loop(1, self.links.ni, go, 0)

    def begin(self, piece):
        odd = 1 - lax.rem(self.links.r, 2)
        for k in range(2):
            self.sb1[k, 0 : self.rows] = piece(odd + 2 * k).astype(self.dtype)
        self.copy1().start()

    def second(self, piece):
        self.copy1().wait()
        r = self.links.r
        kept = self.rb1[self.two // 2, 0 : self.rows].astype(F32)
        self.sb2[0 : self.rows] = (piece(self.two) + kept).astype(self.dtype)
        self.copy2().start()
        self.mine[0 : self.rows] = piece(r) + self.rb1[r // 2, 0 : self.rows].astype(F32)

    def third(self):
        self.copy2().wait()
        total = self.mine[0 : self.rows] + self.rb2[0 : self.rows].astype(F32)
        self.mine[0 : self.rows] = total
        self.sb2[0 : self.rows] = total.astype(self.dtype)
        self.each(self.copy3, lambda c: c.start())

    def fourth(self):
        self.each(self.copy3, lambda c: c.wait())
        total = self.part(self.mine, self.links.i)[...]
        for k in range(1, self.links.ni):
            total = total + self.rb3[self.peer(k)].astype(F32)
        self.part(self.ag, self.links.i)[...] = total.astype(self.dtype)
        self.each(self.copy4, lambda c: c.start())

    def end(self):
        self.each(self.copy4, lambda c: c.wait())
        return self.ag[0 : self.rows].astype(F32)


def norm_terms(total, square, count, gain, shift):
    mean = total / count
    factor = lax.rsqrt(square / count - mean * mean + EPS)
    scale = gain * factor
    return mean, factor, scale, shift - mean * scale


def norm_back_terms(mean, factor, scale, count, s0, s1):
    slope = scale * factor * (s1 / count)
    return slope, scale * (s0 / count) - slope * mean


def forward_kernel(
    n_img,
    n_row,
    counts,
    group,
    x_hbm,
    wr,
    g1,
    h1,
    ws_hbm,
    g2,
    h2,
    down,
    g_at,
    h_at,
    up,
    bias,
    we_hbm,
    g3,
    h3,
    fp_hbm,
    a3_hbm,
    sp_hbm,
    pd_hbm,
    mx_hbm,
    mk_hbm,
    xt_hbm,
    v1,
    v2,
    v3,
    v_at,
    at_norm,
    at_out,
    w0,
    w1,
    pooled,
    area,
    gw_hbm,
    awe_hbm,
    wt_hbm,
    mixed_sum,
    fp,
    sp,
    pp,
    pd,
    mx,
    mk,
    xt,
    xs,
    a3,
    a3b,
    ws,
    we,
    awe,
    wt,
    acc1,
    acc2,
    gram,
    bottom,
    above,
    below,
    buf1,
    buf2,
    rbuf3,
    ibuf3,
    rbuf4,
    ibuf4,
    xsem,
    osem,
    a3sem,
    hsem,
    sem1,
    sem2,
    rsem3,
    isem3,
    rsem4,
    isem4,
):
    images, slots, cols, ch = x_hbm.shape
    mid = wr.shape[1]
    half = mid // 2
    blocks = images // GROUP
    cells = slots * cols
    links = Links(n_img, n_row)
    r = links.r
    links.greet()

    def x_copy(b):
        at = pl.ds(b * GROUP, GROUP)
        return pltpu.make_async_copy(x_hbm.at[at], xs.at[at], xsem.at[b])

    def x_start(b, c):
        x_copy(b).start()
        return c

    lax.fori_loop(0, blocks, x_start, 0)
    pending = []
    in_ws = pltpu.make_async_copy(ws_hbm, ws, osem.at[6])
    in_we = pltpu.make_async_copy(we_hbm, we, osem.at[7])

    def masks(i, c):
        count, height = counts[i], 12 + 2 * group[i]
        area[pl.ds(i, 1)] = jnp.full((1, mid), 1, F32) * (height * height).astype(F32)
        rows = lax.broadcasted_iota(jnp.int32, (slots, cols, 128), 0)
        columns = lax.broadcasted_iota(jnp.int32, (slots, cols, 128), 1)
        mk[i] = jnp.where((rows < count) & (columns < height), 1.0, 0.0).astype(F32)
        return c

    lax.fori_loop(0, images, masks, 0, unroll=4)
    acc1[...] = jnp.zeros_like(acc1)
    lines = GROUP * cells

    def first(b, c):
        x_copy(b).wait()
        at = pl.ds(b * GROUP, GROUP)
        v = mm(xs[at].reshape(lines, ch), wr[...])
        fp[at] = v.reshape(GROUP, slots, cols, mid)
        m = mk[at].reshape(lines, 128)
        w = v * wide(m, mid // 128)
        mx[at] = w.astype(BF16).reshape(GROUP, slots, cols, mid)
        pd[at, :, :, 0:128] = mk[at].astype(BF16)
        acc1[0] += fold(w)
        acc1[1] += fold(w * v)
        acc1[2, :, 0:128] += fold(m)
        for k in range(GROUP):
            i = b * GROUP + k
            bottom[i] = fp[i, jnp.maximum(counts[i] - 1, 0)]
        return c

    lax.fori_loop(0, blocks, first, 0)
    in_ws.start()
    in_we.start()
    pending += [in_ws, in_we]
    out_mk = pltpu.make_async_copy(mk, mk_hbm, osem.at[1])
    out_mk.start()
    pending.append(out_mk)
    out_fp = pltpu.make_async_copy(fp, fp_hbm, osem.at[0])
    out_fp.start()
    pending.append(out_fp)

    me = links.all_me()
    buf1[me, 0:1] = row_sum(acc1[0])
    buf1[me, 1:2] = row_sum(acc1[1])
    n_here = row_sum(acc1[2, :, 0:128])
    buf1[me, 2:3] = wide(n_here, mid // 128)
    buf1[me, 3:4] = jnp.zeros((1, mid), F32)

    prev_dev = (links.i, lax.rem(r + n_row - 1, n_row))
    next_dev = (links.i, lax.rem(r + 1, n_row))
    to_prev = pltpu.make_async_remote_copy(
        src_ref=fp.at[:, 0],
        dst_ref=below,
        send_sem=hsem.at[0],
        recv_sem=hsem.at[1],
        device_id=prev_dev,
        device_id_type=MESH,
    )
    to_next = pltpu.make_async_remote_copy(
        src_ref=bottom,
        dst_ref=above,
        send_sem=hsem.at[2],
        recv_sem=hsem.at[3],
        device_id=next_dev,
        device_id_type=MESH,
    )
    has_prev = r > 0
    has_next = r < n_row - 1

    links.met()
    links.all_start(buf1, sem1)

    @pl.when(has_prev)
    def _():
        to_prev.start()

    @pl.when(has_next)
    def _():
        to_next.start()

    @pl.when(jnp.logical_not(has_prev))
    def _():
        above[...] = jnp.zeros_like(above)

    @pl.when(jnp.logical_not(has_next))
    def _():
        below[...] = jnp.zeros_like(below)

    v = jnp.concatenate(
        [mx[...].reshape(images * cells, mid), pd[:, :, :, 0:128].reshape(images * cells, 128)], axis=1
    )
    width = ch // 2
    for k in range(2):
        xt[:, k * width : (k + 1) * width] = mm_tn(
            v, xs[:, :, :, k * width : (k + 1) * width].reshape(images * cells, width)
        )[0 : mid + 8]
    out_xt = pltpu.make_async_copy(xt, xt_hbm, osem.at[5])
    out_xt.start()
    pending.append(out_xt)
    total = links.all_wait(buf1, sem1)
    n = total[2:3, 0:1]
    mean, factor, scale, offset = norm_terms(total[0:1], total[1:2], n, g1[...], h1[...])
    v1[0:1] = mean
    v1[1:2] = factor
    v1[2:3] = scale
    v1[3:4] = offset
    v1[4:5] = total[2:3]
    v1[5:8] = jnp.zeros((3, mid), F32)

    @pl.when(has_prev)
    def _():
        to_prev.wait_send()
        to_next.wait_recv()

    @pl.when(has_next)
    def _():
        to_next.wait_send()
        to_prev.wait_recv()

    prev_flag = has_prev.astype(F32)
    next_flag = has_next.astype(F32)
    ext = (slots + 2) * cols
    col_index = lax.rem(lax.broadcasted_iota(jnp.int32, (ext, mid), 0), cols)
    acc2[...] = jnp.zeros_like(acc2)

    in_ws.wait()
    in_we.wait()
    del pending[:2]
    buffers = (a3, a3b)

    def a3_copy(b, slot):
        return pltpu.make_async_copy(
            buffers[slot], a3_hbm.at[pl.ds(b * GROUP, GROUP)], a3sem.at[slot]
        )

    def spread(b, slot):
        for k in range(GROUP):
            i = b * GROUP + k
            m = mk[i].reshape(cells, 128)
            cm = wide(m[0:cols], mid // 128)
            z = fp[i].reshape(cells, mid) * v1[2:3] + v1[3:4]
            own = z * sigmoid(z) * wide(m, mid // 128)
            z = above[i] * v1[2:3] + v1[3:4]
            top = z * sigmoid(z) * (cm * prev_flag)
            z = below[i] * v1[2:3] + v1[3:4]
            low = z * sigmoid(z) * (cm * next_flag)
            count = counts[i]
            parts = [top]
            for s in range(slots + 1):
                here = low * jnp.where(count == s, 1.0, 0.0).astype(F32)
                if s < slots:
                    here = here + own[s * cols : (s + 1) * cols]
                parts.append(here)
            full = jnp.concatenate(parts, axis=0)
            left = jnp.where(col_index == 0, 0.0, pltpu.roll(full, 1, 0)).astype(BF16)
            right = jnp.where(col_index == cols - 1, 0.0, pltpu.roll(full, ext - 1, 0)).astype(BF16)
            full = full.astype(BF16)
            for g in range(2):
                for d, v in enumerate((left, full, right)):
                    lanes = slice((3 * g + d) * half, (3 * g + d + 1) * half)
                    buffers[slot][k, :, :, lanes] = v[:, g * half : (g + 1) * half].reshape(
                        slots + 2, cols, half
                    )

    def convolve(b, slot):
        m = wide(mk[pl.ds(b * GROUP, GROUP)].reshape(lines, 128), mid // 128)
        for g in range(2):
            lanes = slice(g * mid, (g + 1) * mid)
            taps = jnp.concatenate(
                [
                    buffers[slot][:, dy : dy + slots, :, g * 3 * half : (g + 1) * 3 * half].reshape(
                        lines, 3 * half
                    )
                    for dy in range(3)
                ],
                axis=1,
            )
            v = mm(taps, ws[:, :, lanes].reshape(9 * half, mid))
            sp[pl.ds(b * GROUP, GROUP), :, :, lanes] = v.reshape(GROUP, slots, cols, mid)
            w = v * m
            acc2[0, :, lanes] += fold(w)
            acc2[1, :, lanes] += fold(w * v)

    def second(b, slot, more):
        a3_copy(b, slot).start()
        convolve(b, slot)
        if more:

            @pl.when(b >= 1)
            def _():
                a3_copy(b - 1, 1 - slot).wait()

            spread(b + 1, 1 - slot)

    spread(0, 0)

    def pair(j, c):
        second(2 * j, 0, True)
        second(2 * j + 1, 1, True)
        return c

    pairs = (blocks - 1) // 2
    lax.fori_loop(0, pairs, pair, 0)
    rest = blocks - 2 * pairs
    second(2 * pairs, 0, rest == 2)
    if rest == 2:
        second(2 * pairs + 1, 1, False)
    pending += [a3_copy(0, 0), a3_copy(0, 1)]
    out_sp = pltpu.make_async_copy(sp, sp_hbm, osem.at[2])
    out_sp.start()
    pending.append(out_sp)

    buf2[me, 0:1] = row_sum(acc2[0])
    buf2[me, 1:2] = row_sum(acc2[1])
    links.all_start(buf2, sem2)
    for g in range(2):
        for dy in range(3):
            wt[g, dy * mid : (dy + 1) * mid] = jnp.transpose(ws[dy, :, g * mid : (g + 1) * mid])
    total = links.all_wait(buf2, sem2)
    mean, factor, scale, offset = norm_terms(total[0:1], total[1:2], n, g2[...], h2[...])
    v2[0:1] = mean
    v2[1:2] = factor
    v2[2:3] = scale
    v2[3:4] = offset
    v2[4:8] = jnp.zeros((4, 2 * mid), F32)

    def second_act(i, c):
        m = wide(mk[i].reshape(cells, 128), mid // 128)
        acts = []
        for g in range(2):
            lanes = slice(g * mid, (g + 1) * mid)
            z = sp[i, :, :, lanes].reshape(cells, mid) * v2[2:3, lanes] + v2[3:4, lanes]
            acts.append(z * sigmoid(z) * m)
        pp[i, :, :, 0:mid] = (acts[0] - acts[1]).reshape(slots, cols, mid)
        pp[i, :, :, mid:] = acts[1].reshape(slots, cols, mid)
        pooled[pl.ds(i, 1)] = row_sum(fold(acts[0] + acts[1]))
        return c

    lax.fori_loop(0, images, second_act, 0, unroll=2)
    pooled[...] = pooled[...] / area[...]
    rbuf3[r] = mm(pooled[...], down[...].astype(F32), HIGH)
    copies = links.row_start(rbuf3, rsem3)

    def difference(i, c):
        pd[i] = pp[i, :, :, 0:mid].astype(BF16)
        return c

    lax.fori_loop(0, images, difference, 0, unroll=4)
    out_pd = pltpu.make_async_copy(pd, pd_hbm, osem.at[3])
    out_pd.start()
    pending.append(out_pd)
    squeeze = links.row_end(rbuf3, copies)
    ibuf3[links.i, 0:1] = row_sum(squeeze)
    ibuf3[links.i, 1:2] = row_sum(squeeze * squeeze)
    total = links.img_total(ibuf3, isem3)
    mean, factor, scale, offset = norm_terms(
        total[0:1], total[1:2], float(images * n_img), g_at[...], h_at[...]
    )
    v_at[0:1] = factor
    v_at[1:8] = jnp.zeros((7, v_at.shape[1]), F32)
    at_norm[...] = (squeeze - mean) * factor
    z = at_norm[...] * g_at[...] + h_at[...]
    at_out[...] = z
    attend = z * sigmoid(z)
    upf = up[...].astype(F32)
    lean = mm(attend, upf[:, :mid] - upf[:, mid:], HIGH) + (bias[:, :mid] - bias[:, mid:])
    w0[...] = sigmoid(lean)
    w1[...] = sigmoid(-lean)


    def mixing(i, c):
        v = w0[pl.ds(i, 1)] * pp[i, :, :, 0:mid].reshape(cells, mid)
        v = v + pp[i, :, :, mid:].reshape(cells, mid)
        mx[i] = v.astype(BF16).reshape(slots, cols, mid)
        return c

    lax.fori_loop(0, images, mixing, 0, unroll=2)
    v = mx[...].reshape(images * cells, mid)
    v = mm_tn(v, jnp.concatenate([v, jnp.ones((images * cells, 128), BF16)], axis=1))
    gram[...] = v[:, 0:mid]
    mixed_sum[...] = v[:, mid:]
    out_mx = pltpu.make_async_copy(mx, mx_hbm, osem.at[4])
    out_mx.start()
    pending.append(out_mx)
    out_xt.wait()
    pending = [c for c in pending if c is not out_xt]
    gw = xt.at[0:mid]
    gw[...] = mm_terms(mm, gram[...], we[...], 3)
    wef = we[...].astype(F32)
    rbuf4[r, 0:1] = row_sum(wide(mixed_sum[...], ch // 128) * wef)
    rbuf4[r, 1:2] = row_sum(gw[...] * wef)
    ibuf4[links.i] = links.row_total(rbuf4, rsem4)
    total = links.img_total(ibuf4, isem4)
    mean, factor, scale, offset = norm_terms(total[0:1], total[1:2], n, g3[...], h3[...])
    v3[0:1] = mean
    v3[1:2] = factor
    v3[2:3] = scale
    v3[3:4] = offset
    v3[4:5] = 0.5 * scale
    v3[5:6] = 0.5 * offset
    v3[6:8] = jnp.zeros((2, ch), F32)
    awe[...] = (wef * scale).astype(BF16)
    for k, (src, dst) in enumerate([(gw, gw_hbm), (awe, awe_hbm), (wt, wt_hbm)]):
        copy = pltpu.make_async_copy(src, dst, osem.at[6 + k])
        copy.start()
        pending.append(copy)

    for copy in pending:
        copy.wait()


def sd(shape, dtype=F32):
    return jax.ShapeDtypeStruct(shape, dtype)


def call_forward(n_img, n_row, args, images, slots, cols, ch, mid, inter):
    n = n_img * n_row
    cells = (images, slots, cols)
    outs = [
        (sd(cells + (mid,)), ANY),
        (sd((images, slots + 2, cols, 3 * mid), BF16), ANY),
        (sd(cells + (2 * mid,)), ANY),
        (sd(cells + (mid,), BF16), ANY),
        (sd(cells + (mid,), BF16), ANY),
        (sd(cells + (128,)), ANY),
        (sd((mid + 8, ch)), ANY),
        (sd((8, mid)), VMEM),
        (sd((8, 2 * mid)), VMEM),
        (sd((8, ch)), VMEM),
        (sd((8, inter)), VMEM),
        (sd((images, inter)), VMEM),
        (sd((images, inter)), VMEM),
        (sd((images, mid)), VMEM),
        (sd((images, mid)), VMEM),
        (sd((images, mid)), VMEM),
        (sd((images, mid)), VMEM),
        (sd((mid, ch)), ANY),
        (sd((mid, ch), BF16), ANY),
        (sd((2, 3 * mid, 3 * mid // 2), BF16), ANY),
        (sd((mid, 128)), VMEM),
    ]
    dma = pltpu.SemaphoreType.DMA
    scratch = [
        pltpu.VMEM(cells + (mid,), F32),
        pltpu.VMEM(cells + (2 * mid,), F32),
        pltpu.VMEM(cells + (2 * mid,), F32),
        pltpu.VMEM(cells + (mid,), BF16),
        pltpu.VMEM(cells + (mid,), BF16),
        pltpu.VMEM(cells + (128,), F32),
        pltpu.VMEM((mid + 8, ch), F32),
        pltpu.VMEM((images, slots, cols, ch), BF16),
        pltpu.VMEM((GROUP, slots + 2, cols, 3 * mid), BF16),
        pltpu.VMEM((GROUP, slots + 2, cols, 3 * mid), BF16),
        pltpu.VMEM(args[6].shape, BF16),
        pltpu.VMEM((mid, ch), BF16),
        pltpu.VMEM((mid, ch), BF16),
        pltpu.VMEM((2, 3 * mid, 3 * mid // 2), BF16),
        pltpu.VMEM((3, 8, mid), F32),
        pltpu.VMEM((2, 8, 2 * mid), F32),
        pltpu.VMEM((mid, mid), F32),
        pltpu.VMEM((images, cols, mid), F32),
        pltpu.VMEM((images, cols, mid), F32),
        pltpu.VMEM((images, cols, mid), F32),
        pltpu.VMEM((n, 4, mid), F32),
        pltpu.VMEM((n, 2, 2 * mid), F32),
        pltpu.VMEM((n_row, images, inter), F32),
        pltpu.VMEM((n_img, 2, inter), F32),
        pltpu.VMEM((n_row, 2, ch), F32),
        pltpu.VMEM((n_img, 2, ch), F32),
        dma((images // GROUP,)),
        dma((9,)),
        dma((2,)),
        dma((4,)),
        dma((2, n)),
        dma((2, n)),
        dma((2, n_row)),
        dma((2, n_img)),
        dma((2, n_row)),
        dma((2, n_img)),
    ]
    in_specs = [SMEM, SMEM, ANY] + [VMEM] * (len(args) - 3)
    for k in (6, 14):
        in_specs[k] = ANY
    return pl.pallas_call(
        functools.partial(forward_kernel, n_img, n_row),
        out_shape=[o for o, _ in outs],
        in_specs=in_specs,
        out_specs=[s for _, s in outs],
        scratch_shapes=scratch,
        name="forward",
        compiler_params=pltpu.CompilerParams(
            collective_id=0, has_side_effects=True, vmem_limit_bytes=62 * 1024 * 1024
        ),
    )(*args)


PART = 4


def third_kernel(counts, group, x, cot, mx, we, awe, v3, bo, sg, q, m_out, *parts):
    per, slots, cols, ch = x.shape
    mid = mx.shape[-1]
    cells = PART * slots * cols
    columns = lax.broadcasted_iota(jnp.int32, (cols, 128), 0)

    @pl.when(pl.program_id(0) == 0)
    def _():
        m_out[...] = jnp.zeros_like(m_out)

    def product(p):
        v = mx[p * PART : (p + 1) * PART].reshape(cells, mid)
        parts[p][...] = mm(v, we[...])

    product(0)
    for p in range(per // PART):
        if p + 1 < per // PART:
            product(p + 1)
        for k in range(PART):
            i = p * PART + k
            image = pl.program_id(0) * per + i
            inside = jnp.where(columns < 12 + 2 * group[image], 1.0, 0.0).astype(F32)
            for s in range(slots):
                held = jnp.where(s < counts[image], 1.0, 0.0).astype(F32)
                m = wide(inside * held, ch // 128)
                at = (k * slots + s) * cols
                half = parts[p][at : at + cols] * v3[4:5] + v3[5:6] + 0.5 * x[i, s].astype(F32)
                th = jnp.tanh(half)
                up = 1.0 + th
                act = half * up
                bo[i, s] = (act * m).astype(BF16)
                slope = up + act * (1.0 - th)
                sg[i, s] = (cot[i, s].astype(F32) * (0.5 * m) * slope).astype(BF16)
        v = sg[p * PART : (p + 1) * PART].reshape(cells, ch)
        q[p * PART : (p + 1) * PART] = mm_nt(v, awe[...]).reshape(PART, slots, cols, mid)
    v = sg[...].reshape(per * slots * cols, ch)
    m_out[0:mid] += mm_tn(mx[...].reshape(per * slots * cols, mid), v)
    m_out[mid : mid + 16] += mm(jnp.ones((16, per * slots * cols), BF16), v)


def call_third(counts, group, x, cot, mx, we, awe, v3):
    images, slots, cols, ch = x.shape
    mid = mx.shape[-1]
    per = 8

    def cells(c):
        return pl.BlockSpec((per, slots, cols, c), lambda b: (b, 0, 0, 0))

    def whole(a):
        return pl.BlockSpec(a.shape, lambda b: (0,) * a.ndim)

    return pl.pallas_call(
        third_kernel,
        out_shape=[
            sd(x.shape, BF16),
            sd(x.shape, BF16),
            sd((images, slots, cols, mid)),
            sd((mid + 16, ch)),
        ],
        grid=(images // per,),
        in_specs=[SMEM, SMEM, cells(ch), cells(ch), cells(mid), whole(we), whole(awe), whole(v3)],
        out_specs=[
            cells(ch),
            cells(ch),
            cells(mid),
            pl.BlockSpec((mid + 16, ch), lambda b: (0, 0)),
        ],
        scratch_shapes=[pltpu.VMEM((PART * slots * cols, ch), F32)] * (per // PART),
        name="third",
        compiler_params=pltpu.CompilerParams(vmem_limit_bytes=60 * 1024 * 1024),
    )(counts, group, x, cot, mx, we, awe, v3)


def backward_kernel(
    n_img,
    n_row,
    counts,
    q_hbm,
    fp_hbm,
    a3_hbm,
    sp_hbm,
    pd_hbm,
    mx_hbm,
    mk_hbm,
    xt_hbm,
    x_hbm,
    v1,
    v2,
    v3,
    v_at,
    at_norm,
    at_out,
    w0,
    w1,
    pooled,
    gw_hbm,
    mixed_sum,
    m_in,
    area,
    g_at,
    wt_hbm,
    down,
    up,
    we,
    awe,
    fg_hbm,
    expand_out,
    split_out,
    reduce_out,
    up_out,
    down_out,
    bias_out,
    b1,
    b2,
    b3,
    b_at,
    mg,
    pd,
    mx,
    mk,
    gw,
    wt,
    split_part,
    small_part,
    rows_all,
    edge,
    ret,
    acc1,
    acc2,
    mb,
    dpart,
    pgrad,
    ibuf5,
    rbuf5,
    rbuf6,
    ibuf6,
    buf7,
    buf8,
    lsem,
    a3sem,
    hsem,
    rsem5,
    isem5,
    rsem6,
    isem6,
    sem7,
    sem8,
    rsem9,
    *reducers,
):
    images, slots, cols, mid = q_hbm.shape
    ch = we.shape[1]
    inter = down.shape[1]
    half = mid // 2
    blocks = images // GROUP
    cells = slots * cols
    links = Links(n_img, n_row)
    r, me = links.r, links.all_me()
    links.greet()
    sizes = reducer_sizes(n_row, ch, mid, inter)
    count = Reducer.COUNT
    expand_red, split_red, reduce_red, small_red = [
        Reducer(links, rows, width, reducers[k * count : (k + 1) * count])
        for k, (rows, width, _) in enumerate(sizes)
    ]
    n = v1[4:5, 0:1]
    up_rows, down_rows = inter // n_row, mid // n_row
    prev_dev = (links.i, lax.rem(r + n_row - 1, n_row))
    next_dev = (links.i, lax.rem(r + 1, n_row))
    has_prev = r > 0
    has_next = r < n_row - 1
    to_prev = pltpu.make_async_remote_copy(
        src_ref=edge.at[0],
        dst_ref=ret.at[1],
        send_sem=hsem.at[0],
        recv_sem=hsem.at[1],
        device_id=prev_dev,
        device_id_type=MESH,
    )
    to_next = pltpu.make_async_remote_copy(
        src_ref=edge.at[1],
        dst_ref=ret.at[0],
        send_sem=hsem.at[2],
        recv_sem=hsem.at[3],
        device_id=next_dev,
        device_id_type=MESH,
    )

    def columns_back(t, lines):
        col = lax.rem(lax.broadcasted_iota(jnp.int32, (lines, half), 0), cols)
        left = jnp.where(col == cols - 1, 0.0, pltpu.roll(t[:, 0:half], lines - 1, 0))
        right = jnp.where(col == 0, 0.0, pltpu.roll(t[:, 2 * half : 3 * half], 1, 0))
        return left + t[:, half : 2 * half] + right

    def small_piece(p):
        return small_part[p]

    def to_second_grads(sp, ub):
        loads = [
            pltpu.make_async_copy(src, dst, lsem.at[k])
            for k, (src, dst) in enumerate(
                [(mx_hbm, mx), (q_hbm, mg), (pd_hbm, pd), (mk_hbm, mk), (sp_hbm, sp)]
            )
        ]
        load_gw = pltpu.make_async_copy(gw_hbm, gw, lsem.at[5])
        load_wt = pltpu.make_async_copy(wt_hbm, wt, lsem.at[6])
        load_gw.start()
        for load in loads:
            load.start()
        load_wt.start()
        pending = list(loads)

        mean3, factor3, scale3 = v3[0:1], v3[1:2], v3[2:3]
        wef = we[...].astype(F32)
        rbuf5[r, 0:1] = m_in[mid : mid + 1]
        rbuf5[r, 1:2] = factor3 * (row_sum(m_in[0:mid] * wef) - mean3 * m_in[mid : mid + 1])
        links.met()
        ibuf5[links.i] = links.row_total(rbuf5, rsem5)
        total = links.img_total(ibuf5, isem5)
        b3[...] = total
        slope3, offset3 = norm_back_terms(mean3, factor3, scale3, n, total[0:1], total[1:2])
        slope = factor3 * (total[1:2] / n)
        level = jnp.broadcast_to(total[0:1] / n - slope * mean3, (16, ch))
        lefts = []
        for v, terms in ((wef * slope, 2), (level, 3)):
            for _ in range(terms):
                lefts.append(v.astype(BF16))
                v = v - lefts[-1].astype(F32)
        v = mm_nt(jnp.concatenate(lefts, axis=0), awe[...])
        fix = v[0:mid] + v[mid : 2 * mid]
        ev = v[2 * mid : 2 * mid + 1] + v[2 * mid + 16 : 2 * mid + 17] + v[2 * mid + 32 : 2 * mid + 33]
        high = fix.astype(BF16)
        mb[0:mid] = high
        mb[mid:] = (fix - high.astype(F32)).astype(BF16)

        def expand_piece(p):
            rows = pl.ds(pl.multiple_of(p * (mid // n_row), mid // n_row), mid // n_row)
            return (
                m_in[rows] * scale3 - wide(mixed_sum[rows], ch // 128) * offset3 - gw[rows] * slope3
            )

        load_gw.wait()
        expand_red.begin(expand_piece)

        for load in loads[:4]:
            load.wait()
        del pending[:4]

        def mix_back(b, c):
            v = mx[pl.ds(b * GROUP, GROUP)].reshape(GROUP * cells, mid)
            v = mm(jnp.concatenate([v, v], axis=1), mb[...])
            for k in range(GROUP):
                i = b * GROUP + k
                m = wide(mk[i].reshape(cells, 128), mid // 128)
                w = mg[i].reshape(cells, mid) - v[k * cells : (k + 1) * cells] - m * ev
                mg[i] = w.reshape(slots, cols, mid)
                dpart[pl.ds(i, 1)] = row_sum(fold(w * pd[i].reshape(cells, mid).astype(F32)))
            return c

        lax.fori_loop(0, blocks, mix_back, 0)

        upf = up[...].astype(F32)
        lean = dpart[...] * w0[...] * w1[...]
        rbuf6[r] = mm_nt(lean, upf[:, :mid] - upf[:, mid:], HIGH)
        copies = links.row_start(rbuf6, rsem6)
        z = at_out[...]
        attend = z * sigmoid(z)
        up_part = mm_tn(attend, lean, HIGH)
        bias_part = row_sum(lean)
        loads[4].wait()
        del pending[0]

        def slopes(i, c):
            m = wide(mk[i].reshape(cells, 128), mid // 128)
            for g in range(2):
                lanes = slice(g * mid, (g + 1) * mid)
                v = sp[i, :, :, lanes].reshape(cells, mid) * v2[2:3, lanes] + v2[3:4, lanes]
                ub[i, :, :, lanes] = (swish_slope(v) * m).reshape(slots, cols, mid)
            return c

        lax.fori_loop(0, images * 2 // 5, slopes, 0, unroll=2)
        attend_grad = links.row_end(rbuf6, copies) * swish_slope(z)
        ibuf6[links.i, 0:1] = row_sum(attend_grad)
        ibuf6[links.i, 1:2] = row_sum(attend_grad * at_norm[...])
        links.img_start(ibuf6, isem6)
        lax.fori_loop(images * 2 // 5, images, slopes, 0, unroll=2)
        total = links.img_end(ibuf6, isem6)
        b_at[...] = total
        count = float(images * n_img)
        squeeze_grad = (
            g_at[...]
            * v_at[0:1]
            * (attend_grad - total[0:1] / count - at_norm[...] * (total[1:2] / count))
        )
        pgrad[...] = mm_nt(squeeze_grad, down[...].astype(F32), HIGH) / area[...]

        def with_second_grads(a3, geb):
            load_wt.wait()
            acc2[...] = jnp.zeros_like(acc2)

            def second_back(i, c):
                v = mg[i].reshape(cells, mid)
                for g, w in enumerate((w0, w1)):
                    lanes = slice(g * mid, (g + 1) * mid)
                    s = sp[i, :, :, lanes].reshape(cells, mid)
                    grad = v * w[pl.ds(i, 1)] + pgrad[pl.ds(i, 1)]
                    grad = grad * ub[i, :, :, lanes].reshape(cells, mid)
                    ub[i, :, :, lanes] = grad.reshape(slots, cols, mid)
                    acc2[0, :, lanes] += fold(grad)
                    acc2[1, :, lanes] += fold(grad * s)
                return c

            lax.fori_loop(0, images, second_back, 0, unroll=2)
            mean2, factor2, scale2 = v2[0:1], v2[1:2], v2[2:3]
            s0 = row_sum(acc2[0])
            buf7[me, 0:1] = s0
            buf7[me, 1:2] = factor2 * (row_sum(acc2[1]) - mean2 * s0)
            links.all_start(buf7, sem7)
            down_part = mm_tn(pooled[...], squeeze_grad, HIGH)
            for p in range(n_row):
                lines = down_part[p * down_rows : (p + 1) * down_rows]
                small_part[p, 0:up_rows] = up_part[p * up_rows : (p + 1) * up_rows]
                small_part[p, up_rows : up_rows + down_rows // 2] = jnp.concatenate(
                    [lines[: down_rows // 2], lines[down_rows // 2 :]], axis=1
                )
                small_part[p, up_rows + down_rows // 2 :] = jnp.broadcast_to(bias_part, (8, mid))

            small_red.begin(small_piece)
            total = links.all_wait(buf7, sem7)
            expand_red.second(expand_piece)
            b2[...] = total
            slope2, offset2 = norm_back_terms(mean2, factor2, scale2, n, total[0:1], total[1:2])

            def second_grad(grad, s, m):
                return (grad * scale2 - m * (offset2 + slope2 * s)).astype(BF16)

            for side, dy in ((0, 0), (1, 2)):

                def edge_rows(i, c):
                    at = 0 if side == 0 else jnp.maximum(counts[i] - 1, 0)
                    m = wide(mk[i, 0], 2 * mid // 128)
                    geb[i] = second_grad(ub[i, at], sp[i, at], m)
                    return c

                lax.fori_loop(0, images, edge_rows, 0, unroll=4)
                for g in range(2):
                    v = geb[:, :, g * mid : (g + 1) * mid].reshape(images * cols, mid)
                    t = mm(v, wt[g, dy * mid : (dy + 1) * mid])
                    edge[side, :, :, g * half : (g + 1) * half] = (
                        columns_back(t, images * cols).astype(BF16).reshape(images, cols, half)
                    )
                if side == 0:

                    @pl.when(has_prev)
                    def _():
                        to_prev.start()

                else:

                    @pl.when(has_next)
                    def _():
                        to_next.start()

            @pl.when(jnp.logical_not(has_prev))
            def _():
                ret[0] = jnp.zeros(ret.shape[1:], BF16)

            @pl.when(jnp.logical_not(has_next))
            def _():
                ret[1] = jnp.zeros(ret.shape[1:], BF16)

            def a3_copy(b, slot):
                return pltpu.make_async_copy(
                    a3_hbm.at[pl.ds(b * GROUP, GROUP)], a3.at[slot], a3sem.at[slot]
                )

            a3_copy(0, 0).start()
            split_part[...] = jnp.zeros_like(split_part)

            def split_grads(b, c):
                slot = lax.rem(b, 2)

                @pl.when(b + 1 < blocks)
                def _():
                    a3_copy(b + 1, 1 - slot).start()

                @pl.when(b == 2)
                def _():
                    small_red.second(small_piece)

                @pl.when(b == 1)
                def _():
                    expand_red.third()

                @pl.when(b == 5)
                def _():
                    expand_red.fourth()

                @pl.when(b == 6)
                def _():
                    small_red.third()

                def one(k, c):
                    i = b * GROUP + k
                    m = wide(mk[i].reshape(cells, 128), 2 * mid // 128)
                    v = second_grad(ub[i].reshape(cells, 2 * mid), sp[i].reshape(cells, 2 * mid), m)
                    mx[i] = v[:, 0:mid].reshape(slots, cols, mid)
                    pd[i] = v[:, mid:].reshape(slots, cols, mid)
                    return c

                lax.fori_loop(0, GROUP, one, 0)
                a3_copy(b, slot).wait()
                for g, grads in enumerate((mx, pd)):
                    v = grads[pl.ds(b * GROUP, GROUP)].reshape(GROUP * cells, mid)
                    taps = jnp.concatenate(
                        [
                            a3[slot, :, dy : dy + slots, :, g * 3 * half : (g + 1) * 3 * half].reshape(
                                GROUP * cells, 3 * half
                            )
                            for dy in range(3)
                        ],
                        axis=1,
                    )
                    split_part[g] += mm_tn(v, taps)
                return c

            lax.fori_loop(0, blocks, split_grads, 0)

        pl.run_scoped(
            with_second_grads,
            pltpu.VMEM((2, GROUP, slots + 2, cols, 3 * mid), BF16),
            pltpu.VMEM((images, cols, 2 * mid), BF16),
        )

    pl.run_scoped(
        to_second_grads,
        pltpu.VMEM((images, slots, cols, 2 * mid), F32),
        pltpu.VMEM((images, slots, cols, 2 * mid), F32),
    )

    def to_inputs(fp, xs, xt, xu, split_rows):
        loads = [
            pltpu.make_async_copy(fp_hbm, fp, lsem.at[5]),
            pltpu.make_async_copy(xt_hbm, xt, lsem.at[6]),
            pltpu.make_async_copy(x_hbm, xs, lsem.at[4]),
        ]
        for load in loads:
            load.start()

        def split_piece(p):
            lines = []
            for tap in range(9):
                at = pl.multiple_of(tap * half + p * (half // n_row), half // n_row)
                lines.append(split_rows[pl.ds(at, half // n_row)])
            return jnp.concatenate(lines, axis=0).astype(F32)

        for g in range(2):
            for tap in range(9):
                split_rows[tap * half : (tap + 1) * half, g * mid : (g + 1) * mid] = jnp.transpose(
                    split_part[g, :, tap * half : (tap + 1) * half].astype(BF16)
                )
        split_red.begin(split_piece)
        @pl.when(has_prev)
        def _():
            to_prev.wait_send()
            to_next.wait_recv()

        @pl.when(has_next)
        def _():
            to_next.wait_send()
            to_prev.wait_recv()

        loads[0].wait()
        acc1[...] = jnp.zeros_like(acc1)

        def conv_back(b, c):
            @pl.when(b == 1)
            def _():
                split_red.second(split_piece)

            @pl.when(b == 3)
            def _():
                small_red.fourth()

            @pl.when(b == 5)
            def _():
                split_red.third()

            blank = jnp.zeros((GROUP, 1, cols, mid), BF16)
            for g, grads in enumerate((mx, pd)):
                v = grads[pl.ds(b * GROUP, GROUP)]
                moved = (
                    jnp.concatenate([v[:, 1:], blank], axis=1),
                    v,
                    jnp.concatenate([blank, v[:, : slots - 1]], axis=1),
                )
                v = jnp.concatenate(
                    [moved[dy].reshape(GROUP * cells, mid) for dy in range(3)], axis=1
                )
                value = mm(v, wt[g])
                back = columns_back(value, GROUP * cells)
                lanes = slice(g * half, (g + 1) * half)
                for k in range(GROUP):
                    i = b * GROUP + k
                    m = mk[i].reshape(cells, 128)
                    low = ret[1, i, :, lanes].astype(F32)
                    parts = []
                    for s in range(slots):
                        at = k * cells + s * cols
                        here = back[at : at + cols] + low * jnp.where(counts[i] - 1 == s, 1.0, 0.0).astype(F32)
                        if s == 0:
                            here = here + ret[0, i, :, lanes].astype(F32)
                        parts.append(here)
                    v = fp[i, :, :, lanes].reshape(cells, half)
                    z = v * v1[2:3, lanes] + v1[3:4, lanes]
                    grad = jnp.concatenate(parts, axis=0) * swish_slope(z) * wide(m, half // 128)
                    mg[i, :, :, lanes] = grad.reshape(slots, cols, half)
                    acc1[0, :, lanes] += fold(grad)
                    acc1[1, :, lanes] += fold(grad * v)
            return c

        lax.fori_loop(0, blocks, conv_back, 0)
        expand_out[...] = expand_red.end()
        rows_all[r] = small_red.end()
        rows_copies = links.row_copies(rows_all, rsem9)
        s0 = row_sum(acc1[0])
        buf8[me, 0:1] = s0
        buf8[me, 1:2] = v1[1:2] * (row_sum(acc1[1]) - v1[0:1] * s0)
        links.all_start(buf8, sem8)

        def narrow(i, c):
            pd[i] = mg[i].astype(BF16)
            return c

        lax.fori_loop(0, images, narrow, 0, unroll=4)
        loads[2].wait()
        lines = images * cells
        width = ch // 2
        for k in range(2):
            xu[:, k * width : (k + 1) * width] = mm_tn(
                pd[...].reshape(lines, mid), xs[:, :, :, k * width : (k + 1) * width].reshape(lines, width)
            )
        loads[1].wait()
        total = links.all_wait(buf8, sem8)
        b1[...] = total
        slope1, offset1 = norm_back_terms(v1[0:1], v1[1:2], v1[2:3], n, total[0:1], total[1:2])

        def column(v):
            return wide(jnp.transpose(jnp.broadcast_to(v, (128, mid))), ch // n_row // 128)

        scale_c, slope_c, offset_c = column(v1[2:3]), column(slope1), column(offset1)

        def reduce_piece(p):
            lanes = pl.ds(pl.multiple_of(p * (ch // n_row), ch // n_row), ch // n_row)
            v = xu[:, lanes] * scale_c - xt[mid : mid + 1, lanes] * offset_c - xt[0:mid, lanes] * slope_c
            return jnp.transpose(v.astype(BF16)).astype(F32)

        reduce_red.begin(reduce_piece)
        for copy in rows_copies:
            copy.start()
        split_red.fourth()

        def first_grad(i, c):
            m = wide(mk[i].reshape(cells, 128), mid // 128)
            v = mg[i].reshape(cells, mid) * v1[2:3] - m * (
                offset1 + slope1 * fp[i].reshape(cells, mid)
            )
            mx[i] = v.astype(BF16).reshape(slots, cols, mid)
            return c

        lax.fori_loop(0, images // 2, first_grad, 0, unroll=2)
        reduce_red.second(reduce_piece)
        lax.fori_loop(images // 2, images, first_grad, 0, unroll=2)
        out_fg = pltpu.make_async_copy(mx, fg_hbm, lsem.at[7])
        out_fg.start()
        reduce_red.third()
        split_out[...] = split_red.end()
        for copy in rows_copies:
            copy.wait()
        for p in range(n_row):
            up_out[p * up_rows : (p + 1) * up_rows] = rows_all[p, 0:up_rows]
            lines = rows_all[p, up_rows : up_rows + down_rows // 2]
            down_out[p * down_rows : (p + 1) * down_rows] = jnp.concatenate(
                [lines[:, 0:inter], lines[:, inter:]], axis=0
            )
        bias_out[...] = rows_all[0, up_rows + down_rows // 2 :]
        reduce_red.fourth()
        reduce_out[...] = reduce_red.end()
        out_fg.wait()

    pl.run_scoped(
        to_inputs,
        pltpu.VMEM((images, slots, cols, mid), F32),
        pltpu.VMEM((images, slots, cols, ch), BF16),
        pltpu.VMEM((mid + 8, ch), F32),
        pltpu.VMEM((mid, ch), F32),
        pltpu.VMEM((9 * half, 2 * mid), BF16),
    )


def reducer_sizes(n_row, ch, mid, inter):
    return [
        (mid // n_row, ch, BF16),
        (9 * (mid // 2) // n_row, 2 * mid, BF16),
        (ch // n_row, mid, BF16),
        (inter // n_row + mid // n_row // 2 + 8, mid, F32),
    ]


def call_backward(n_img, n_row, args, gw, wt, ch, inter):
    q = args[1]
    images, slots, cols, mid = q.shape
    half = mid // 2
    n = n_img * n_row
    cells = (images, slots, cols)
    sizes = reducer_sizes(n_row, ch, mid, inter)
    outs = [
        (sd(cells + (mid,), BF16), ANY),
        (sd((mid // n_row, ch)), VMEM),
        (sd((9 * half // n_row, 2 * mid)), VMEM),
        (sd((ch // n_row, mid)), VMEM),
        (sd((inter, mid)), VMEM),
        (sd((mid, inter)), VMEM),
        (sd((8, mid)), VMEM),
        (sd((2, mid)), VMEM),
        (sd((2, 2 * mid)), VMEM),
        (sd((2, ch)), VMEM),
        (sd((2, inter)), VMEM),
    ]
    dma = pltpu.SemaphoreType.DMA
    scratch = [
        pltpu.VMEM(cells + (mid,), F32),
        pltpu.VMEM(cells + (mid,), BF16),
        pltpu.VMEM(cells + (mid,), BF16),
        pltpu.VMEM(cells + (128,), F32),
        pltpu.VMEM((mid, ch), F32),
        pltpu.VMEM((2, 3 * mid, 3 * half), BF16),
        pltpu.VMEM((2, mid, 9 * half), F32),
        pltpu.VMEM((n_row, sizes[3][0], mid), F32),
        pltpu.VMEM((n_row, sizes[3][0], mid), F32),
        pltpu.VMEM((2, images, cols, mid), BF16),
        pltpu.VMEM((2, images, cols, mid), BF16),
        pltpu.VMEM((2, 8, mid), F32),
        pltpu.VMEM((2, 8, 2 * mid), F32),
        pltpu.VMEM((2 * mid, mid), BF16),
        pltpu.VMEM((images, mid), F32),
        pltpu.VMEM((images, mid), F32),
        pltpu.VMEM((n_img, 2, ch), F32),
        pltpu.VMEM((n_row, 2, ch), F32),
        pltpu.VMEM((n_row, images, inter), F32),
        pltpu.VMEM((n_img, 2, inter), F32),
        pltpu.VMEM((n, 2, 2 * mid), F32),
        pltpu.VMEM((n, 2, mid), F32),
        dma((8,)),
        dma((2,)),
        dma((4,)),
        dma((2, n_row)),
        dma((2, n_img)),
        dma((2, n_row)),
        dma((2, n_img)),
        dma((2, n)),
        dma((2, n)),
        dma((2, n_row)),
    ]
    for rows, width, dtype in sizes:
        scratch += Reducer.scratch(n_img, rows, width, dtype)
    in_specs = [SMEM] + [ANY] * 9 + [VMEM] * (len(args) - 10)
    for k, a in enumerate(args):
        if a is gw or a is wt:
            in_specs[k] = ANY
    return pl.pallas_call(
        functools.partial(backward_kernel, n_img, n_row),
        out_shape=[o for o, _ in outs],
        in_specs=in_specs,
        out_specs=[s for _, s in outs],
        scratch_shapes=scratch,
        name="backward",
        compiler_params=pltpu.CompilerParams(
            collective_id=1, has_side_effects=True, vmem_limit_bytes=62 * 1024 * 1024
        ),
    )(*args)


def input_kernel(
    fg, sg, wr, expand, split, reduce, up, down, bias, b1, b2, b3, b_at,
    gi, expand_out, split_out, reduce_out, up_out, down_out, bias_out, *lines,
):
    per, slots, cols, ch = sg.shape
    cells = per * slots * cols
    mid = fg.shape[-1]
    value = mm_nt(fg[...].reshape(cells, mid), wr[...])
    gi[...] = (value + sg[...].reshape(cells, ch).astype(F32)).astype(BF16).reshape(gi.shape)

    @pl.when(pl.program_id(0) == 0)
    def _():
        expand_out[...] = expand[...]
        split_out[...] = split[...]
        reduce_out[...] = reduce[...]
        down_out[...] = down[...]
        up_out[:, 0:mid] = up[...]
        up_out[:, mid:] = -up[...]
        bias_out[:, 0:mid] = bias[0:1]
        bias_out[:, mid:] = -bias[0:1]
        for k, v in enumerate((b1, b2, b_at, b3)):
            lines[2 * k][...] = v[1:2]
            lines[2 * k + 1][...] = v[0:1]


def call_input(fg, sg, wr, *small):
    images, slots, cols, ch = sg.shape
    mid = fg.shape[-1]
    expand, split, reduce, up, down, _, b1, b2, b3, b_at = small
    per = 14

    def cells(c):
        return pl.BlockSpec((per, slots, cols, c), lambda b: (b, 0, 0, 0))

    def whole(a):
        return pl.BlockSpec(a.shape, lambda b: (0,) * len(a.shape))

    outs = [sd(a.shape) for a in (expand, split, reduce)]
    outs += [sd((up.shape[0], 2 * mid)), sd(down.shape), sd((1, 2 * mid))]
    for v in (b1, b2, b_at, b3):
        outs += [sd((1, v.shape[1]))] * 2
    return pl.pallas_call(
        input_kernel,
        out_shape=[sd(sg.shape, BF16)] + outs,
        grid=(images // per,),
        in_specs=[cells(mid), cells(ch), whole(wr)] + [whole(a) for a in small],
        out_specs=[cells(ch)] + [whole(a) for a in outs],
        name="input_grad",
        compiler_params=pltpu.CompilerParams(vmem_limit_bytes=60 * 1024 * 1024),
    )(fg, sg, wr, *small)


def body(
    n_img,
    n_row,
    feature_map,
    image_group,
    row_counts,
    reduce_weight,
    gain_first,
    shift_first,
    split_weight,
    gain_second,
    shift_second,
    attn_down,
    gain_attend,
    shift_attend,
    attn_up,
    attn_bias,
    expand_weight,
    gain_third,
    shift_third,
    cotangent,
):
    images, slots, cols, ch = feature_map.shape
    mid = reduce_weight.shape[1]
    inter = attn_down.shape[1]
    half = mid // 2
    counts = row_counts[:, 0]
    ws = split_weight.reshape(3, 3 * half, 2 * mid)

    def line(v):
        return v[None, :]

    (
        fp, a3, sp, pd, mx, mk, xt, v1, v2, v3, v_at, at_norm, at_out, w0, w1, pooled, area,
        gw, awe, wt, mixed_sum,
    ) = call_forward(
        n_img,
        n_row,
        (
            counts,
            image_group,
            feature_map,
            reduce_weight,
            line(gain_first),
            line(shift_first),
            ws,
            line(gain_second),
            line(shift_second),
            attn_down,
            line(gain_attend),
            line(shift_attend),
            attn_up,
            line(attn_bias),
            expand_weight,
            line(gain_third),
            line(shift_third),
        ),
        images, slots, cols, ch, mid, inter,
    )
    block_out, sg, q, m_sum = call_third(
        counts, image_group, feature_map, cotangent, mx, expand_weight, awe, v3
    )
    (
        fg, grad_expand, grad_split, grad_reduce, grad_up, grad_down, bias, b1, b2, b3, b_at,
    ) = call_backward(
        n_img,
        n_row,
        (
            counts, q, fp, a3, sp, pd, mx, mk, xt, feature_map, v1, v2, v3, v_at, at_norm, at_out, w0, w1, pooled,
            gw, mixed_sum, m_sum, area, line(gain_attend), wt, attn_down, attn_up, expand_weight,
            awe,
        ),
        gw, wt, ch, inter,
    )
    small = call_input(
        fg, sg, reduce_weight, grad_expand, grad_split, grad_reduce, grad_up, grad_down, bias,
        b1, b2, b3, b_at,
    )
    grad_input, grad_expand, grad_split, grad_reduce, grad_up, grad_down = small[:6]
    return (
        block_out,
        grad_input,
        grad_reduce,
        grad_split.reshape(3, 3, half // n_row, 2 * mid),
        grad_expand,
        grad_down,
        grad_up,
    ) + tuple(v.reshape(-1) for v in small[6:])


def solution(mesh):
    cells = P("img", "row", None, None)
    in_specs = (cells, P("img"), P("img", "row")) + (P(),) * 14 + (cells,)
    out_specs = (cells, cells, P("row", None), P(None, None, "row", None), P("row", None)) + (P(),) * 11
    return jax.shard_map(
        functools.partial(body, mesh.shape["img"], mesh.shape["row"]),
        mesh=mesh,
        in_specs=in_specs,
        out_specs=out_specs,
        check_vma=False,
    )
```
